32 devices in a mesh: dp: 4 (over y, core), row: 2 (over x), col: 4 (over z).
Axes of the slice: x: 2, y: 2, z: 4, core: 2. Of those that a mesh axis runs over, the one named last changes fastest.
Arguments:
- image_in: bfloat16 [3584, 1536], P(('dp', 'row'), 'col'), may hold values from -16 to 16
- text_in: bfloat16 [1232, 1536], P(('dp', 'row'), 'col'), may hold values from -16 to 16
- condition: float32 [8, 1536], P('dp', 'row'), may hold values from -6 to 6
- image_mod_weight: bfloat16 [1536, 6, 1536], P('row', None, 'col'), may hold values from -0.15625 to 0.15625
- image_mod_bias: float32 [6, 1536], P(None, 'col'), may hold values from -1 to 1
- image_qkv_weight: bfloat16 [1536, 4608], P('col', 'row'), may hold values from -0.15625 to 0.15625
- image_qv_bias: float32 [24, 2, 64], P(('row', 'col')), may hold values from -1.2 to 1.2
- image_out_weight: bfloat16 [1536, 1536], P('row', 'col'), may hold values from -0.875 to 0.875
- image_out_bias: float32 [1536], P('col'), may hold values from -1.8 to 1.8
- image_up_weight: bfloat16 [1536, 6144], P('col', 'row'), may hold values from -0.15625 to 0.15625
- image_up_bias: float32 [6144], P('row'), may hold values from -3 to 3
- image_down_weight: bfloat16 [6144, 1536], P('row', 'col'), may hold values from -0.078125 to 0.078125
- image_down_bias: float32 [1536], P('col'), may hold values from -1.8 to 1.8
- text_mod_weight: bfloat16 [1536, 6, 1536], P('row', None, 'col'), may hold values from -0.15625 to 0.15625
- text_mod_bias: float32 [6, 1536], P(None, 'col'), may hold values from -1 to 1
- text_qkv_weight: bfloat16 [1536, 4608], P('col', 'row'), may hold values from -0.15625 to 0.15625
- text_qv_bias: float32 [24, 2, 64], P(('row', 'col')), may hold values from -1.2 to 1.2
- text_out_weight: bfloat16 [1536, 1536], P('row', 'col'), may hold values from -0.875 to 0.875
- text_out_bias: float32 [1536], P('col'), may hold values from -1.8 to 1.8
- text_up_weight: bfloat16 [1536, 6144], P('col', 'row'), may hold values from -0.15625 to 0.15625
- text_up_bias: float32 [6144], P('row'), may hold values from -3 to 3
- text_down_weight: bfloat16 [6144, 1536], P('row', 'col'), may hold values from -0.078125 to 0.078125
- text_down_bias: float32 [1536], P('col'), may hold values from -1.8 to 1.8
- image_cotangent: bfloat16 [3584, 1536], P(('dp', 'row'), 'col'), may hold values from -6 to 6
- text_cotangent: bfloat16 [1232, 1536], P(('dp', 'row'), 'col'), may hold values from -6 to 6
Outputs:
- image_out: bfloat16 [3584, 1536], P(('dp', 'row'), 'col')
- text_out: bfloat16 [1232, 1536], P(('dp', 'row'), 'col')
- image_in_grad: float32 [3584, 1536], P(('dp', 'row'), 'col')
- text_in_grad: float32 [1232, 1536], P(('dp', 'row'), 'col')
- condition_grad: float32 [8, 1536], P('dp', 'row')
- image_mod_weight_grad: float32 [2, 768, 6, 1536], P('row', 'dp', None, 'col')
- image_mod_bias_grad: float32 [4, 384, 6], P('col', 'dp')
- image_qkv_weight_grad: float32 [4, 384, 4608], P('col', 'dp', 'row')
- image_qv_bias_grad: float32 [64, 24, 2], P('dp', ('row', 'col'))
- image_out_weight_grad: float32 [2, 768, 1536], P('row', 'dp', 'col')
- image_out_bias_grad: float32 [4, 384], P('col', 'dp')
- image_up_weight_grad: float32 [4, 384, 6144], P('col', 'dp', 'row')
- image_up_bias_grad: float32 [2, 3072], P('row', 'dp')
- image_down_weight_grad: float32 [2, 3072, 1536], P('row', 'dp', 'col')
- image_down_bias_grad: float32 [4, 384], P('col', 'dp')
- text_mod_weight_grad: float32 [2, 768, 6, 1536], P('row', 'dp', None, 'col')
- text_mod_bias_grad: float32 [4, 384, 6], P('col', 'dp')
- text_qkv_weight_grad: float32 [4, 384, 4608], P('col', 'dp', 'row')
- text_qv_bias_grad: float32 [64, 24, 2], P('dp', ('row', 'col'))
- text_out_weight_grad: float32 [2, 768, 1536], P('row', 'dp', 'col')
- text_out_bias_grad: float32 [4, 384], P('col', 'dp')
- text_up_weight_grad: float32 [4, 384, 6144], P('col', 'dp', 'row')
- text_up_bias_grad: float32 [2, 3072], P('row', 'dp')
- text_down_weight_grad: float32 [2, 3072, 1536], P('row', 'dp', 'col')
- text_down_bias_grad: float32 [4, 384], P('col', 'dp')
The draws below stay inside these ranges and needn't reach their ends.
All inputs are finite; a program needn't handle non-finite values.
Results may differ from the reference program's by a relative error of at most 0.019.
The reference program's roundings to bfloat16 on the way count: a program that leaves them out, or rounds other values in their place, can miss the bound.
Values may be sent and summed in bfloat16 or wider, within the bound.
No kernel may reach another device: no remote copies, remote signals or barrier semaphores. Data moves between devices by JAX's collectives and lax.ppermute only.
A program may use at most 192 MiB of HBM per device.

```python
import math
import jax
import jax.numpy as jnp
from jax import lax

D = 1536
HEADS = 24
HD = 64
FF = 6144
IMG_LEN = 448
TXT_LEN = 154
SEQS = 8
IMG_TOK = 3584
TXT_TOK = 1232
ROW_BLOCKS = 2
COL_BLOCKS = 4


def stream_input(base_seed, row_count):
    base_key, rough_key = jax.random.split(base_seed, 2)
    rising = jnp.exp(math.log(3.0) * jnp.arange(D, dtype=jnp.float32) / (D - 1))
    roughness = jnp.exp(jax.random.uniform(rough_key, (D,), jnp.float32, -0.4, 0.4))
    column_scale = (rising * roughness)[None, :]
    values = jax.random.normal(base_key, (row_count, D), jnp.float32) * column_scale
    return jnp.clip(values, -16.0, 16.0).astype(jnp.bfloat16)


def mod_shift(base_seed):
    noise = jnp.clip(0.3 * jax.random.normal(base_seed, (6, D), jnp.float32), -1.0, 1.0)
    rising = -0.5 + 1.2 * jnp.arange(D, dtype=jnp.float32) / (D - 1)
    row_ids = jnp.arange(6)
    scale_rows = (row_ids == 1) | (row_ids == 4)
    return jnp.where(scale_rows[:, None], rising[None, :] + 0.3 * noise, noise)


def draw_image_in(key, part):
    return stream_input(jax.random.fold_in(key, 11), IMG_TOK)


def draw_text_in(key, part):
    return stream_input(jax.random.fold_in(key, 12), TXT_TOK)


def draw_image_mod_bias(key, part):
    return mod_shift(jax.random.fold_in(key, 21))


def draw_text_mod_bias(key, part):
    return mod_shift(jax.random.fold_in(key, 22))


def steps_of(own_key, shape, cuts, low, top_value):
    loudness = 1.0
    for axis_at, blocks in cuts:
        draws = jax.random.uniform(jax.random.fold_in(jax.random.fold_in(own_key, 6), axis_at), (blocks,), jnp.float32, low / len(cuts), top_value / len(cuts))
        loudness = loudness * jnp.repeat(jnp.exp(draws), shape[axis_at] // blocks).reshape((-1,) + (1,) * (len(shape) - 1 - axis_at))
    return loudness


def bell_draw(own_key, extent, deviation, bound, cuts=(), kind=jnp.bfloat16):
    factor_of = steps_of(own_key, extent, cuts, -0.22, 0.18) if cuts else 1.0
    array = jax.random.normal(own_key, extent, jnp.float32) * deviation * factor_of
    return jnp.minimum(jnp.maximum(array, -bound), bound).astype(kind)


def setup_inputs(seed: int = 0) -> dict:
    seeds = jax.random.split(jax.random.key(seed), 26)
    return {
        "image_in": draw_image_in(jax.random.fold_in(seeds[25], 71), 0),
        "text_in": draw_text_in(jax.random.fold_in(seeds[25], 71), 0),
        "condition": bell_draw(seeds[2], (SEQS, D), 1.0, 6.0, ((0, 4), (1, 2)), jnp.float32),
        "image_mod_weight": bell_draw(seeds[3], (D, 6, D), D ** -0.5, 0.15625, ((0, 2), (2, 4))),
        "image_mod_bias": draw_image_mod_bias(jax.random.fold_in(seeds[25], 71), 0),
        "image_qkv_weight": bell_draw(seeds[5], (D, 3 * D), D ** -0.5, 0.15625, ((0, 4), (1, 2))),
        "image_qv_bias": bell_draw(seeds[6], (HEADS, 2, HD), 0.2, 1.2, ((0, 8),), jnp.float32),
        "image_out_weight": bell_draw(seeds[7], (D, D), (max(D // 32, 1)) ** -0.5, 0.875, ((0, 2), (1, 4))),
        "image_out_bias": bell_draw(seeds[8], (D,), 0.3, 1.8, ((0, 4),), jnp.float32),
        "image_up_weight": bell_draw(seeds[9], (D, FF), D ** -0.5, 0.15625, ((0, 4), (1, 2))),
        "image_up_bias": bell_draw(seeds[10], (FF,), 0.5, 3.0, ((0, 2),), jnp.float32),
        "image_down_weight": bell_draw(seeds[11], (FF, D), FF ** -0.5, 0.078125, ((0, 2), (1, 4))),
        "image_down_bias": bell_draw(seeds[12], (D,), 0.3, 1.8, ((0, 4),), jnp.float32),
        "text_mod_weight": bell_draw(seeds[13], (D, 6, D), D ** -0.5, 0.15625, ((0, 2), (2, 4))),
        "text_mod_bias": draw_text_mod_bias(jax.random.fold_in(seeds[25], 71), 0),
        "text_qkv_weight": bell_draw(seeds[15], (D, 3 * D), D ** -0.5, 0.15625, ((0, 4), (1, 2))),
        "text_qv_bias": bell_draw(seeds[16], (HEADS, 2, HD), 0.2, 1.2, ((0, 8),), jnp.float32),
        "text_out_weight": bell_draw(seeds[17], (D, D), (max(D // 32, 1)) ** -0.5, 0.875, ((0, 2), (1, 4))),
        "text_out_bias": bell_draw(seeds[18], (D,), 0.3, 1.8, ((0, 4),), jnp.float32),
        "text_up_weight": bell_draw(seeds[19], (D, FF), D ** -0.5, 0.15625, ((0, 4), (1, 2))),
        "text_up_bias": bell_draw(seeds[20], (FF,), 0.5, 3.0, ((0, 2),), jnp.float32),
        "text_down_weight": bell_draw(seeds[21], (FF, D), FF ** -0.5, 0.078125, ((0, 2), (1, 4))),
        "text_down_bias": bell_draw(seeds[22], (D,), 0.3, 1.8, ((0, 4),), jnp.float32),
        "image_cotangent": bell_draw(seeds[23], (IMG_TOK, D), 1.0, 6.0, ((0, 8), (1, 4))),
        "text_cotangent": bell_draw(seeds[24], (TXT_TOK, D), 1.0, 6.0, ((0, 8), (1, 4))),
    }


EPS = 1e-06
GELU_C = 0.7978845608028654
GELU_K = 0.044715

def rounded(values):
    return lax.optimization_barrier(values.astype(jnp.bfloat16)).astype(jnp.float32)

def product(left_side, right_side):
    return jnp.dot(left_side, right_side, preferred_element_type=jnp.float32)

def norm_forward(values):
    average = lax.optimization_barrier(jnp.mean(values, axis=-1, keepdims=True))
    centred = values - average
    variance = lax.optimization_barrier(jnp.mean(centred * centred, axis=-1, keepdims=True))
    inv_std = lax.rsqrt(variance + EPS)
    return (centred * inv_std, inv_std)

def norm_backward(grad_hat, normed, inv_std):
    first_mean = lax.optimization_barrier(jnp.mean(grad_hat, axis=-1, keepdims=True))
    second_mean = lax.optimization_barrier(jnp.mean(grad_hat * normed, axis=-1, keepdims=True))
    return inv_std * (grad_hat - first_mean - normed * second_mean)

def gelu_parts(hidden):
    tangent = jnp.tanh(GELU_C * (hidden + GELU_K * hidden * hidden * hidden))
    gelu_value = 0.5 * hidden * (1.0 + tangent)
    gelu_slope = 0.5 * (1.0 + tangent) + 0.5 * hidden * (1.0 - tangent * tangent) * GELU_C * (1.0 + 3.0 * GELU_K * hidden * hidden)
    return (gelu_value, gelu_slope)

def bias_rows(qv_bias):
    zero_rows = jnp.zeros(qv_bias[:, 0].shape, jnp.float32)
    return jnp.stack([qv_bias[:, 0], zero_rows, qv_bias[:, 1]], axis=1)

def attend(packed):
    queries = packed[:, :, 0].astype(jnp.float32)
    key_rows = packed[:, :, 1].astype(jnp.float32)
    value_rows = packed[:, :, 2].astype(jnp.float32)
    score_scale = packed.shape[-1] ** (-0.5)
    scores = jnp.einsum('qhd,khd->hqk', queries, key_rows) * score_scale
    log_total = jnp.log(lax.optimization_barrier(jnp.sum(jnp.exp(scores), axis=-1)))
    attn_probs = rounded(jnp.exp(scores - log_total[..., None]))
    attended = jnp.einsum('hqk,khd->qhd', attn_probs, value_rows).astype(jnp.bfloat16)
    return (attended, log_total)

def attend_back(packed, attended, log_total, d_attended):
    queries = packed[:, :, 0].astype(jnp.float32)
    key_rows = packed[:, :, 1].astype(jnp.float32)
    value_rows = packed[:, :, 2].astype(jnp.float32)
    score_scale = packed.shape[-1] ** (-0.5)
    scores = jnp.einsum('qhd,khd->hqk', queries, key_rows) * score_scale
    soft_weights = jnp.exp(scores - log_total[..., None])
    probs_low = rounded(soft_weights)
    d_att = d_attended.astype(jnp.float32)
    row_delta = jnp.transpose(lax.optimization_barrier(jnp.sum(d_att * attended.astype(jnp.float32), axis=-1)))
    d_values = jnp.einsum('hqk,qhd->khd', probs_low, d_att)
    d_probs = jnp.einsum('qhd,khd->hqk', d_att, value_rows)
    d_scores = rounded(soft_weights * (d_probs - row_delta[..., None]) * score_scale)
    d_queries = jnp.einsum('hqk,khd->qhd', d_scores, key_rows)
    d_keys = jnp.einsum('hqk,qhd->khd', d_scores, queries)
    return jnp.stack([d_queries, d_keys, d_values], axis=2).astype(jnp.bfloat16)

def stream_front(inputs, weights, act_cond):
    mod_weight, mod_bias, qkv_weight, qv_bias = (weights[0], weights[1], weights[2], weights[3])
    modulation = jnp.einsum('k,kjn->jn', act_cond, mod_weight.astype(jnp.float32)) + mod_bias
    values = inputs.astype(jnp.float32)
    normed_one, inv_one = norm_forward(values)
    mod_in = (normed_one * (1.0 + modulation[1]) + modulation[0]).astype(jnp.bfloat16)
    qkv_sum = product(mod_in, qkv_weight).reshape(values.shape[0], qv_bias.shape[0], 3, qv_bias.shape[2])
    packed = (qkv_sum + bias_rows(qv_bias)).astype(jnp.bfloat16)
    return (modulation, values, normed_one, inv_one, mod_in, packed)

def stream_middle(front, attn_flat, weights, cotangent):
    modulation, values = (front[0], front[1])
    out_weight, out_bias, up_weight, up_bias, down_weight, down_bias = (weights[4], weights[5], weights[6], weights[7], weights[8], weights[9])
    branch_one = product(attn_flat, out_weight) + out_bias
    middle = values + modulation[2] * branch_one
    normed_two, inv_two = norm_forward(middle)
    mod_two = (normed_two * (1.0 + modulation[4]) + modulation[3]).astype(jnp.bfloat16)
    hidden = product(mod_two, up_weight) + up_bias
    gelu_value, gelu_slope = gelu_parts(hidden)
    gelu_low = gelu_value.astype(jnp.bfloat16)
    branch_two = product(gelu_low, down_weight) + down_bias
    output = (middle + modulation[5] * branch_two).astype(jnp.bfloat16)
    grad_out = cotangent.astype(jnp.float32)
    d_gate_two = lax.optimization_barrier(jnp.sum(grad_out * branch_two, axis=0))
    d_branch_two = (grad_out * modulation[5]).astype(jnp.bfloat16)
    down_w_grad = product(gelu_low.T, d_branch_two)
    down_b_grad = lax.optimization_barrier(jnp.sum(d_branch_two.astype(jnp.float32), axis=0))
    d_hidden = (product(d_branch_two, down_weight.T) * gelu_slope).astype(jnp.bfloat16)
    up_w_grad = product(mod_two.T, d_hidden)
    up_b_grad = lax.optimization_barrier(jnp.sum(d_hidden.astype(jnp.float32), axis=0))
    d_mod_two = product(d_hidden, up_weight.T)
    d_shift_two = lax.optimization_barrier(jnp.sum(d_mod_two, axis=0))
    d_scale_two = lax.optimization_barrier(jnp.sum(d_mod_two * normed_two, axis=0))
    d_middle = grad_out + norm_backward(d_mod_two * (1.0 + modulation[4]), normed_two, inv_two)
    d_gate_one = lax.optimization_barrier(jnp.sum(d_middle * branch_one, axis=0))
    d_branch_one = (d_middle * modulation[2]).astype(jnp.bfloat16)
    out_w_grad = product(attn_flat.T, d_branch_one)
    out_b_grad = lax.optimization_barrier(jnp.sum(d_branch_one.astype(jnp.float32), axis=0))
    d_attn = product(d_branch_one, out_weight.T).astype(jnp.bfloat16)
    upper_sums = (d_gate_one, d_shift_two, d_scale_two, d_gate_two)
    upper_grads = (out_w_grad, out_b_grad, up_w_grad, up_b_grad, down_w_grad, down_b_grad)
    return (output, d_middle, d_attn, upper_sums, upper_grads)

def stream_back(front, middle_out, d_qkv, weights, act_cond):
    modulation, normed_one, inv_one, mod_in = (front[0], front[2], front[3], front[4])
    d_middle, upper_sums, upper_grads = (middle_out[1], middle_out[3], middle_out[4])
    d_flat = d_qkv.reshape(d_qkv.shape[0], -1)
    qkv_w_grad = product(mod_in.T, d_flat)
    d_sums = lax.optimization_barrier(jnp.sum(d_qkv.astype(jnp.float32), axis=0))
    qv_b_grad = jnp.stack([d_sums[:, 0], d_sums[:, 2]], axis=1)
    d_mod_one = product(d_flat, weights[2].T)
    d_shift_one = lax.optimization_barrier(jnp.sum(d_mod_one, axis=0))
    d_scale_one = lax.optimization_barrier(jnp.sum(d_mod_one * normed_one, axis=0))
    in_grad = d_middle + norm_backward(d_mod_one * (1.0 + modulation[1]), normed_one, inv_one)
    d_mod = rounded(jnp.stack([d_shift_one, d_scale_one, upper_sums[0], upper_sums[1], upper_sums[2], upper_sums[3]], axis=0))
    mod_w_grad = act_cond[:, None, None] * d_mod[None]
    cond_part = jnp.einsum('jn,kjn->k', d_mod, weights[0].astype(jnp.float32))
    grads = (mod_w_grad, d_mod, qkv_w_grad, qv_b_grad) + upper_grads
    return (in_grad, cond_part, grads)

def lay_out(grads):
    mod_w, mod_b, qkv_w, qv_b, out_w, out_b, up_w, up_b, down_w, down_b = grads
    return (mod_w.reshape(ROW_BLOCKS, -1, mod_w.shape[1], mod_w.shape[2]), jnp.transpose(mod_b).reshape(COL_BLOCKS, -1, mod_b.shape[0]), qkv_w.reshape(COL_BLOCKS, -1, qkv_w.shape[1]), jnp.transpose(qv_b, (2, 0, 1)), out_w.reshape(ROW_BLOCKS, -1, out_w.shape[1]), out_b.reshape(COL_BLOCKS, -1), up_w.reshape(COL_BLOCKS, -1, up_w.shape[1]), up_b.reshape(ROW_BLOCKS, -1), down_w.reshape(ROW_BLOCKS, -1, down_w.shape[1]), down_b.reshape(COL_BLOCKS, -1))

def reference(image_in, text_in, condition, image_mod_weight, image_mod_bias, image_qkv_weight, image_qv_bias, image_out_weight, image_out_bias, image_up_weight, image_up_bias, image_down_weight, image_down_bias, text_mod_weight, text_mod_bias, text_qkv_weight, text_qv_bias, text_out_weight, text_out_bias, text_up_weight, text_up_bias, text_down_weight, text_down_bias, image_cotangent, text_cotangent):
    image_weights = (image_mod_weight, image_mod_bias, image_qkv_weight, image_qv_bias, image_out_weight, image_out_bias, image_up_weight, image_up_bias, image_down_weight, image_down_bias)
    text_weights = (text_mod_weight, text_mod_bias, text_qkv_weight, text_qv_bias, text_out_weight, text_out_bias, text_up_weight, text_up_bias, text_down_weight, text_down_bias)

    def one_sequence(totals, seq_items):
        image_rows, text_rows, cond_row, image_grad_rows, text_grad_rows = seq_items
        act_cond = rounded(cond_row * jax.nn.sigmoid(cond_row))
        front_image = stream_front(image_rows, image_weights, act_cond)
        front_text = stream_front(text_rows, text_weights, act_cond)
        joint_qkv = jnp.concatenate([front_image[5], front_text[5]], axis=0)
        attended, log_total = attend(joint_qkv)
        image_len = image_rows.shape[0]
        attn_image = attended[:image_len]
        attn_text = attended[image_len:]
        middle_image = stream_middle(front_image, attn_image.reshape(attn_image.shape[0], -1), image_weights, image_grad_rows)
        middle_text = stream_middle(front_text, attn_text.reshape(attn_text.shape[0], -1), text_weights, text_grad_rows)
        d_attn = jnp.concatenate([middle_image[2].reshape(attn_image.shape), middle_text[2].reshape(attn_text.shape)], axis=0)
        d_packed = attend_back(joint_qkv, attended, log_total, d_attn)
        back_image = stream_back(front_image, middle_image, d_packed[:image_len], image_weights, act_cond)
        back_text = stream_back(front_text, middle_text, d_packed[image_len:], text_weights, act_cond)
        sigmoid_cond = jax.nn.sigmoid(cond_row)
        cond_grad = (back_image[1] + back_text[1]) * sigmoid_cond * (1.0 + cond_row * (1.0 - sigmoid_cond))
        new_grads = back_image[2] + back_text[2]
        new_totals = tuple((totals[position] + new_grads[position] for position in range(len(new_grads))))
        return (new_totals, (middle_image[0], middle_text[0], back_image[0], back_text[0], cond_grad))
    start_totals = tuple((jnp.zeros(weight.shape, jnp.float32) for weight in image_weights + text_weights))
    seq_inputs = (image_in.reshape(SEQS, IMG_LEN, D), text_in.reshape(SEQS, TXT_LEN, D), condition, image_cotangent.reshape(SEQS, IMG_LEN, D), text_cotangent.reshape(SEQS, TXT_LEN, D))
    totals, stacked = lax.scan(one_sequence, start_totals, seq_inputs)
    image_grads = lay_out(totals[:10])
    text_grads = lay_out(totals[10:])
    image_out = stacked[0].reshape(IMG_TOK, D)
    text_out = stacked[1].reshape(TXT_TOK, D)
    image_in_grad = stacked[2].reshape(IMG_TOK, D)
    text_in_grad = stacked[3].reshape(TXT_TOK, D)
    condition_grad = stacked[4]
    return (image_out, text_out, image_in_grad, text_in_grad, condition_grad, image_grads[0], image_grads[1], image_grads[2], image_grads[3], image_grads[4], image_grads[5], image_grads[6], image_grads[7], image_grads[8], image_grads[9], text_grads[0], text_grads[1], text_grads[2], text_grads[3], text_grads[4], text_grads[5], text_grads[6], text_grads[7], text_grads[8], text_grads[9])
```

```python
import jax
import jax.numpy as jnp
from jax import lax
from jax.sharding import PartitionSpec as P

EPS = 1e-06
GELU_C = 0.7978845608028654
GELU_K = 0.044715
BF = jnp.bfloat16
F32 = jnp.float32
PLANE = ("dp", "col")
IMAGE, TEXT = 0, 1


def gelu_parts(hidden):
    tangent = jnp.tanh(GELU_C * (hidden + GELU_K * hidden * hidden * hidden))
    gelu_value = 0.5 * hidden * (1.0 + tangent)
    gelu_slope = 0.5 * (1.0 + tangent) + 0.5 * hidden * (1.0 - tangent * tangent) * GELU_C * (
        1.0 + 3.0 * GELU_K * hidden * hidden
    )
    return (gelu_value, gelu_slope)


def product(left_side, right_side):
    return jnp.dot(left_side, right_side, preferred_element_type=F32)


def transposed_left(left_side, right_side):
    return lax.dot_general(
        left_side, right_side, (((0,), (0,)), ((), ())), preferred_element_type=F32
    )


def transposed_right(left_side, right_side):
    return lax.dot_general(
        left_side, right_side, (((1,), (1,)), ((), ())), preferred_element_type=F32
    )


class Grid:
    def __init__(self):
        self.dps = lax.axis_size("dp")
        self.cols = lax.axis_size("col")
        self.dp = lax.axis_index("dp")
        self.row = lax.axis_index("row")
        self.col = lax.axis_index("col")

    def hop(self, dp, block):
        mixed = (dp % self.cols) ^ block
        return (mixed % 2) * 2 + mixed // 2

    def along_plane(self, target):
        pairs = []
        for dp in range(self.dps):
            for col in range(self.cols):
                to_dp, to_col = target(dp, col)
                pairs.append((dp * self.cols + col, to_dp * self.cols + to_col % self.cols))
        return pairs

    def spread(self, values, block):
        return lax.ppermute(
            values, PLANE, self.along_plane(lambda d, c: (d, c + self.hop(d, block)))
        )

    def bring_back(self, values, block):
        return lax.ppermute(
            values, PLANE, self.along_plane(lambda d, c: (d, c - self.hop(d, block)))
        )

    def swap_dp(self, values, bit):
        return lax.ppermute(values, "dp", [(d, d ^ bit) for d in range(self.dps)])

    def swap_row(self, values):
        return lax.ppermute(values, "row", [(0, 1), (1, 0)])

    def col_others(self, values):
        return [
            lax.ppermute(
                values, "col", [(i, (i + shift) % self.cols) for i in range(self.cols)]
            )
            for shift in range(1, self.cols)
        ]

    def gather(self, values):
        blocks = [self.spread(values, block) for block in range(self.cols)]
        return (
            jnp.concatenate([blocks[0], blocks[2]], axis=1),
            jnp.concatenate([blocks[1], blocks[3]], axis=1),
        )

    def scatter(self, even, odd):
        width = even.shape[1] // 2
        blocks = [even[:, :width], odd[:, :width], even[:, width:], odd[:, width:]]
        total = None
        for block in range(self.cols):
            part = self.bring_back(blocks[block], block).astype(F32)
            total = part if total is None else total + part
        return total

    def fetch(self, shard, axis):
        width = shard.shape[axis] // self.cols
        index = (self.col + self.hop(self.dp, 0)) % self.cols
        piece = lax.dynamic_slice_in_dim(shard, index * width, width, axis)
        return self.spread(piece, 0)

    def fetch_pair(self, mine, axis, by_row):
        other = self.swap_row(mine) if by_row else self.swap_dp(mine, 2)
        return jnp.concatenate([mine, other], axis=axis if by_row else 1 - axis)

    def fold(self, total, axis, by_row):
        cut = axis if by_row else 1 - axis
        half = total.shape[cut] // 2
        keep = lax.slice_in_dim(total, 0, half, axis=cut)
        send = lax.slice_in_dim(total, half, 2 * half, axis=cut).astype(BF)
        other = self.swap_row(send) if by_row else self.swap_dp(send, 2)
        return keep.astype(F32) + other.astype(F32)

    def fold_rest(self, total):
        bit = self.dps // 2
        while bit >= self.cols:
            half = total.shape[0] // 2
            upper = (self.dp // bit) % 2
            keep = lax.dynamic_slice_in_dim(total, upper * half, half, 0)
            send = lax.dynamic_slice_in_dim(total, (1 - upper) * half, half, 0).astype(BF)
            total = keep + self.swap_dp(send, bit).astype(F32)
            bit //= 2
        return total.astype(BF)

    def place_rows(self, part):
        share = self.dps // self.cols
        moved = lax.ppermute(
            part,
            PLANE,
            self.along_plane(
                lambda d, c: (c * share + d // self.cols, c - self.hop(d, 0))
            ),
        )
        return moved.astype(F32)[None]

    def place_cols(self, part):
        count = part.shape[0] // self.cols
        low = self.dp % self.cols
        pieces, places = [], []
        for flip in range(self.cols):
            piece = lax.dynamic_slice_in_dim(part, (low ^ flip) * count, count, 0)
            pieces.append(
                lax.ppermute(
                    piece,
                    PLANE,
                    self.along_plane(lambda d, c: (d ^ flip, c - self.hop(d, 0))),
                )
            )
            places.append((self.col + self.hop(low ^ flip, 0)) % self.cols)
        columns = []
        for place in range(self.cols):
            chosen = pieces[0]
            for flip in range(1, self.cols):
                chosen = jnp.where(places[flip] == place, pieces[flip], chosen)
            columns.append(chosen.astype(F32))
        return jnp.concatenate(columns, axis=1)[None]


def after(values, *earlier):
    return lax.optimization_barrier((values, *earlier))[0]


def norm_forward(grid, values):
    width = values.shape[1]
    own_mean = jnp.mean(values, axis=1)
    centred = values - own_mean[:, None]
    packed = jnp.stack([own_mean, jnp.sum(centred * centred, axis=1)])
    everyone = [packed] + grid.col_others(packed)
    mean = sum(item[0] for item in everyone) / grid.cols
    squares = sum(item[1] + width * (item[0] - mean) ** 2 for item in everyone)
    inv_std = lax.rsqrt(squares / (width * grid.cols) + EPS)
    return ((values - mean[:, None]) * inv_std[:, None], inv_std[:, None])


def norm_backward(grid, grad_hat, normed, inv_std):
    full_width = grad_hat.shape[1] * grid.cols
    packed = jnp.stack([jnp.sum(grad_hat, axis=1), jnp.sum(grad_hat * normed, axis=1)])
    total = (packed + sum(grid.col_others(packed))) / full_width
    return inv_std * (grad_hat - total[0][:, None] - normed * total[1][:, None])


def attend(packed):
    queries = packed[:, :, 0]
    key_rows = packed[:, :, 1]
    value_rows = packed[:, :, 2]
    score_scale = packed.shape[-1] ** (-0.5)
    scores = jnp.einsum("qhd,khd->hqk", queries, key_rows, preferred_element_type=F32) * score_scale
    log_total = jnp.log(jnp.sum(jnp.exp(scores), axis=-1))
    attn_probs = jnp.exp(scores - log_total[..., None]).astype(BF)
    attended = jnp.einsum("hqk,khd->qhd", attn_probs, value_rows, preferred_element_type=F32)
    return (attended.astype(BF), log_total)


def attend_back(packed, attended, log_total, d_attended):
    queries = packed[:, :, 0]
    key_rows = packed[:, :, 1]
    value_rows = packed[:, :, 2]
    score_scale = packed.shape[-1] ** (-0.5)
    scores = jnp.einsum("qhd,khd->hqk", queries, key_rows, preferred_element_type=F32) * score_scale
    soft_weights = jnp.exp(scores - log_total[..., None])
    row_delta = jnp.transpose(jnp.sum(d_attended.astype(F32) * attended.astype(F32), axis=-1))
    d_values = jnp.einsum(
        "hqk,qhd->khd", soft_weights.astype(BF), d_attended, preferred_element_type=F32
    )
    d_probs = jnp.einsum("qhd,khd->hqk", d_attended, value_rows, preferred_element_type=F32)
    d_scores = (soft_weights * (d_probs - row_delta[..., None]) * score_scale).astype(BF)
    d_queries = jnp.einsum("hqk,khd->qhd", d_scores, key_rows, preferred_element_type=F32)
    d_keys = jnp.einsum("hqk,qhd->khd", d_scores, queries, preferred_element_type=F32)
    return jnp.stack([d_queries, d_keys, d_values], axis=2).astype(BF)


def shards(
    image_in,
    text_in,
    condition,
    image_mod_weight,
    image_mod_bias,
    image_qkv_weight,
    image_qv_bias,
    image_out_weight,
    image_out_bias,
    image_up_weight,
    image_up_bias,
    image_down_weight,
    image_down_bias,
    text_mod_weight,
    text_mod_bias,
    text_qkv_weight,
    text_qv_bias,
    text_out_weight,
    text_out_bias,
    text_up_weight,
    text_up_bias,
    text_down_weight,
    text_down_bias,
    image_cotangent,
    text_cotangent,
):
    grid = Grid()
    streams = (IMAGE, TEXT)
    seq_count = condition.shape[0]
    col_width = image_in.shape[1]
    lengths = (image_in.shape[0], text_in.shape[0])
    heads = image_qv_bias.shape[0]
    head_size = image_qv_bias.shape[2]
    mod_weights = (image_mod_weight, text_mod_weight)
    mod_rows = image_mod_weight.shape[0]

    def join(parts):
        return jnp.concatenate(parts, axis=0)

    def rows_of(values):
        return (values[: lengths[0]], values[lengths[0] :])

    by_row_first = (True, False)

    def fetch(weights, axis):
        return [grid.fetch(weight, axis) for weight in weights]

    def fetch_first(parts, axis):
        return [grid.fetch_pair(parts[s], axis, by_row_first[s]) for s in streams]

    def fetch_last(parts, axis):
        evens = [grid.fetch_pair(parts[s], axis, not by_row_first[s]) for s in streams]
        return [(even, grid.swap_dp(even, 1)) for even in evens]

    def all_after(parts, *earlier):
        return [after(part, *earlier) for part in parts]

    def fold_core(grads):
        return [even.astype(F32) + grid.swap_dp(odd, 1).astype(F32) for even, odd in grads]

    def fold_first(totals, axis):
        return [grid.fold(totals[s], axis, by_row_first[s]) for s in streams]

    def fold_last(totals, axis):
        return [
            grid.fold_rest(grid.fold(totals[s], axis, not by_row_first[s])) for s in streams
        ]

    qkv_mine = fetch((image_qkv_weight, text_qkv_weight), 1)
    qkv_w = fetch_last(fetch_first(qkv_mine, 1), 1)

    act_cond = (condition * jax.nn.sigmoid(condition)).astype(BF)
    partial_mod = jnp.stack(
        [
            jnp.stack([product(act_cond, weight[:, j]) for j in range(6)], axis=1)
            for weight in mod_weights
        ],
        axis=1,
    )
    own_mod = lax.dynamic_index_in_dim(partial_mod, grid.row, 0, False)
    other_mod = lax.dynamic_index_in_dim(partial_mod, 1 - grid.row, 0, False)
    modulation = own_mod + grid.swap_row(other_mod) + jnp.stack([image_mod_bias, text_mod_bias])

    def field(position):
        return join(
            [
                jnp.broadcast_to(modulation[s, position], (lengths[s], col_width))
                for s in streams
            ]
        )

    def token_sums(values):
        return jnp.stack([jnp.sum(part, axis=0) for part in rows_of(values)])

    own_bias = jnp.stack([image_qv_bias, text_qv_bias])
    qv_bias = jnp.concatenate([own_bias, grid.swap_row(own_bias)], axis=1)
    bias_rows = jnp.stack(
        [qv_bias[:, :, 0], jnp.zeros(qv_bias[:, :, 0].shape, F32), qv_bias[:, :, 1]], axis=2
    ).reshape(2, -1)
    up_count = image_up_bias.shape[0] // grid.cols
    own_up = lax.dynamic_slice_in_dim(
        jnp.stack([image_up_bias, text_up_bias]), grid.col * up_count, up_count, 1
    )
    up_bias = jnp.concatenate([own_up, grid.swap_row(own_up)], axis=1)
    out_bias = (image_out_bias, text_out_bias)
    down_bias = (image_down_bias, text_down_bias)

    def with_bias(values, bias):
        return join([part + bias[s][None, :] for s, part in enumerate(rows_of(values))])

    def forward(gathered, weight):
        even, odd = (rows_of(part) for part in gathered)
        return [
            product(even[s], weight[s][0]) + product(odd[s], weight[s][1]) for s in streams
        ]

    def partials(inputs, weight):
        return tuple(
            join([product(inputs[s], weight[s][half]).astype(BF) for s in streams])
            for half in range(2)
        )

    def forward_back(gathered, weight):
        even, odd = (rows_of(part) for part in gathered)
        return [
            transposed_right(even[s], weight[s][0]) + transposed_right(odd[s], weight[s][1])
            for s in streams
        ]

    def partials_back(inputs, weight):
        return tuple(
            join([transposed_right(inputs[s], weight[s][half]).astype(BF) for s in streams])
            for half in range(2)
        )

    def tokens_by_features(gathered, grads):
        even, odd = (rows_of(part) for part in gathered)
        return [
            tuple(transposed_left(part[s], grads[s]).astype(BF) for part in (even, odd))
            for s in streams
        ]

    def features_by_tokens(inputs, gathered):
        even, odd = (rows_of(part) for part in gathered)
        return [
            tuple(transposed_left(inputs[s], part[s]).astype(BF) for part in (even, odd))
            for s in streams
        ]

    values = join([image_in, text_in]).astype(F32)
    xhat1, inv1 = norm_forward(grid, values)
    scale1 = 1.0 + field(1)
    normed1_own = (xhat1 * scale1 + field(0)).astype(BF)
    out_mine = fetch(all_after((image_out_weight, text_out_weight), normed1_own), 0)
    normed1 = grid.gather(normed1_own)
    up_mine = fetch(all_after((image_up_weight, text_up_weight), *normed1), 1)
    out_w = fetch_last(fetch_first(all_after(out_mine, *normed1), 0), 0)
    qkv_sum = forward(normed1, qkv_w)
    packed = join([(qkv_sum[s] + bias_rows[s][None, :]).astype(BF) for s in streams])
    down_mine = fetch(all_after((image_down_weight, text_down_weight), packed), 0)
    up_pair = fetch_first(all_after(up_mine, packed), 1)
    packed = packed.reshape(-1, 2 * heads, 3, head_size)
    attended, log_total = attend(packed)
    attn = rows_of(attended.reshape(attended.shape[0], -1))
    attn_out = partials(attn, out_w)
    branch1 = with_bias(grid.scatter(*attn_out), out_bias)
    up_w = fetch_last(all_after(up_pair, *attn_out), 1)

    gate1 = field(2)
    middle = values + gate1 * branch1
    down_pair = fetch_first(all_after(down_mine, middle), 0)
    xhat2, inv2 = norm_forward(grid, middle)
    scale2 = 1.0 + field(4)
    gate2 = field(5)
    normed2_own = (xhat2 * scale2 + field(3)).astype(BF)
    normed2 = grid.gather(normed2_own)
    grad_out = join([image_cotangent, text_cotangent]).astype(F32)
    d_branch2_own = (grad_out * gate2).astype(BF)
    d_branch2 = grid.gather(after(d_branch2_own, middle))
    down_w = fetch_last(all_after(down_pair, normed2_own), 0)
    hidden = forward(normed2, up_w)
    gelu_both = [gelu_parts(hidden[s] + up_bias[s][None, :]) for s in streams]
    gelu = [gelu_both[s][0].astype(BF) for s in streams]

    d_gelu = forward_back(d_branch2, down_w)
    d_hidden = [(d_gelu[s] * gelu_both[s][1]).astype(BF) for s in streams]
    hidden_back = partials_back(d_hidden, up_w)
    down_grad = features_by_tokens(all_after(gelu, *hidden_back), d_branch2)
    up_grad = tokens_by_features(normed2, all_after(d_hidden, *hidden_back))
    d_normed2 = grid.scatter(*hidden_back)
    down_fold = fold_first(fold_core(down_grad), 0)
    up_fold = fold_first(fold_core(up_grad), 1)
    gelu_down = partials(all_after(gelu, d_normed2), down_w)
    branch2 = with_bias(grid.scatter(*gelu_down), down_bias)
    outputs = rows_of((middle + gate2 * branch2).astype(BF))
    d_gate2 = token_sums(grad_out * branch2)
    d_shift2 = token_sums(d_normed2)
    d_scale2 = token_sums(d_normed2 * xhat2)
    d_middle = grad_out + norm_backward(grid, d_normed2 * scale2, xhat2, inv2)

    d_gate1 = token_sums(d_middle * branch1)
    d_branch1_own = (d_middle * gate1).astype(BF)
    d_branch1 = grid.gather(d_branch1_own)
    down_fold = fold_last(all_after(down_fold, d_branch1_own), 0)
    up_fold = fold_last(all_after(up_fold, d_branch1_own), 1)
    d_attn = join([part.astype(BF) for part in forward_back(d_branch1, out_w)])
    down_total = [grid.place_rows(part) for part in all_after(down_fold, d_attn)]
    up_total = [grid.place_cols(part) for part in all_after(up_fold, d_attn)]
    d_packed = attend_back(packed, attended, log_total, d_attn.reshape(attended.shape))
    d_qkv = rows_of(d_packed.reshape(d_packed.shape[0], -1))
    qkv_back = partials_back(d_qkv, qkv_w)
    d_normed1 = grid.scatter(*qkv_back)
    qkv_grad = tokens_by_features(normed1, all_after(d_qkv, *qkv_back))
    qkv_fold = fold_last(fold_first(fold_core(qkv_grad), 1), 1)
    out_grad = features_by_tokens(all_after(attn, *qkv_back), d_branch1)
    out_fold = fold_last(fold_first(fold_core(out_grad), 0), 0)
    d_shift1 = token_sums(d_normed1)
    d_scale1 = token_sums(d_normed1 * xhat1)
    in_grads = rows_of(d_middle + norm_backward(grid, d_normed1 * scale1, xhat1, inv1))
    qkv_total = [grid.place_cols(part) for part in qkv_fold]
    out_total = [grid.place_rows(part) for part in out_fold]

    up_sums = jnp.stack([jnp.sum(d_hidden[s].astype(F32), axis=0) for s in streams])
    head_sums = jnp.stack([jnp.sum(d_qkv[s].astype(F32), axis=0) for s in streams])
    head_sums = head_sums.reshape(2, 2, heads, 3, head_size)
    head_sums = jnp.stack([head_sums[:, :, :, 0], head_sums[:, :, :, 2]], axis=3)
    vectors = jnp.concatenate(
        [
            jnp.stack([d_shift1, d_scale1, d_gate1, d_shift2, d_scale2, d_gate2], axis=1),
            token_sums(d_branch1_own.astype(F32))[:, None],
            token_sums(d_branch2_own.astype(F32))[:, None],
            head_sums.reshape(2, -1, col_width),
            up_sums.reshape(2, -1, col_width),
        ],
        axis=1,
    ).astype(BF)
    everyone = lax.all_gather(vectors, ("dp", "row"), axis=0, tiled=False)
    vector_sums = jnp.sum(everyone.astype(F32), axis=0)
    feature_share = col_width // grid.dps
    shares = lax.dynamic_slice_in_dim(vector_sums, grid.dp * feature_share, feature_share, 2)

    def over_rows(rows, shape):
        parts = jnp.sum(rows.astype(F32).reshape(grid.dps, 2, 2, 2, *shape), axis=0)
        return jnp.where(
            grid.row == 0, parts[0, :, 0] + parts[1, :, 1], parts[1, :, 0] + parts[0, :, 1]
        )

    head_rows = 2 * heads * 2 * head_size // col_width
    head_total = over_rows(everyone[:, :, 8 : 8 + head_rows], (heads, 2, head_size))
    up_total_own = over_rows(everyone[:, :, 8 + head_rows :], (up_count,))
    head_share = head_size // grid.dps
    head_total = lax.dynamic_slice_in_dim(head_total, grid.dp * head_share, head_share, 3)
    qv_b_grad = jnp.transpose(head_total, (0, 3, 1, 2))

    d_mod = everyone[:, :, :6]
    mod_share = mod_rows // grid.dps
    act_all = lax.all_gather(act_cond, "dp", axis=0, tiled=True)
    act_share = lax.dynamic_slice_in_dim(act_all, grid.dp * mod_share, mod_share, 1)
    mod_w_grad = [
        jnp.stack([transposed_left(act_share, d_mod[:, s, j]) for j in range(6)], axis=1)[None]
        for s in streams
    ]
    own_d_mod = lax.dynamic_slice_in_dim(d_mod, grid.dp * seq_count, seq_count, 0)
    cond_part = sum(
        transposed_right(own_d_mod[:, s, j], mod_weights[s][:, j])
        for s in streams
        for j in range(6)
    )
    last = jnp.stack([cond_part, up_total_own])
    lasts = [last] + grid.col_others(last)
    cond_sum = sum(item[0] for item in lasts)
    up_share = up_count * grid.cols // grid.dps
    up_from = (grid.col - grid.dp * grid.cols // grid.dps) % grid.cols
    up_chosen = sum(jnp.where(up_from == j, lasts[j][1], 0.0) for j in range(grid.cols))
    up_start = (grid.dp % (grid.dps // grid.cols)) * up_share
    up_b_grad = lax.dynamic_slice_in_dim(up_chosen, up_start, up_share, 1)
    sigmoid_cond = jax.nn.sigmoid(condition)
    condition_grad = cond_sum * sigmoid_cond * (1.0 + condition * (1.0 - sigmoid_cond))

    grads = []
    for s in streams:
        grads += [
            mod_w_grad[s],
            jnp.transpose(shares[s, :6])[None],
            qkv_total[s],
            qv_b_grad[s],
            out_total[s],
            shares[s, 6][None],
            up_total[s],
            up_b_grad[s][None],
            down_total[s],
            shares[s, 7][None],
        ]
    return (*outputs, *in_grads, condition_grad, *grads)


def solution(mesh):
    in_specs = (
        P(("dp", "row"), "col"),
        P(("dp", "row"), "col"),
        P("dp", "row"),
        P("row", None, "col"),
        P(None, "col"),
        P("col", "row"),
        P(("row", "col"), None, None),
        P("row", "col"),
        P("col"),
        P("col", "row"),
        P("row"),
        P("row", "col"),
        P("col"),
        P("row", None, "col"),
        P(None, "col"),
        P("col", "row"),
        P(("row", "col"), None, None),
        P("row", "col"),
        P("col"),
        P("col", "row"),
        P("row"),
        P("row", "col"),
        P("col"),
        P(("dp", "row"), "col"),
        P(("dp", "row"), "col"),
    )
    out_specs = (
        P(("dp", "row"), "col"),
        P(("dp", "row"), "col"),
        P(("dp", "row"), "col"),
        P(("dp", "row"), "col"),
        P("dp", "row"),
        P("row", "dp", None, "col"),
        P("col", "dp", None),
        P("col", "dp", "row"),
        P("dp", ("row", "col"), None),
        P("row", "dp", "col"),
        P("col", "dp"),
        P("col", "dp", "row"),
        P("row", "dp"),
        P("row", "dp", "col"),
        P("col", "dp"),
        P("row", "dp", None, "col"),
        P("col", "dp", None),
        P("col", "dp", "row"),
        P("dp", ("row", "col"), None),
        P("row", "dp", "col"),
        P("col", "dp"),
        P("col", "dp", "row"),
        P("row", "dp"),
        P("row", "dp", "col"),
        P("col", "dp"),
    )
    return jax.shard_map(shards, mesh=mesh, in_specs=in_specs, out_specs=out_specs, check_vma=False)
```

```python
import jax
import jax.numpy as jnp
from jax import lax
from jax.experimental import pallas as pl
from jax.experimental.pallas import tpu as pltpu
from jax.sharding import PartitionSpec as P

EPS = 1e-06
GELU_C = 0.7978845608028654
GELU_K = 0.044715
BF = jnp.bfloat16
F32 = jnp.float32
PLANE = ("dp", "col")
IMAGE, TEXT = 0, 1


def gelu_parts(hidden):
    tangent = jnp.tanh(GELU_C * (hidden + GELU_K * hidden * hidden * hidden))
    gelu_value = 0.5 * hidden * (1.0 + tangent)
    gelu_slope = 0.5 * (1.0 + tangent) + 0.5 * hidden * (1.0 - tangent * tangent) * GELU_C * (
        1.0 + 3.0 * GELU_K * hidden * hidden
    )
    return (gelu_value, gelu_slope)


def transposed_left(left_side, right_side):
    return lax.dot_general(
        left_side, right_side, (((0,), (0,)), ((), ())), preferred_element_type=F32
    )


def transposed_right(left_side, right_side):
    return lax.dot_general(
        left_side, right_side, (((1,), (1,)), ((), ())), preferred_element_type=F32
    )


def product(left_side, right_side):
    return jnp.dot(left_side, right_side, preferred_element_type=F32)


VMEM_BYTES = 56 * 1024 * 1024
FREE = pl.CostEstimate(flops=0, bytes_accessed=0, transcendentals=0)


def call(body, grid, in_specs, out_specs, out_shape, operands):
    return pl.pallas_call(
        body,
        grid_spec=pltpu.PrefetchScalarGridSpec(
            num_scalar_prefetch=1, grid=grid, in_specs=in_specs, out_specs=out_specs
        ),
        out_shape=out_shape,
        cost_estimate=FREE,
        compiler_params=pltpu.CompilerParams(vmem_limit_bytes=VMEM_BYTES),
    )(*operands)


def whole(shape):
    return pl.BlockSpec(shape, lambda step, order: (0,) * len(shape))


def on_rows(shape):
    return pl.BlockSpec(shape, lambda step, order: (step, 0))


def on_columns(shape):
    return pl.BlockSpec(shape, lambda step, order: (0, step))


def mix(columns, weights, order, split, back, extra, outs, finish):
    tokens, width = columns.shape[1:]
    total = weights[0][0].shape[0 if back else 1]
    block = width
    pair = (block, 2 * width) if back else (2 * width, block)
    ranges = ((0, split), (split, tokens))

    def body(order_ref, columns_ref, *refs):
        multiply = transposed_right if back else product
        for stream, (low, high) in enumerate(ranges):
            blocks = [columns_ref[order_ref[4 * stream + b], low:high] for b in range(4)]
            even = jnp.concatenate([blocks[0], blocks[2]], axis=1)
            odd = jnp.concatenate([blocks[1], blocks[3]], axis=1)
            value = multiply(even, refs[2 * stream][...]) + multiply(odd, refs[2 * stream + 1][...])
            finish(stream, slice(low, high), value, refs[4:])

    return call(
        body,
        (total // block,),
        [whole(columns.shape)]
        + [on_rows(pair) if back else on_columns(pair)] * 4
        + [on_columns((item.shape[0], block)) for item in extra],
        [on_columns((rows, block)) for rows, _ in outs],
        [jax.ShapeDtypeStruct((rows, total), kind) for rows, kind in outs],
        (order, columns, *weights[0], *weights[1], *extra),
    )


def parts(inputs, weights, order, split, back):
    tokens, depth = inputs.shape
    width = weights[0][0].shape[0 if back else 1] // 2
    pair = (width, depth) if back else (depth, width)
    ranges = ((0, split), (split, tokens))

    def body(order_ref, inputs_ref, *refs):
        multiply = transposed_right if back else product
        for half in range(2):
            for stream, (low, high) in enumerate(ranges):
                place = order_ref[4 * stream + 2 * pl.program_id(0) + half]
                value = multiply(inputs_ref[low:high], refs[2 * stream + half][...])
                refs[4][place, low:high] = value.astype(BF)

    return call(
        body,
        (2,),
        [whole(inputs.shape)] + [on_rows(pair) if back else on_columns(pair)] * 4,
        whole((4, tokens, width)),
        jax.ShapeDtypeStruct((4, tokens, width), BF),
        (order, inputs, *weights[0], *weights[1]),
    )


def weight_grads(columns, inputs, order, split, back):
    tokens, width = columns.shape[1:]
    depth = inputs.shape[1]
    shape = (2 * width, depth) if back else (depth, 2 * width)
    pair = (width, depth) if back else (depth, width)
    ranges = ((0, split), (split, tokens))

    def body(order_ref, columns_ref, inputs_ref, *refs):
        for half in range(2):
            for stream, (low, high) in enumerate(ranges):
                place = order_ref[4 * stream + 2 * pl.program_id(0) + half]
                column = columns_ref[place, low:high]
                other = inputs_ref[low:high]
                if back:
                    value = transposed_left(column, other)
                else:
                    value = transposed_left(other, column)
                refs[2 * stream + half][...] = value.astype(BF)

    grads = call(
        body,
        (2,),
        [whole(columns.shape), whole(inputs.shape)],
        [on_rows(pair) if back else on_columns(pair)] * 4,
        [jax.ShapeDtypeStruct(shape, BF)] * 4,
        (order, columns, inputs),
    )
    return [(grads[0], grads[1]), (grads[2], grads[3])]


def steps_for(extents, lanes):
    tile = 128 if lanes else 16
    return 3 if all(extent % (3 * tile) == 0 for extent in extents) else 1


def beside(first, second, axis):
    shape = list(first.shape)
    shape[axis] *= 2
    half = first.shape[axis]
    steps = steps_for([first.shape[1 - axis]], axis == 0)
    other = first.shape[1 - axis] // steps
    spec = on_columns if axis == 0 else on_rows

    def block(rows, columns):
        return spec((rows, other) if axis == 0 else (other, columns))

    def body(order_ref, first_ref, second_ref, out_ref):
        if axis == 0:
            out_ref[:half] = first_ref[...]
            out_ref[half:] = second_ref[...]
        else:
            out_ref[...] = jnp.concatenate([first_ref[...], second_ref[...]], axis=1)

    return call(
        body,
        (steps,),
        [block(*first.shape)] * 2,
        block(*shape),
        jax.ShapeDtypeStruct(tuple(shape), first.dtype),
        (jnp.zeros((1,), jnp.int32), first, second),
    )


def add_and_cut(pairs, cuts):
    over_columns = [pair[0].shape[1] for pair, cut in zip(pairs, cuts) if cut == 0]
    over_rows = [pair[0].shape[0] for pair, cut in zip(pairs, cuts) if cut == 1]
    steps = min(steps_for(over_columns, True), steps_for(over_rows, False))
    in_specs, out_specs, out_shape = [], [], []
    for (first, _), cut in zip(pairs, cuts):
        rows, columns = first.shape
        if cut == 0:
            in_specs += [on_columns((rows, columns // steps))] * 2
            out_specs += [on_columns((rows // 2, columns // steps))] * 2
            out_shape += [jax.ShapeDtypeStruct((rows // 2, columns), BF)] * 2
        else:
            in_specs += [on_rows((rows // steps, columns))] * 2
            out_specs += [on_rows((rows // steps, columns // 2))] * 2
            out_shape += [jax.ShapeDtypeStruct((rows, columns // 2), BF)] * 2

    def body(order_ref, *refs):
        for item, cut in enumerate(cuts):
            total = refs[2 * item][...].astype(F32) + refs[2 * item + 1][...].astype(F32)
            total = total.astype(BF)
            outs = refs[2 * len(cuts) + 2 * item :]
            half = total.shape[cut] // 2
            outs[0][...] = total[:half] if cut == 0 else total[:, :half]
            outs[1][...] = total[half:] if cut == 0 else total[:, half:]

    flat = [array for pair in pairs for array in pair]
    halves = call(
        body, (steps,), in_specs, out_specs, out_shape, (jnp.zeros((1,), jnp.int32), *flat)
    )
    return [(halves[2 * item], halves[2 * item + 1]) for item in range(len(pairs))]


def add_up(pairs):
    steps = steps_for([pair[0].shape[0] for pair in pairs], False)
    specs = [on_rows((pair[0].shape[0] // steps, pair[0].shape[1])) for pair in pairs]

    def body(order_ref, *refs):
        for item in range(len(pairs)):
            total = refs[2 * item][...].astype(F32) + refs[2 * item + 1][...].astype(F32)
            refs[2 * len(pairs) + item][...] = total.astype(BF)

    return call(
        body,
        (steps,),
        [spec for spec in specs for _ in range(2)],
        specs,
        [jax.ShapeDtypeStruct(pair[0].shape, BF) for pair in pairs],
        (jnp.zeros((1,), jnp.int32), *[array for pair in pairs for array in pair]),
    )


def head_parts(packed_ref, head, size):
    start = head * 3 * size
    return [packed_ref[:, start + j * size : start + (j + 1) * size] for j in range(3)]


def attend(packed, order, size, count):
    tokens = packed.shape[0]
    heads = packed.shape[1] // (3 * size)
    scale = size ** (-0.5)

    def body(order_ref, packed_ref, out_ref, log_ref):
        keep = lax.broadcasted_iota(jnp.int32, (tokens, tokens), 0) < count
        for pair in range(heads // 2):
            attended = []
            for head in (2 * pair, 2 * pair + 1):
                query, key, value = head_parts(packed_ref, head, size)
                scores = transposed_right(key, query) * scale
                powers = jnp.where(keep, jnp.exp(scores), 0.0)
                log_total = jnp.log(jnp.sum(powers, axis=0, keepdims=True))
                log_ref[head : head + 1] = log_total
                probs = jnp.where(keep, jnp.exp(scores - log_total), 0.0).astype(BF)
                attended.append(transposed_left(value, probs))
            both = jnp.concatenate(attended, axis=0)
            out_ref[:, 2 * pair * size : 2 * (pair + 1) * size] = both.T.astype(BF)

    return call(
        body,
        (1,),
        [whole(packed.shape)],
        [whole((tokens, heads * size)), whole((heads, tokens))],
        [
            jax.ShapeDtypeStruct((tokens, heads * size), BF),
            jax.ShapeDtypeStruct((heads, tokens), F32),
        ],
        (order, packed),
    )


def attend_back(packed, attended, log_total, d_attended, order, size, count):
    tokens = packed.shape[0]
    heads = packed.shape[1] // (3 * size)
    scale = size ** (-0.5)

    def body(order_ref, packed_ref, attended_ref, log_ref, d_ref, out_ref):
        keep = lax.broadcasted_iota(jnp.int32, (tokens, tokens), 0) < count
        for pair in range(heads // 2):
            lanes = slice(2 * pair * size, 2 * (pair + 1) * size)
            d_pair = d_ref[:, lanes]
            both = d_pair.astype(F32) * attended_ref[:, lanes].astype(F32)
            both = both.T
            grads = []
            for side in range(2):
                head = 2 * pair + side
                delta = jnp.sum(both[side * size : (side + 1) * size], axis=0, keepdims=True)
                query, key, value = head_parts(packed_ref, head, size)
                d_out = d_pair[:, side * size : (side + 1) * size]
                scores = transposed_right(key, query) * scale
                weights = jnp.where(keep, jnp.exp(scores - log_ref[head : head + 1]), 0.0)
                d_value = product(weights.astype(BF), d_out)
                d_probs = transposed_right(value, d_out)
                d_scores = (weights * (d_probs - delta) * scale).astype(BF)
                d_key = product(d_scores, query)
                d_query = transposed_left(key, d_scores).T
                grads += [d_query, d_key, d_value]
            start = 2 * pair * 3 * size
            merged = jnp.concatenate(grads, axis=1).astype(BF)
            out_ref[:, start : start + 6 * size] = merged

    return call(
        body,
        (1,),
        [
            whole(packed.shape),
            whole(attended.shape),
            whole(log_total.shape),
            whole(d_attended.shape),
        ],
        whole(packed.shape),
        jax.ShapeDtypeStruct(packed.shape, BF),
        (order, packed, attended, log_total, d_attended),
    )


class Grid:
    def __init__(self):
        self.dps = lax.axis_size("dp")
        self.cols = lax.axis_size("col")
        self.dp = lax.axis_index("dp")
        self.row = lax.axis_index("row")
        self.col = lax.axis_index("col")

    def hop(self, dp, block, stream):
        mixed = (dp % self.cols) ^ block
        return ((mixed % 2) * 2 + mixed // 2) ^ (2 * stream)

    def along_plane(self, target):
        pairs = []
        for dp in range(self.dps):
            for col in range(self.cols):
                to_dp, to_col = target(dp, col)
                pairs.append((dp * self.cols + col, to_dp * self.cols + to_col % self.cols))
        return pairs

    def spread(self, values, stream):
        return lax.ppermute(
            values, PLANE, self.along_plane(lambda d, c: (d, c + self.hop(d, 0, stream)))
        )

    def bring_back(self, values, stream):
        return lax.ppermute(
            values, PLANE, self.along_plane(lambda d, c: (d, c - self.hop(d, 0, stream)))
        )

    def swap_dp(self, values, bit):
        return lax.ppermute(values, "dp", [(d, d ^ bit) for d in range(self.dps)])

    def swap_row(self, values):
        return lax.ppermute(values, "row", [(0, 1), (1, 0)])

    def copies(self, values):
        return jnp.broadcast_to(values[None], (self.cols, *values.shape))

    def exchange(self, values):
        return lax.all_to_all(values, "col", 0, 0, tiled=True)

    def everyone(self, values):
        return self.exchange(self.copies(values))

    def order(self):
        hops = [
            self.hop(self.dp, block, stream)
            for stream in (IMAGE, TEXT)
            for block in range(self.cols)
        ]
        return jnp.stack([(self.col - hop) % self.cols for hop in hops]).astype(jnp.int32)

    def piece(self, shard, axis, stream):
        width = shard.shape[axis] // self.cols
        index = (self.col + self.hop(self.dp, 0, stream)) % self.cols
        return lax.dynamic_slice_in_dim(shard, index * width, width, axis)

    def move(self, values, by_row):
        return self.swap_row(values) if by_row else self.swap_dp(values, 2)

    def fold_rest(self, total):
        bit = self.dps // 2
        while bit >= self.cols:
            half = total.shape[0] // 2
            upper = (self.dp // bit) % 2
            keep = lax.dynamic_slice_in_dim(total, upper * half, half, 0)
            send = lax.dynamic_slice_in_dim(total, (1 - upper) * half, half, 0).astype(BF)
            total = keep + self.swap_dp(send, bit).astype(F32)
            bit //= 2
        return total.astype(BF)

    def place_rows(self, parts):
        share = self.dps // self.cols
        placed = []
        for stream, part in enumerate(parts):
            pairs = self.along_plane(
                lambda d, c: (c * share + d // self.cols, c - self.hop(d, 0, stream))
            )
            placed.append(lax.ppermute(self.fold_rest(part), PLANE, pairs))
        return placed

    def place_cols(self, parts):
        return [self.bring_back(part, stream) for stream, part in enumerate(parts)]

    def place_cols_end(self, groups):
        widths = [group[0].shape[1] for group in groups]
        moved = jnp.concatenate([jnp.stack(group) for group in groups], axis=2)
        moved = moved.reshape(moved.shape[0], self.dps, -1, moved.shape[2])
        from_dp = lax.all_to_all(moved, "dp", 1, 1, tiled=True).astype(F32)
        from_low = from_dp.reshape(from_dp.shape[0], -1, self.cols, *from_dp.shape[2:])
        from_low = jnp.sum(from_low, axis=1)
        placed = []
        for place in range(self.cols):
            streams = []
            for stream in (IMAGE, TEXT):
                hops = ((place - self.col) % self.cols) ^ (2 * stream)
                low = (hops % 2) * 2 + hops // 2
                streams.append(lax.dynamic_index_in_dim(from_low[stream], low, 0, False))
            placed.append(jnp.stack(streams))
        results, start = [], 0
        for width in widths:
            whole_rows = jnp.concatenate(
                [item[:, :, start : start + width] for item in placed], axis=2
            )
            results.append([whole_rows[s][None] for s in range(whole_rows.shape[0])])
            start += width
        return results


def after(values, *earlier):
    return lax.optimization_barrier((values, earlier))[0]


def added(parts):
    return sum(part.astype(F32) for part in parts)


def column_sum(parts):
    return jnp.sum(parts.astype(F32), axis=0)


def norm_forward(grid, values):
    width = values.shape[1]
    own_mean = jnp.mean(values, axis=1)
    centred = values - own_mean[:, None]
    packed = jnp.stack([own_mean, jnp.sum(centred * centred, axis=1)])
    everyone = grid.everyone(packed)
    mean = jnp.mean(everyone[:, 0], axis=0)
    squares = jnp.sum(everyone[:, 1] + width * (everyone[:, 0] - mean) ** 2, axis=0)
    inv_std = lax.rsqrt(squares / (width * grid.cols) + EPS)
    return ((values - mean[:, None]) * inv_std[:, None], inv_std[:, None])


def norm_backward(grid, grad_hat, normed, inv_std):
    full_width = grad_hat.shape[1] * grid.cols
    packed = jnp.stack([jnp.sum(grad_hat, axis=1), jnp.sum(grad_hat * normed, axis=1)])
    total = jnp.sum(grid.everyone(packed), axis=0) / full_width
    return inv_std * (grad_hat - total[0][:, None] - normed * total[1][:, None])


def shards(
    image_in,
    text_in,
    condition,
    image_mod_weight,
    image_mod_bias,
    image_qkv_weight,
    image_qv_bias,
    image_out_weight,
    image_out_bias,
    image_up_weight,
    image_up_bias,
    image_down_weight,
    image_down_bias,
    text_mod_weight,
    text_mod_bias,
    text_qkv_weight,
    text_qv_bias,
    text_out_weight,
    text_out_bias,
    text_up_weight,
    text_up_bias,
    text_down_weight,
    text_down_bias,
    image_cotangent,
    text_cotangent,
):
    grid = Grid()
    streams = (IMAGE, TEXT)
    seq_count = condition.shape[0]
    col_width = image_in.shape[1]
    order = grid.order()
    split = image_in.shape[0]
    count = split + text_in.shape[0]
    padding = -count % 16
    lengths = (split, text_in.shape[0] + padding)
    heads = image_qv_bias.shape[0]
    head_size = image_qv_bias.shape[2]
    mod_weights = (image_mod_weight, text_mod_weight)
    mod_rows = image_mod_weight.shape[0]

    def join(parts):
        return jnp.concatenate(parts, axis=0)

    def padded(parts):
        zeros = jnp.zeros((padding, col_width), F32)
        return join([part.astype(F32) for part in parts] + [zeros])

    def rows_of(values):
        return (values[:split], values[split:])

    def unpadded(values):
        return (values[:split], values[split:count])

    by_row_first = (True, False)

    def pieces(weights, axis):
        return [grid.piece(weight, axis, s) for s, weight in enumerate(weights)]

    def fetch(parts):
        return [grid.spread(part, s) for s, part in enumerate(parts)]

    def fetch_pairs(parts, axis, first):
        pairs = []
        for s in streams:
            by_row = by_row_first[s] == first
            other = grid.move(parts[s], by_row)
            pairs.append(beside(parts[s], other, axis if by_row else 1 - axis))
        return pairs

    def fetch_last(evens):
        return [(even, grid.swap_dp(even, 1)) for even in evens]

    def fold_core(grads):
        return [(even, grid.swap_dp(odd, 1)) for even, odd in grads]

    def cut_axes(axis, first):
        return [axis if by_row == first else 1 - axis for by_row in by_row_first]

    def fold(pairs, axes, first):
        flat = [pair for group in pairs for pair in group]
        halves = add_and_cut(flat, [cut for axis in axes for cut in cut_axes(axis, first)])
        return [halves[2 * group : 2 * group + 2] for group in range(len(pairs))]

    def move(groups, first):
        return [
            [(keep, grid.move(send, by_row_first[s] == first)) for s, (keep, send) in enumerate(group)]
            for group in groups
        ]

    def fold_end(groups):
        sums = add_up([pair for group in groups for pair in group])
        return [sums[2 * group : 2 * group + 2] for group in range(len(groups))]

    qkv_pieces = pieces((image_qkv_weight, text_qkv_weight), 1)
    qkv_mine = fetch(qkv_pieces)
    qkv_pair = fetch_pairs(qkv_mine, 1, True)
    image_in, text_in, condition = after((image_in, text_in, condition), qkv_pieces)

    act_cond = (condition * jax.nn.sigmoid(condition)).astype(BF)
    partial_mod = jnp.stack(
        [
            jnp.stack([product(act_cond, weight[:, j]) for j in range(6)], axis=1)
            for weight in mod_weights
        ],
        axis=1,
    )
    own_mod = lax.dynamic_index_in_dim(partial_mod, grid.row, 0, False)
    other_mod = lax.dynamic_index_in_dim(partial_mod, 1 - grid.row, 0, False)
    up_count = image_up_bias.shape[0] // grid.cols
    own_qv = jnp.stack([image_qv_bias, text_qv_bias])
    own_up = lax.dynamic_slice_in_dim(
        jnp.stack([image_up_bias, text_up_bias]), grid.col * up_count, up_count, 1
    )
    to_row = [values.reshape(-1, col_width) for values in (other_mod, own_qv, own_up)]
    cuts = (to_row[0].shape[0], to_row[0].shape[0] + to_row[1].shape[0])
    from_row = jnp.split(grid.swap_row(after(jnp.concatenate(to_row), qkv_mine)), cuts)
    modulation = own_mod + from_row[0].reshape(own_mod.shape)
    modulation = modulation + jnp.stack([image_mod_bias, text_mod_bias])

    def field(position):
        return join(
            [
                jnp.broadcast_to(modulation[s, position], (lengths[s], col_width))
                for s in streams
            ]
        )

    def token_sums(values):
        return jnp.stack([jnp.sum(part, axis=0) for part in rows_of(values)])

    qv_bias = jnp.concatenate([own_qv, from_row[1].reshape(own_qv.shape)], axis=1)
    bias_rows = jnp.stack(
        [qv_bias[:, :, 0], jnp.zeros(qv_bias[:, :, 0].shape, F32), qv_bias[:, :, 1]], axis=2
    ).reshape(2, -1)
    up_bias = jnp.concatenate([own_up, from_row[2].reshape(own_up.shape)], axis=1)
    out_bias = (image_out_bias, text_out_bias)
    down_bias = (image_down_bias, text_down_bias)

    def with_bias(values, bias):
        return join([part + bias[s][None, :] for s, part in enumerate(rows_of(values))])

    def keep_bf16(stream, rows, value, refs):
        refs[-1][rows] = value.astype(BF)

    def add_bias(stream, rows, value, refs):
        refs[1][rows] = (value + refs[0][stream : stream + 1]).astype(BF)

    def into_gelu(stream, rows, value, refs):
        gelu_value, gelu_slope = gelu_parts(value + refs[0][stream : stream + 1])
        refs[1][rows] = gelu_value.astype(BF)
        refs[2][rows] = gelu_slope

    def times_slope(stream, rows, value, refs):
        d_hidden = (value * refs[0][rows]).astype(BF)
        refs[1][rows] = d_hidden
        refs[2][stream : stream + 1] = jnp.sum(d_hidden.astype(F32), axis=0, keepdims=True)

    values = padded([image_in, text_in])
    xhat1, inv1 = norm_forward(grid, values)
    scale1 = 1.0 + field(1)
    normed1_own = (xhat1 * scale1 + field(0)).astype(BF)
    normed1_copies = after(grid.copies(normed1_own), qkv_mine)
    normed1 = grid.exchange(normed1_copies)
    qkv_even = fetch_pairs(after(qkv_pair, normed1_copies), 1, False)
    late_weights = after(
        (
            (image_out_weight, text_out_weight),
            (image_up_weight, text_up_weight),
            (image_down_weight, text_down_weight),
        ),
        qkv_mine,
    )
    out_mine = fetch(pieces(late_weights[0], 0))
    up_pieces = pieces(late_weights[1], 1)
    down_pieces = pieces(late_weights[2], 0)
    out_pair = fetch_pairs(after(out_mine, normed1_copies), 0, True)
    normed1, qkv_even, out_pair, up_pieces, down_pieces = lax.optimization_barrier(
        (normed1, qkv_even, out_pair, up_pieces, down_pieces)
    )
    out_even = fetch_pairs(out_pair, 0, False)
    qkv_w = fetch_last(qkv_even)
    up_mine = fetch(up_pieces)
    down_mine = fetch(down_pieces)
    tokens = values.shape[0]
    (packed,) = mix(
        normed1, qkv_w, order, split, False, [bias_rows], [(tokens, BF)], add_bias
    )
    attn, log_total = attend(packed, order, head_size, count)
    out_w = fetch_last(after(out_even, packed))
    attn_out = parts(attn, out_w, order, split, False)
    attn_out, up_mine = lax.optimization_barrier((attn_out, up_mine))
    parts_out = grid.exchange(attn_out)
    up_pair = fetch_pairs(up_mine, 1, True)
    parts_out, up_pair, down_mine = lax.optimization_barrier((parts_out, up_pair, down_mine))
    branch1 = with_bias(column_sum(parts_out), out_bias)

    gate1 = field(2)
    middle = values + gate1 * branch1
    xhat2, inv2 = norm_forward(grid, middle)
    scale2 = 1.0 + field(4)
    gate2 = field(5)
    normed2_copies = grid.copies((xhat2 * scale2 + field(3)).astype(BF))
    normed2 = grid.exchange(normed2_copies)
    grad_out = padded([image_cotangent, text_cotangent])
    d_branch2_own = (grad_out * gate2).astype(BF)
    d_branch2_copies = grid.copies(after(d_branch2_own, normed2_copies))
    up_even = fetch_pairs(up_pair, 1, False)
    down_pair = fetch_pairs(down_mine, 0, True)
    normed2, down_pair, d_branch2_copies, up_even = lax.optimization_barrier(
        (normed2, down_pair, d_branch2_copies, up_even)
    )
    d_branch2 = grid.exchange(d_branch2_copies)
    up_w = fetch_last(up_even)
    down_even = fetch_pairs(down_pair, 0, False)
    gelu, slope = mix(
        normed2, up_w, order, split, False, [up_bias], [(tokens, BF), (tokens, F32)], into_gelu
    )

    d_branch2, gelu, down_even = lax.optimization_barrier((d_branch2, gelu, down_even))
    down_w = fetch_last(down_even)
    d_hidden, up_sums = mix(
        d_branch2, down_w, order, split, True, [slope], [(tokens, BF), (2, F32)], times_slope
    )
    hidden_back = parts(d_hidden, up_w, order, split, True)
    parts_normed2 = grid.exchange(hidden_back)
    gelu_late, d_hidden_late = after((gelu, d_hidden), hidden_back)
    down_fold = fold_core(weight_grads(d_branch2, gelu_late, order, split, False))
    up_fold = fold_core(weight_grads(normed2, d_hidden_late, order, split, True))
    gelu_down = parts(gelu_late, down_w, order, split, False)
    folds = fold([down_fold, up_fold], (0, 1), True)
    parts_normed2, folds, gelu_down = lax.optimization_barrier((parts_normed2, folds, gelu_down))
    folds = move(folds, True)
    d_normed2 = column_sum(parts_normed2)
    d_shift2 = token_sums(d_normed2)
    d_scale2 = token_sums(d_normed2 * xhat2)
    d_middle = grad_out + norm_backward(grid, d_normed2 * scale2, xhat2, inv2)

    d_gate1 = token_sums(d_middle * branch1)
    d_branch1_own = (d_middle * gate1).astype(BF)
    d_branch1 = grid.exchange(grid.copies(d_branch1_own))
    down_fold, up_fold = folds
    d_branch1, gelu_down, down_fold = lax.optimization_barrier((d_branch1, gelu_down, down_fold))
    parts_branch2 = grid.exchange(gelu_down)
    (d_attn,) = mix(d_branch1, out_w, order, split, True, [], [(tokens, BF)], keep_bf16)
    down_fold = move(fold([down_fold], (0,), False), False)
    d_qkv = attend_back(packed, attn, log_total, d_attn, order, head_size, count)
    qkv_back = parts(d_qkv, qkv_w, order, split, True)
    qkv_back, parts_branch2, up_fold = lax.optimization_barrier((qkv_back, parts_branch2, up_fold))
    folds = down_fold + move(fold([up_fold], (1,), False), False)
    parts_normed1 = grid.exchange(qkv_back)
    d_qkv_late, attn_late = after((d_qkv, attn), qkv_back)
    qkv_fold = fold_core(weight_grads(normed1, d_qkv_late, order, split, True))
    out_fold = fold_core(weight_grads(d_branch1, attn_late, order, split, False))
    late_folds = fold([qkv_fold, out_fold], (1, 0), True)
    parts_normed1, late_folds = lax.optimization_barrier((parts_normed1, late_folds))
    folds = after(folds, parts_normed1)
    late_folds = move(late_folds, True)
    down_fold, up_fold = fold_end(folds)
    d_normed1 = column_sum(parts_normed1)
    d_shift1 = token_sums(d_normed1)
    d_scale1 = token_sums(d_normed1 * xhat1)
    norm_back1 = norm_backward(grid, d_normed1 * scale1, xhat1, inv1)
    branch2 = with_bias(column_sum(parts_branch2), down_bias)
    outputs = unpadded((middle + gate2 * branch2).astype(BF))
    d_gate2 = token_sums(grad_out * branch2)
    norm_back1, late_folds, down_fold, up_fold, d_gate2 = lax.optimization_barrier(
        (norm_back1, late_folds, down_fold, up_fold, d_gate2)
    )
    down_placed, up_placed = grid.place_rows(down_fold), grid.place_cols(up_fold)
    late_folds = move(fold(late_folds, (1, 0), False), False)

    head_sums = token_sums(d_qkv.astype(F32))
    head_sums = head_sums.reshape(2, 2, heads, 3, head_size)
    head_sums = jnp.stack([head_sums[:, :, :, 0], head_sums[:, :, :, 2]], axis=3)
    vectors = jnp.concatenate(
        [
            jnp.stack([d_shift1, d_scale1, d_gate1, d_shift2, d_scale2, d_gate2], axis=1),
            token_sums(d_branch1_own.astype(F32))[:, None],
            token_sums(d_branch2_own.astype(F32))[:, None],
            head_sums.reshape(2, -1, col_width),
            up_sums.reshape(2, -1, col_width),
        ],
        axis=1,
    ).astype(BF)
    act_all = act_cond
    everyone = jnp.stack([vectors, grid.swap_row(vectors)])
    bit = grid.dps // 2
    while bit:
        everyone = jnp.concatenate([everyone, grid.swap_dp(everyone, bit)])
        act_all = jnp.concatenate([act_all, grid.swap_dp(after(act_all, vectors), bit)])
        bit //= 2
    everyone, late_folds = lax.optimization_barrier((everyone, late_folds))
    qkv_fold, out_fold = fold_end(late_folds)
    qkv_placed, out_placed = grid.place_cols(qkv_fold), grid.place_rows(out_fold)
    in_grads = unpadded(d_middle + norm_back1)
    vector_sums = jnp.sum(everyone.astype(F32), axis=0)
    feature_share = col_width // grid.dps
    shares = lax.dynamic_slice_in_dim(vector_sums, grid.dp * feature_share, feature_share, 2)

    def over_rows(rows, shape):
        halves = rows.reshape(grid.dps, 2, 2, 2, -1).astype(F32)
        total = jnp.sum(halves[:, 0, :, 0] + halves[:, 1, :, 1], axis=0)
        return total.reshape(2, *shape)

    head_rows = 2 * heads * 2 * head_size // col_width
    head_total = over_rows(everyone[:, :, 8 : 8 + head_rows], (heads, 2, head_size))
    up_total_own = over_rows(everyone[:, :, 8 + head_rows :], (up_count,))
    head_share = head_size // grid.dps
    head_total = lax.dynamic_slice_in_dim(head_total, grid.dp * head_share, head_share, 3)
    qv_b_grad = jnp.transpose(head_total, (0, 3, 1, 2))

    by_row = everyone[:, :, :6].reshape(grid.dps, 2, 2, 6, col_width)
    d_mod = jnp.where(grid.row == 0, by_row, by_row[:, ::-1]).reshape(-1, 2, 6, col_width)
    mod_share = mod_rows // grid.dps
    act_share = lax.dynamic_slice_in_dim(act_all, grid.dp * mod_share, mod_share, 1)
    mod_w_grad = [
        jnp.stack([transposed_left(act_share, d_mod[:, s, j]) for j in range(6)], axis=1)[None]
        for s in streams
    ]
    own_d_mod = d_mod[:seq_count]
    cond_part = sum(
        transposed_right(own_d_mod[:, s, j], mod_weights[s][:, j])
        for s in streams
        for j in range(6)
    )
    lasts = grid.everyone(jnp.stack([cond_part, up_total_own]))
    cond_sum = jnp.sum(lasts[:, 0], axis=0)
    up_share = up_count * grid.cols // grid.dps
    up_chosen = lax.dynamic_index_in_dim(
        lasts[:, 1], grid.dp * grid.cols // grid.dps, 0, False
    )
    up_start = (grid.dp % (grid.dps // grid.cols)) * up_share
    up_b_grad = lax.dynamic_slice_in_dim(up_chosen, up_start, up_share, 1)
    qkv_total, up_total = grid.place_cols_end([qkv_placed, up_placed])
    down_total = [down_placed[s].astype(F32)[None] for s in streams]
    out_total = [out_placed[s].astype(F32)[None] for s in streams]
    sigmoid_cond = jax.nn.sigmoid(condition)
    condition_grad = cond_sum * sigmoid_cond * (1.0 + condition * (1.0 - sigmoid_cond))

    grads = []
    for s in streams:
        grads += [
            mod_w_grad[s],
            jnp.transpose(shares[s, :6])[None],
            qkv_total[s],
            qv_b_grad[s],
            out_total[s],
            shares[s, 6][None],
            up_total[s],
            up_b_grad[s][None],
            down_total[s],
            shares[s, 7][None],
        ]
    return (*outputs, *in_grads, condition_grad, *grads)


def solution(mesh):
    in_specs = (
        P(("dp", "row"), "col"),
        P(("dp", "row"), "col"),
        P("dp", "row"),
        P("row", None, "col"),
        P(None, "col"),
        P("col", "row"),
        P(("row", "col"), None, None),
        P("row", "col"),
        P("col"),
        P("col", "row"),
        P("row"),
        P("row", "col"),
        P("col"),
        P("row", None, "col"),
        P(None, "col"),
        P("col", "row"),
        P(("row", "col"), None, None),
        P("row", "col"),
        P("col"),
        P("col", "row"),
        P("row"),
        P("row", "col"),
        P("col"),
        P(("dp", "row"), "col"),
        P(("dp", "row"), "col"),
    )
    out_specs = (
        P(("dp", "row"), "col"),
        P(("dp", "row"), "col"),
        P(("dp", "row"), "col"),
        P(("dp", "row"), "col"),
        P("dp", "row"),
        P("row", "dp", None, "col"),
        P("col", "dp", None),
        P("col", "dp", "row"),
        P("dp", ("row", "col"), None),
        P("row", "dp", "col"),
        P("col", "dp"),
        P("col", "dp", "row"),
        P("row", "dp"),
        P("row", "dp", "col"),
        P("col", "dp"),
        P("row", "dp", None, "col"),
        P("col", "dp", None),
        P("col", "dp", "row"),
        P("dp", ("row", "col"), None),
        P("row", "dp", "col"),
        P("col", "dp"),
        P("col", "dp", "row"),
        P("row", "dp"),
        P("row", "dp", "col"),
        P("col", "dp"),
    )
    return jax.shard_map(shards, mesh=mesh, in_specs=in_specs, out_specs=out_specs, check_vma=False)
```

```python
import jax
import jax.numpy as jnp
from jax import lax
from jax.experimental import pallas as pl
from jax.experimental.pallas import tpu as pltpu
from jax.sharding import PartitionSpec as P

EPS = 1e-06
GELU_C = 0.7978845608028654
GELU_K = 0.044715
BF = jnp.bfloat16
F32 = jnp.float32
PLANE = ("dp", "col")
IMAGE, TEXT = 0, 1


def gelu_parts(hidden):
    tangent = jnp.tanh(GELU_C * (hidden + GELU_K * hidden * hidden * hidden))
    gelu_value = 0.5 * hidden * (1.0 + tangent)
    gelu_slope = 0.5 * (1.0 + tangent) + 0.5 * hidden * (1.0 - tangent * tangent) * GELU_C * (
        1.0 + 3.0 * GELU_K * hidden * hidden
    )
    return (gelu_value, gelu_slope)


def transposed_left(left_side, right_side):
    return lax.dot_general(
        left_side, right_side, (((0,), (0,)), ((), ())), preferred_element_type=F32
    )


def transposed_right(left_side, right_side):
    return lax.dot_general(
        left_side, right_side, (((1,), (1,)), ((), ())), preferred_element_type=F32
    )


def product(left_side, right_side):
    return jnp.dot(left_side, right_side, preferred_element_type=F32)


VMEM_BYTES = 56 * 1024 * 1024
FREE = pl.CostEstimate(flops=0, bytes_accessed=0, transcendentals=0)


def call(body, grid, in_specs, out_specs, out_shape, operands):
    return pl.pallas_call(
        body,
        grid_spec=pltpu.PrefetchScalarGridSpec(
            num_scalar_prefetch=1, grid=grid, in_specs=in_specs, out_specs=out_specs
        ),
        out_shape=out_shape,
        cost_estimate=FREE,
        compiler_params=pltpu.CompilerParams(vmem_limit_bytes=VMEM_BYTES),
    )(*operands)


def whole(shape):
    return pl.BlockSpec(shape, lambda step, order: (0,) * len(shape))


def on_rows(shape):
    return pl.BlockSpec(shape, lambda step, order: (step, 0))


def on_columns(shape):
    return pl.BlockSpec(shape, lambda step, order: (0, step))


def mix(columns, weights, order, split, back, extra, outs, finish):
    tokens, width = columns.shape[1:]
    total = weights[0][0].shape[0 if back else 1]
    block = width
    pair = (block, 2 * width) if back else (2 * width, block)
    ranges = ((0, split), (split, tokens))

    def body(order_ref, columns_ref, *refs):
        multiply = transposed_right if back else product
        for stream, (low, high) in enumerate(ranges):
            blocks = [columns_ref[order_ref[4 * stream + b], low:high] for b in range(4)]
            even = jnp.concatenate([blocks[0], blocks[2]], axis=1)
            odd = jnp.concatenate([blocks[1], blocks[3]], axis=1)
            value = multiply(even, refs[2 * stream][...]) + multiply(odd, refs[2 * stream + 1][...])
            finish(stream, slice(low, high), value, refs[4:])

    return call(
        body,
        (total // block,),
        [whole(columns.shape)]
        + [on_rows(pair) if back else on_columns(pair)] * 4
        + [on_columns((item.shape[0], block)) for item in extra],
        [on_columns((rows, block)) for rows, _ in outs],
        [jax.ShapeDtypeStruct((rows, total), kind) for rows, kind in outs],
        (order, columns, *weights[0], *weights[1], *extra),
    )


def parts(inputs, weights, order, split, back):
    tokens, depth = inputs.shape
    width = weights[0][0].shape[0 if back else 1] // 2
    pair = (width, depth) if back else (depth, width)
    ranges = ((0, split), (split, tokens))

    def body(order_ref, inputs_ref, *refs):
        multiply = transposed_right if back else product
        for half in range(2):
            for stream, (low, high) in enumerate(ranges):
                place = order_ref[4 * stream + 2 * pl.program_id(0) + half]
                value = multiply(inputs_ref[low:high], refs[2 * stream + half][...])
                refs[4][place, low:high] = value.astype(BF)

    return call(
        body,
        (2,),
        [whole(inputs.shape)] + [on_rows(pair) if back else on_columns(pair)] * 4,
        whole((4, tokens, width)),
        jax.ShapeDtypeStruct((4, tokens, width), BF),
        (order, inputs, *weights[0], *weights[1]),
    )


def weight_grads(columns, inputs, order, split, back):
    tokens, width = columns.shape[1:]
    depth = inputs.shape[1]
    shape = (2 * width, depth) if back else (depth, 2 * width)
    pair = (width, depth) if back else (depth, width)
    ranges = ((0, split), (split, tokens))

    def body(order_ref, columns_ref, inputs_ref, *refs):
        for half in range(2):
            for stream, (low, high) in enumerate(ranges):
                place = order_ref[4 * stream + 2 * pl.program_id(0) + half]
                column = columns_ref[place, low:high]
                other = inputs_ref[low:high]
                if back:
                    value = transposed_left(column, other)
                else:
                    value = transposed_left(other, column)
                refs[2 * stream + half][...] = value.astype(BF)

    grads = call(
        body,
        (2,),
        [whole(columns.shape), whole(inputs.shape)],
        [on_rows(pair) if back else on_columns(pair)] * 4,
        [jax.ShapeDtypeStruct(shape, BF)] * 4,
        (order, columns, inputs),
    )
    return [(grads[0], grads[1]), (grads[2], grads[3])]


def steps_for(extents, lanes):
    tile = 128 if lanes else 16
    return 3 if all(extent % (3 * tile) == 0 for extent in extents) else 1


def assemble(groups):
    shapes = [(2 * group[0].shape[0], 2 * group[0].shape[1]) for group in groups]

    def body(order_ref, *refs):
        for item, (rows, _) in enumerate(shapes):
            out_ref = refs[4 * len(groups) + item]
            for side in range(2):

                @pl.when(pl.program_id(0) == side)
                def _():
                    out_ref[: rows // 2] = refs[4 * item + side][...]
                    out_ref[rows // 2 :] = refs[4 * item + 2 + side][...]

    flat = [array for group in groups for array in group]
    return call(
        body,
        (2,),
        [whole(array.shape) for array in flat],
        [on_columns((rows, columns // 2)) for rows, columns in shapes],
        [jax.ShapeDtypeStruct(shape, BF) for shape in shapes],
        (jnp.zeros((1,), jnp.int32), *flat),
    )


def add_and_cut(pairs, cuts):
    over_columns = [pair[0].shape[1] for pair, cut in zip(pairs, cuts) if cut == 0]
    over_rows = [pair[0].shape[0] for pair, cut in zip(pairs, cuts) if cut == 1]
    steps = min(steps_for(over_columns, True), steps_for(over_rows, False))
    in_specs, out_specs, out_shape = [], [], []
    for (first, _), cut in zip(pairs, cuts):
        rows, columns = first.shape
        if cut == 0:
            in_specs += [on_columns((rows, columns // steps))] * 2
            out_specs += [on_columns((rows // 2, columns // steps))] * 2
            out_shape += [jax.ShapeDtypeStruct((rows // 2, columns), BF)] * 2
        else:
            in_specs += [on_rows((rows // steps, columns))] * 2
            out_specs += [on_rows((rows // steps, columns // 2))] * 2
            out_shape += [jax.ShapeDtypeStruct((rows, columns // 2), BF)] * 2

    def body(order_ref, *refs):
        for item, cut in enumerate(cuts):
            total = refs[2 * item][...].astype(F32) + refs[2 * item + 1][...].astype(F32)
            total = total.astype(BF)
            outs = refs[2 * len(cuts) + 2 * item :]
            half = total.shape[cut] // 2
            outs[0][...] = total[:half] if cut == 0 else total[:, :half]
            outs[1][...] = total[half:] if cut == 0 else total[:, half:]

    flat = [array for pair in pairs for array in pair]
    halves = call(
        body, (steps,), in_specs, out_specs, out_shape, (jnp.zeros((1,), jnp.int32), *flat)
    )
    return [(halves[2 * item], halves[2 * item + 1]) for item in range(len(pairs))]


def add_up(pairs):
    steps = steps_for([pair[0].shape[0] for pair in pairs], False)
    specs = [on_rows((pair[0].shape[0] // steps, pair[0].shape[1])) for pair in pairs]

    def body(order_ref, *refs):
        for item in range(len(pairs)):
            total = refs[2 * item][...].astype(F32) + refs[2 * item + 1][...].astype(F32)
            refs[2 * len(pairs) + item][...] = total.astype(BF)

    return call(
        body,
        (steps,),
        [spec for spec in specs for _ in range(2)],
        specs,
        [jax.ShapeDtypeStruct(pair[0].shape, BF) for pair in pairs],
        (jnp.zeros((1,), jnp.int32), *[array for pair in pairs for array in pair]),
    )


def unpack(fronts, width, by_row_first):
    rows, columns = fronts[0].shape[0] // 4, fronts[0].shape[1]
    deep = rows - width

    def body(order_ref, *refs):
        shorter = rows - width
        for stream, by_row in enumerate(by_row_first):
            front_ref, qkv_ref, out_ref = refs[stream], refs[2 + 2 * stream], refs[3 + 2 * stream]
            for block in range(2):
                qkv_halves = []
                for half in range(2):
                    start = rows * (2 * block + half if by_row else 2 * half + block)
                    qkv_halves.append(front_ref[start : start + width])
                    lanes = slice(block * width, (block + 1) * width)
                    out_ref[half * shorter : (half + 1) * shorter, lanes] = front_ref[
                        start + width : start + rows, :width
                    ]
                qkv_ref[block * width : (block + 1) * width] = jnp.concatenate(qkv_halves, axis=1)

    shapes = [(2 * width, 2 * columns), (2 * deep, 2 * width)] * 2
    return call(
        body,
        (1,),
        [whole(front.shape) for front in fronts],
        [whole(shape) for shape in shapes],
        [jax.ShapeDtypeStruct(shape, BF) for shape in shapes],
        (jnp.zeros((1,), jnp.int32), *fronts),
    )


def rows_for(values, rows):
    gap = rows - values.shape[-2]
    return jnp.pad(values, [(0, 0)] * (values.ndim - 2) + [(0, gap), (0, 0)])


def modulation_grads(act, d_mod, mod_rows):
    sequences, count = act.shape
    width = d_mod.shape[-1]
    act = act.astype(F32)
    d_mod = jnp.moveaxis(d_mod, 0, 2).astype(F32).reshape(-1, sequences, width)

    def body(order_ref, act_ref, d_ref, *refs):
        for stream in range(2):
            d_row = d_ref[stream * mod_rows + pl.program_id(0)].astype(BF)
            refs[stream][0] = transposed_left(act_ref[...].astype(BF), d_row)

    spec = pl.BlockSpec((1, count, width), lambda step, order: (step, 0, 0))
    grads = call(
        body,
        (mod_rows,),
        [whole(act.shape), whole(d_mod.shape)],
        [spec] * 2,
        [jax.ShapeDtypeStruct((mod_rows, count, width), F32)] * 2,
        (jnp.zeros((1,), jnp.int32), act, d_mod),
    )
    return [jnp.transpose(grad, (1, 0, 2))[None] for grad in grads]


def condition_part(d_mod, weights):
    sequences, _, mod_rows, width = d_mod.shape
    inputs = weights[0].shape[0]
    d_mod = jnp.moveaxis(d_mod, 0, 2).astype(F32).reshape(-1, sequences, width)
    d_mod = rows_for(d_mod, 8)

    def body(order_ref, d_ref, image_ref, text_ref, out_ref):
        @pl.when(pl.program_id(0) == 0)
        def _():
            out_ref[...] = jnp.zeros_like(out_ref)

        for stream, weight_ref in enumerate((image_ref, text_ref)):
            d_row = d_ref[stream * mod_rows + pl.program_id(0)].astype(BF)
            out_ref[...] += transposed_right(d_row, weight_ref[0])

    spec = pl.BlockSpec((1, inputs, width), lambda step, order: (step, 0, 0))
    total = call(
        body,
        (mod_rows,),
        [whole(d_mod.shape), spec, spec],
        whole((8, inputs)),
        jax.ShapeDtypeStruct((8, inputs), F32),
        (jnp.zeros((1,), jnp.int32), d_mod, *[jnp.transpose(w, (1, 0, 2)) for w in weights]),
    )
    return total[:sequences]


def head_parts(packed_ref, head, size):
    start = head * 3 * size
    return [packed_ref[:, start + j * size : start + (j + 1) * size] for j in range(3)]


def attend(packed, order, size, count):
    tokens = packed.shape[0]
    heads = packed.shape[1] // (3 * size)
    scale = size ** (-0.5)

    def body(order_ref, packed_ref, out_ref, log_ref):
        keep = lax.broadcasted_iota(jnp.int32, (tokens, tokens), 0) < count
        for pair in range(heads // 2):
            attended = []
            for head in (2 * pair, 2 * pair + 1):
                query, key, value = head_parts(packed_ref, head, size)
                scores = transposed_right(key, query) * scale
                powers = jnp.where(keep, jnp.exp(scores), 0.0)
                log_total = jnp.log(jnp.sum(powers, axis=0, keepdims=True))
                log_ref[head : head + 1] = log_total
                probs = jnp.where(keep, jnp.exp(scores - log_total), 0.0).astype(BF)
                attended.append(transposed_left(value, probs))
            both = jnp.concatenate(attended, axis=0)
            out_ref[:, 2 * pair * size : 2 * (pair + 1) * size] = both.T.astype(BF)

    return call(
        body,
        (1,),
        [whole(packed.shape)],
        [whole((tokens, heads * size)), whole((heads, tokens))],
        [
            jax.ShapeDtypeStruct((tokens, heads * size), BF),
            jax.ShapeDtypeStruct((heads, tokens), F32),
        ],
        (order, packed),
    )


def attend_back(packed, attended, log_total, d_attended, order, size, count):
    tokens = packed.shape[0]
    heads = packed.shape[1] // (3 * size)
    scale = size ** (-0.5)

    def body(order_ref, packed_ref, attended_ref, log_ref, d_ref, out_ref):
        keep = lax.broadcasted_iota(jnp.int32, (tokens, tokens), 0) < count
        for pair in range(heads // 2):
            lanes = slice(2 * pair * size, 2 * (pair + 1) * size)
            d_pair = d_ref[:, lanes]
            both = d_pair.astype(F32) * attended_ref[:, lanes].astype(F32)
            both = both.T
            grads = []
            for side in range(2):
                head = 2 * pair + side
                delta = jnp.sum(both[side * size : (side + 1) * size], axis=0, keepdims=True)
                query, key, value = head_parts(packed_ref, head, size)
                d_out = d_pair[:, side * size : (side + 1) * size]
                scores = transposed_right(key, query) * scale
                weights = jnp.where(keep, jnp.exp(scores - log_ref[head : head + 1]), 0.0)
                d_value = product(weights.astype(BF), d_out)
                d_probs = transposed_right(value, d_out)
                d_scores = (weights * (d_probs - delta) * scale).astype(BF)
                d_key = product(d_scores, query)
                d_query = transposed_left(key, d_scores).T
                grads += [d_query, d_key, d_value]
            start = 2 * pair * 3 * size
            merged = jnp.concatenate(grads, axis=1).astype(BF)
            out_ref[:, start : start + 6 * size] = merged

    return call(
        body,
        (1,),
        [
            whole(packed.shape),
            whole(attended.shape),
            whole(log_total.shape),
            whole(d_attended.shape),
        ],
        whole(packed.shape),
        jax.ShapeDtypeStruct(packed.shape, BF),
        (order, packed, attended, log_total, d_attended),
    )


class Grid:
    def __init__(self):
        self.dps = lax.axis_size("dp")
        self.cols = lax.axis_size("col")
        self.dp = lax.axis_index("dp")
        self.row = lax.axis_index("row")
        self.col = lax.axis_index("col")

    def hop(self, dp, block, stream):
        mixed = (dp % self.cols) ^ block
        return ((mixed % 2) * 2 + mixed // 2) ^ (2 * stream)

    def along_plane(self, target):
        pairs = []
        for dp in range(self.dps):
            for col in range(self.cols):
                to_dp, to_col = target(dp, col)
                pairs.append((dp * self.cols + col, to_dp * self.cols + to_col % self.cols))
        return pairs

    def spread(self, values, stream):
        return lax.ppermute(
            values, PLANE, self.along_plane(lambda d, c: (d, c + self.hop(d, 0, stream)))
        )

    def bring_back(self, values, stream):
        return lax.ppermute(
            values, PLANE, self.along_plane(lambda d, c: (d, c - self.hop(d, 0, stream)))
        )

    def swap_dp(self, values, bit):
        return lax.ppermute(values, "dp", [(d, d ^ bit) for d in range(self.dps)])

    def swap_row(self, values):
        return lax.ppermute(values, "row", [(0, 1), (1, 0)])

    def col_others(self, values):
        return [
            lax.ppermute(values, "col", [(c, (c + shift) % self.cols) for c in range(self.cols)])
            for shift in range(1, self.cols)
        ]

    def copies(self, values):
        return jnp.broadcast_to(values[None], (self.cols, *values.shape))

    def exchange(self, values):
        return lax.all_to_all(values, "col", 0, 0, tiled=True)

    def everyone(self, values):
        return self.exchange(self.copies(values))

    def order(self):
        hops = [
            self.hop(self.dp, block, stream)
            for stream in (IMAGE, TEXT)
            for block in range(self.cols)
        ]
        return jnp.stack([(self.col - hop) % self.cols for hop in hops]).astype(jnp.int32)

    def piece(self, shard, axis, stream):
        width = shard.shape[axis] // self.cols
        index = (self.col + self.hop(self.dp, 0, stream)) % self.cols
        return lax.dynamic_slice_in_dim(shard, index * width, width, axis)

    def move(self, values, by_row):
        return self.swap_row(values) if by_row else self.swap_dp(values, 2)

    def fold_rest(self, total):
        bit = self.dps // 2
        while bit >= self.cols:
            half = total.shape[0] // 2
            upper = (self.dp // bit) % 2
            keep = lax.dynamic_slice_in_dim(total, upper * half, half, 0)
            send = lax.dynamic_slice_in_dim(total, (1 - upper) * half, half, 0).astype(BF)
            total = keep + self.swap_dp(send, bit).astype(F32)
            bit //= 2
        return total.astype(BF)

    def place(self, by_cols, by_rows):
        share = self.dps // self.cols
        cols_placed, rows_placed = [], []
        for stream, (wide, tall) in enumerate(zip(by_cols, by_rows)):
            pairs = self.along_plane(
                lambda d, c: (c * share + d // self.cols, c - self.hop(d, 0, stream))
            )
            rest = self.fold_rest(tall)
            both = jnp.concatenate([wide, rest.reshape(-1, wide.shape[1])])
            moved = lax.ppermute(both, PLANE, pairs)
            cols_placed.append(moved[: wide.shape[0]])
            rows_placed.append(moved[wide.shape[0] :].reshape(rest.shape))
        return cols_placed, rows_placed

    def place_end(self, parts):
        moved = jnp.stack(parts)
        moved = moved.reshape(len(parts), self.dps, -1, moved.shape[2])
        return lax.all_to_all(moved, "dp", 1, 1, tiled=True)

    def placed(self, moved):
        total = moved.astype(F32).reshape(moved.shape[0], self.cols, -1, *moved.shape[2:])
        total = jnp.sum(total, axis=2)
        return [
            jnp.concatenate([part[col] for col in range(self.cols)], axis=1)[None]
            for part in total
        ]


def after(values, *earlier):
    return lax.optimization_barrier((values, earlier))[0]


def added(parts):
    return sum(part.astype(F32) for part in parts)


def column_sum(parts):
    return jnp.sum(parts.astype(F32), axis=0)


def norm_forward(grid, values):
    width = values.shape[1]
    own_mean = jnp.mean(values, axis=1)
    centred = values - own_mean[:, None]
    packed = jnp.stack([own_mean, jnp.sum(centred * centred, axis=1)])
    everyone = grid.everyone(packed)
    mean = jnp.mean(everyone[:, 0], axis=0)
    squares = jnp.sum(everyone[:, 1] + width * (everyone[:, 0] - mean) ** 2, axis=0)
    inv_std = lax.rsqrt(squares / (width * grid.cols) + EPS)
    return ((values - mean[:, None]) * inv_std[:, None], inv_std[:, None], everyone)


def norm_backward(grid, grad_hat, normed, inv_std):
    full_width = grad_hat.shape[1] * grid.cols
    packed = jnp.stack([jnp.sum(grad_hat, axis=1), jnp.sum(grad_hat * normed, axis=1)])
    total = jnp.sum(grid.everyone(packed), axis=0) / full_width
    return inv_std * (grad_hat - total[0][:, None] - normed * total[1][:, None])


def shards(
    image_in,
    text_in,
    condition,
    image_mod_weight,
    image_mod_bias,
    image_qkv_weight,
    image_qv_bias,
    image_out_weight,
    image_out_bias,
    image_up_weight,
    image_up_bias,
    image_down_weight,
    image_down_bias,
    text_mod_weight,
    text_mod_bias,
    text_qkv_weight,
    text_qv_bias,
    text_out_weight,
    text_out_bias,
    text_up_weight,
    text_up_bias,
    text_down_weight,
    text_down_bias,
    image_cotangent,
    text_cotangent,
):
    grid = Grid()
    streams = (IMAGE, TEXT)
    seq_count = condition.shape[0]
    col_width = image_in.shape[1]
    order = grid.order()
    split = image_in.shape[0]
    count = split + text_in.shape[0]
    padding = -count % 16
    lengths = (split, text_in.shape[0] + padding)
    heads = image_qv_bias.shape[0]
    head_size = image_qv_bias.shape[2]
    mod_weights = (image_mod_weight, text_mod_weight)
    mod_rows = image_mod_weight.shape[0]

    def rows_of(values):
        return (values[:split], values[split:])

    def unpadded(values):
        return (values[:split], values[split:count])

    by_row_first = (True, False)

    def pieces(weights, axis):
        return [grid.piece(weight, axis, s) for s, weight in enumerate(weights)]

    def fetch(parts):
        return [grid.spread(part, s) for s, part in enumerate(parts)]

    def fetch_even(parts, axis):
        groups = []
        for s in streams:
            by_row = by_row_first[s]
            first, second = grid.move(parts[s], by_row), grid.move(parts[s], not by_row)
            corner = grid.move(first, not by_row)
            row_other, block_other = (first, second) if by_row else (second, first)
            edges = (row_other, block_other) if axis == 1 else (block_other, row_other)
            groups.append((parts[s], *edges, corner))
        return assemble(groups)

    def fetch_last(evens):
        return [(even, grid.swap_dp(even, 1)) for even in evens]

    def fold_core(grads):
        return [(even, grid.swap_dp(odd, 1)) for even, odd in grads]

    def cut_axes(axis, first):
        return [axis if by_row == first else 1 - axis for by_row in by_row_first]

    def fold(pairs, axes, first):
        flat = [pair for group in pairs for pair in group]
        halves = add_and_cut(flat, [cut for axis in axes for cut in cut_axes(axis, first)])
        return [halves[2 * group : 2 * group + 2] for group in range(len(pairs))]

    def move(groups, first):
        return [
            [(keep, grid.move(send, by_row_first[s] == first)) for s, (keep, send) in enumerate(group)]
            for group in groups
        ]

    def fold_end(groups):
        sums = add_up([pair for group in groups for pair in group])
        return [sums[2 * group : 2 * group + 2] for group in range(len(groups))]

    def join(parts):
        return jnp.concatenate(parts, axis=0)

    qkv_pieces = pieces((image_qkv_weight, text_qkv_weight), 1)
    out_pieces = pieces((image_out_weight, text_out_weight), 0)
    front_pieces = [
        join([qkv_piece, jnp.pad(out_piece, ((0, 0), (0, qkv_piece.shape[1] - col_width)))])
        for qkv_piece, out_piece in zip(qkv_pieces, out_pieces)
    ]
    front_mine = fetch(front_pieces)
    front_other = [grid.move(front_mine[s], by_row_first[s]) for s in streams]
    image_in, text_in, condition = after((image_in, text_in, condition), front_pieces)

    def padded(parts):
        zeros = jnp.zeros((padding, col_width), F32)
        return join([part.astype(F32) for part in parts] + [zeros])

    act_cond = (condition * jax.nn.sigmoid(condition)).astype(BF)
    partial_mod = jnp.stack(
        [
            jnp.stack([product(act_cond, weight[:, j]) for j in range(6)], axis=1)
            for weight in mod_weights
        ],
        axis=1,
    )
    own_mod = lax.dynamic_index_in_dim(partial_mod, grid.row, 0, False)
    other_mod = lax.dynamic_index_in_dim(partial_mod, 1 - grid.row, 0, False)
    up_count = image_up_bias.shape[0] // grid.cols
    own_qv = jnp.stack([image_qv_bias, text_qv_bias])
    own_up = lax.dynamic_slice_in_dim(
        jnp.stack([image_up_bias, text_up_bias]), grid.col * up_count, up_count, 1
    )
    to_row = [values.reshape(-1, col_width) for values in (other_mod, own_qv, own_up)]
    cuts = (to_row[0].shape[0], to_row[0].shape[0] + to_row[1].shape[0])
    values = padded([image_in, text_in])
    xhat1, inv1, statistics = norm_forward(grid, values)
    to_row = after(jnp.concatenate(to_row), front_mine, statistics)
    from_row = jnp.split(grid.swap_row(to_row), cuts)
    modulation = own_mod + from_row[0].reshape(own_mod.shape)
    modulation = modulation + jnp.stack([image_mod_bias, text_mod_bias])

    def field(position):
        return join(
            [
                jnp.broadcast_to(modulation[s, position], (lengths[s], col_width))
                for s in streams
            ]
        )

    def token_sums(values):
        return jnp.stack([jnp.sum(part, axis=0) for part in rows_of(values)])

    qv_bias = jnp.concatenate([own_qv, from_row[1].reshape(own_qv.shape)], axis=1)
    bias_rows = jnp.stack(
        [qv_bias[:, :, 0], jnp.zeros(qv_bias[:, :, 0].shape, F32), qv_bias[:, :, 1]], axis=2
    ).reshape(2, -1)
    up_bias = jnp.concatenate([own_up, from_row[2].reshape(own_up.shape)], axis=1)
    out_bias = (image_out_bias, text_out_bias)
    down_bias = (image_down_bias, text_down_bias)

    def with_bias(values, bias):
        return join([part + bias[s][None, :] for s, part in enumerate(rows_of(values))])

    def keep_bf16(stream, rows, value, refs):
        refs[-1][rows] = value.astype(BF)

    def add_bias(stream, rows, value, refs):
        refs[1][rows] = (value + refs[0][stream : stream + 1]).astype(BF)

    def into_gelu(stream, rows, value, refs):
        gelu_value, gelu_slope = gelu_parts(value + refs[0][stream : stream + 1])
        refs[1][rows] = gelu_value.astype(BF)
        refs[2][rows] = gelu_slope

    def times_slope(stream, rows, value, refs):
        d_hidden = (value * refs[0][rows]).astype(BF)
        refs[1][rows] = d_hidden
        refs[2][stream : stream + 1] = jnp.sum(d_hidden.astype(F32), axis=0, keepdims=True)

    scale1 = 1.0 + field(1)
    normed1_own = (xhat1 * scale1 + field(0)).astype(BF)
    normed1_copies = after(grid.copies(normed1_own), front_mine)
    normed1 = grid.exchange(normed1_copies)
    front_pairs = [
        join([mine, other])
        for mine, other in zip(front_mine, after(front_other, normed1_copies))
    ]
    front_even = [
        join([front_pairs[s], grid.move(front_pairs[s], not by_row_first[s])]) for s in streams
    ]
    up_weights, down_weights = after(
        ((image_up_weight, text_up_weight), (image_down_weight, text_down_weight)), front_mine
    )
    up_pieces, down_pieces = pieces(up_weights, 1), pieces(down_weights, 0)
    up_mine = fetch(up_pieces)
    grad_out = padded([image_cotangent, text_cotangent])
    gate2 = field(5)
    d_branch2_own = (grad_out * gate2).astype(BF)
    d_branch2_copies = grid.copies(after(d_branch2_own, normed1_copies))
    normed1, front_even, up_mine, down_pieces, d_branch2_copies = lax.optimization_barrier(
        (normed1, front_even, up_mine, down_pieces, d_branch2_copies)
    )
    front_odd = [grid.swap_dp(even, 1) for even in front_even]
    evens = unpack(front_even, col_width, by_row_first)
    odds = unpack(front_odd, col_width, by_row_first)
    qkv_w = [(evens[2 * s], odds[2 * s]) for s in streams]
    out_w = [(evens[2 * s + 1], odds[2 * s + 1]) for s in streams]
    down_mine = fetch(down_pieces)
    d_branch2 = grid.exchange(d_branch2_copies)
    tokens = values.shape[0]
    (packed,) = mix(
        normed1, qkv_w, order, split, False, [bias_rows], [(tokens, BF)], add_bias
    )
    attn, log_total = attend(packed, order, head_size, count)
    attn_out = parts(attn, out_w, order, split, False)
    attn_out, up_mine, down_mine, d_branch2 = lax.optimization_barrier(
        (attn_out, up_mine, down_mine, d_branch2)
    )
    parts_out = grid.exchange(attn_out)
    up_even = fetch_even(up_mine, 1)
    parts_out, up_even, down_mine = lax.optimization_barrier((parts_out, up_even, down_mine))
    branch1 = with_bias(column_sum(parts_out), out_bias)

    gate1 = field(2)
    middle = values + gate1 * branch1
    xhat2, inv2, _ = norm_forward(grid, middle)
    scale2 = 1.0 + field(4)
    normed2_copies = grid.copies((xhat2 * scale2 + field(3)).astype(BF))
    normed2 = grid.exchange(normed2_copies)
    up_w = fetch_last(up_even)
    down_even = fetch_even(after(down_mine, normed2_copies), 0)
    normed2, up_w, down_even = lax.optimization_barrier((normed2, up_w, down_even))
    down_w = fetch_last(down_even)
    gelu, slope = mix(
        normed2, up_w, order, split, False, [up_bias], [(tokens, BF), (tokens, F32)], into_gelu
    )

    d_hidden, up_sums = mix(
        d_branch2, down_w, order, split, True, [slope], [(tokens, BF), (2, F32)], times_slope
    )
    hidden_back = parts(d_hidden, up_w, order, split, True)
    parts_normed2 = grid.exchange(hidden_back)
    gelu_late, d_hidden_late = after((gelu, d_hidden), hidden_back)
    down_fold = fold_core(weight_grads(d_branch2, gelu_late, order, split, False))
    up_fold = fold_core(weight_grads(normed2, d_hidden_late, order, split, True))
    gelu_down = parts(gelu_late, down_w, order, split, False)
    folds = fold([down_fold, up_fold], (0, 1), True)
    parts_normed2, folds, gelu_down = lax.optimization_barrier((parts_normed2, folds, gelu_down))
    folds = move(folds, True)
    d_normed2 = column_sum(parts_normed2)
    d_shift2 = token_sums(d_normed2)
    d_scale2 = token_sums(d_normed2 * xhat2)
    d_middle = grad_out + norm_backward(grid, d_normed2 * scale2, xhat2, inv2)

    d_gate1 = token_sums(d_middle * branch1)
    d_branch1_own = (d_middle * gate1).astype(BF)
    d_branch1 = grid.exchange(grid.copies(d_branch1_own))
    down_fold, up_fold = folds
    d_branch1, gelu_down, down_fold, up_fold = lax.optimization_barrier(
        (d_branch1, gelu_down, down_fold, up_fold)
    )
    parts_branch2 = grid.exchange(gelu_down)
    (d_attn,) = mix(d_branch1, out_w, order, split, True, [], [(tokens, BF)], keep_bf16)
    folds = move(fold([down_fold, up_fold], (0, 1), False), False)
    d_qkv = attend_back(packed, attn, log_total, d_attn, order, head_size, count)
    qkv_back = parts(d_qkv, qkv_w, order, split, True)
    qkv_back, parts_branch2, folds = lax.optimization_barrier((qkv_back, parts_branch2, folds))
    down_fold, up_fold = fold_end(folds)
    parts_normed1 = grid.exchange(qkv_back)
    d_qkv_late, attn_late = after((d_qkv, attn), qkv_back)
    qkv_fold = fold_core(weight_grads(normed1, d_qkv_late, order, split, True))
    out_fold = fold_core(weight_grads(d_branch1, attn_late, order, split, False))
    late_folds = fold([qkv_fold, out_fold], (1, 0), True)
    parts_normed1, late_folds = lax.optimization_barrier((parts_normed1, late_folds))
    down_fold, up_fold = after((down_fold, up_fold), parts_normed1)
    up_placed, down_placed = grid.place(up_fold, down_fold)
    late_folds = move(late_folds, True)
    d_normed1 = column_sum(parts_normed1)
    d_shift1 = token_sums(d_normed1)
    d_scale1 = token_sums(d_normed1 * xhat1)
    norm_back1 = norm_backward(grid, d_normed1 * scale1, xhat1, inv1)
    branch2 = with_bias(column_sum(parts_branch2), down_bias)
    outputs = unpadded((middle + gate2 * branch2).astype(BF))
    d_gate2 = token_sums(grad_out * branch2)
    head_sums = token_sums(d_qkv.astype(F32))
    head_sums = head_sums.reshape(2, 2, heads, 3, head_size)
    head_sums = jnp.stack([head_sums[:, :, :, 0], head_sums[:, :, :, 2]], axis=3)
    vectors = jnp.concatenate(
        [
            jnp.stack([d_shift1, d_scale1, d_gate1, d_shift2, d_scale2, d_gate2], axis=1),
            token_sums(d_branch1_own.astype(F32))[:, None],
            token_sums(d_branch2_own.astype(F32))[:, None],
            head_sums.reshape(2, -1, col_width),
            up_sums.reshape(2, -1, col_width),
        ],
        axis=1,
    ).astype(BF)
    act_all = act_cond
    everyone = jnp.stack([vectors, grid.swap_row(vectors)])
    bit = grid.dps // 2
    while bit:
        everyone = jnp.concatenate([everyone, grid.swap_dp(everyone, bit)])
        act_all = jnp.concatenate([act_all, grid.swap_dp(after(act_all, vectors), bit)])
        bit //= 2
    norm_back1, late_folds, everyone, act_all = lax.optimization_barrier(
        (norm_back1, late_folds, everyone, act_all)
    )
    late_folds = move(fold(late_folds, (1, 0), False), False)
    late_folds, up_placed, down_placed = lax.optimization_barrier(
        (late_folds, up_placed, down_placed)
    )
    qkv_fold, out_fold = fold_end(late_folds)
    qkv_placed, out_placed = grid.place(qkv_fold, out_fold)
    up_moved = grid.place_end(up_placed)

    in_grads = unpadded(d_middle + norm_back1)
    vector_sums = jnp.sum(everyone.astype(F32), axis=0)
    feature_share = col_width // grid.dps
    shares = lax.dynamic_slice_in_dim(vector_sums, grid.dp * feature_share, feature_share, 2)

    def over_rows(rows, shape):
        halves = rows.reshape(grid.dps, 2, 2, 2, -1).astype(F32)
        total = jnp.sum(halves[:, 0, :, 0] + halves[:, 1, :, 1], axis=0)
        return total.reshape(2, *shape)

    head_rows = 2 * heads * 2 * head_size // col_width
    head_total = over_rows(everyone[:, :, 8 : 8 + head_rows], (heads, 2, head_size))
    up_total_own = over_rows(everyone[:, :, 8 + head_rows :], (up_count,))
    head_share = head_size // grid.dps
    head_total = lax.dynamic_slice_in_dim(head_total, grid.dp * head_share, head_share, 3)
    qv_b_grad = jnp.transpose(head_total, (0, 3, 1, 2))

    by_row = everyone[:, :, :6].reshape(grid.dps, 2, 2, 6, col_width)
    d_mod = jnp.where(grid.row == 0, by_row, by_row[:, ::-1]).reshape(-1, 2, 6, col_width)
    mod_share = mod_rows // grid.dps
    act_share = lax.dynamic_slice_in_dim(act_all, grid.dp * mod_share, mod_share, 1)
    mod_w_grad = modulation_grads(after(act_share, late_folds), d_mod, 6)
    own_d_mod = after(d_mod[:seq_count], late_folds)
    cond_part = condition_part(own_d_mod, mod_weights)
    last = jnp.stack([cond_part, up_total_own])
    lasts = [last] + grid.col_others(last)
    lasts, qkv_placed, out_placed, up_moved = lax.optimization_barrier(
        (lasts, qkv_placed, out_placed, up_moved)
    )
    qkv_moved = grid.place_end(qkv_placed)
    cond_sum = sum(item[0] for item in lasts)
    up_share = up_count * grid.cols // grid.dps
    up_from = (grid.col - grid.dp * grid.cols // grid.dps) % grid.cols
    up_chosen = sum(jnp.where(up_from == j, lasts[j][1], 0.0) for j in range(grid.cols))
    up_start = (grid.dp % (grid.dps // grid.cols)) * up_share
    up_b_grad = lax.dynamic_slice_in_dim(up_chosen, up_start, up_share, 1)
    qkv_total, up_total = grid.placed(qkv_moved), grid.placed(up_moved)
    down_total = [down_placed[s].astype(F32)[None] for s in streams]
    out_total = [out_placed[s].astype(F32)[None] for s in streams]
    sigmoid_cond = jax.nn.sigmoid(condition)
    condition_grad = cond_sum * sigmoid_cond * (1.0 + condition * (1.0 - sigmoid_cond))

    grads = []
    for s in streams:
        grads += [
            mod_w_grad[s],
            jnp.transpose(shares[s, :6])[None],
            qkv_total[s],
            qv_b_grad[s],
            out_total[s],
            shares[s, 6][None],
            up_total[s],
            up_b_grad[s][None],
            down_total[s],
            shares[s, 7][None],
        ]
    return (*outputs, *in_grads, condition_grad, *grads)


def solution(mesh):
    in_specs = (
        P(("dp", "row"), "col"),
        P(("dp", "row"), "col"),
        P("dp", "row"),
        P("row", None, "col"),
        P(None, "col"),
        P("col", "row"),
        P(("row", "col"), None, None),
        P("row", "col"),
        P("col"),
        P("col", "row"),
        P("row"),
        P("row", "col"),
        P("col"),
        P("row", None, "col"),
        P(None, "col"),
        P("col", "row"),
        P(("row", "col"), None, None),
        P("row", "col"),
        P("col"),
        P("col", "row"),
        P("row"),
        P("row", "col"),
        P("col"),
        P(("dp", "row"), "col"),
        P(("dp", "row"), "col"),
    )
    out_specs = (
        P(("dp", "row"), "col"),
        P(("dp", "row"), "col"),
        P(("dp", "row"), "col"),
        P(("dp", "row"), "col"),
        P("dp", "row"),
        P("row", "dp", None, "col"),
        P("col", "dp", None),
        P("col", "dp", "row"),
        P("dp", ("row", "col"), None),
        P("row", "dp", "col"),
        P("col", "dp"),
        P("col", "dp", "row"),
        P("row", "dp"),
        P("row", "dp", "col"),
        P("col", "dp"),
        P("row", "dp", None, "col"),
        P("col", "dp", None),
        P("col", "dp", "row"),
        P("dp", ("row", "col"), None),
        P("row", "dp", "col"),
        P("col", "dp"),
        P("col", "dp", "row"),
        P("row", "dp"),
        P("row", "dp", "col"),
        P("col", "dp"),
    )
    return jax.shard_map(shards, mesh=mesh, in_specs=in_specs, out_specs=out_specs, check_vma=False)
```

```python
import jax
import jax.numpy as jnp
from jax import lax
from jax.experimental import pallas as pl
from jax.experimental.pallas import tpu as pltpu
from jax.sharding import PartitionSpec as P

EPS = 1e-06
GELU_C = 0.7978845608028654
GELU_K = 0.044715
BF = jnp.bfloat16
F32 = jnp.float32
PLANE = ("dp", "col")
IMAGE, TEXT = 0, 1


def gelu_parts(hidden):
    tangent = jnp.tanh(GELU_C * (hidden + GELU_K * hidden * hidden * hidden))
    gelu_value = 0.5 * hidden * (1.0 + tangent)
    gelu_slope = 0.5 * (1.0 + tangent) + 0.5 * hidden * (1.0 - tangent * tangent) * GELU_C * (
        1.0 + 3.0 * GELU_K * hidden * hidden
    )
    return (gelu_value, gelu_slope)


def transposed_left(left_side, right_side):
    return lax.dot_general(
        left_side, right_side, (((0,), (0,)), ((), ())), preferred_element_type=F32
    )


def transposed_right(left_side, right_side):
    return lax.dot_general(
        left_side, right_side, (((1,), (1,)), ((), ())), preferred_element_type=F32
    )


def product(left_side, right_side):
    return jnp.dot(left_side, right_side, preferred_element_type=F32)


VMEM_BYTES = 56 * 1024 * 1024
FREE = pl.CostEstimate(flops=0, bytes_accessed=0, transcendentals=0)


def call(body, grid, in_specs, out_specs, out_shape, operands):
    return pl.pallas_call(
        body,
        grid_spec=pltpu.PrefetchScalarGridSpec(
            num_scalar_prefetch=1, grid=grid, in_specs=in_specs, out_specs=out_specs
        ),
        out_shape=out_shape,
        cost_estimate=FREE,
        compiler_params=pltpu.CompilerParams(vmem_limit_bytes=VMEM_BYTES),
    )(*operands)


def whole(shape):
    return pl.BlockSpec(shape, lambda step, order: (0,) * len(shape))


def on_rows(shape):
    return pl.BlockSpec(shape, lambda step, order: (step, 0))


def on_columns(shape):
    return pl.BlockSpec(shape, lambda step, order: (0, step))


def mix(columns, weights, order, split, back, extra, outs, finish):
    tokens, width = columns.shape[1:]
    total = weights[0][0].shape[0 if back else 1]
    block = 512 if total % 512 == 0 else width
    pair = (block, 2 * width) if back else (2 * width, block)
    ranges = ((0, split), (split, tokens))

    def body(order_ref, columns_ref, *refs):
        multiply = transposed_right if back else product
        for stream, (low, high) in enumerate(ranges):
            blocks = [columns_ref[order_ref[4 * stream + b], low:high] for b in range(4)]
            even = jnp.concatenate([blocks[0], blocks[2]], axis=1)
            odd = jnp.concatenate([blocks[1], blocks[3]], axis=1)
            value = multiply(even, refs[2 * stream][...]) + multiply(odd, refs[2 * stream + 1][...])
            finish(stream, slice(low, high), value, refs[4:])

    return call(
        body,
        (total // block,),
        [whole(columns.shape)]
        + [on_rows(pair) if back else on_columns(pair)] * 4
        + [on_columns((item.shape[0], block)) for item in extra],
        [on_columns((rows, block)) for rows, _ in outs],
        [jax.ShapeDtypeStruct((rows, total), kind) for rows, kind in outs],
        (order, columns, *weights[0], *weights[1], *extra),
    )


def parts(inputs, weights, order, split, back):
    tokens, depth = inputs.shape
    width = weights[0][0].shape[0 if back else 1] // 2
    pair = (width, depth) if back else (depth, width)
    ranges = ((0, split), (split, tokens))

    def body(order_ref, inputs_ref, *refs):
        multiply = transposed_right if back else product
        for half in range(2):
            for stream, (low, high) in enumerate(ranges):
                place = order_ref[4 * stream + 2 * pl.program_id(0) + half]
                value = multiply(inputs_ref[low:high], refs[2 * stream + half][...])
                refs[4][place, low:high] = value.astype(BF)

    return call(
        body,
        (2,),
        [whole(inputs.shape)] + [on_rows(pair) if back else on_columns(pair)] * 4,
        whole((4, tokens, width)),
        jax.ShapeDtypeStruct((4, tokens, width), BF),
        (order, inputs, *weights[0], *weights[1]),
    )


def weight_grads(columns, inputs, order, split, back):
    tokens, width = columns.shape[1:]
    depth = inputs.shape[1]
    shape = (2 * width, depth) if back else (depth, 2 * width)
    pair = (width, depth) if back else (depth, width)
    ranges = ((0, split), (split, tokens))

    def body(order_ref, columns_ref, inputs_ref, *refs):
        for half in range(2):
            for stream, (low, high) in enumerate(ranges):
                place = order_ref[4 * stream + 2 * pl.program_id(0) + half]
                column = columns_ref[place, low:high]
                other = inputs_ref[low:high]
                if back:
                    value = transposed_left(column, other)
                else:
                    value = transposed_left(other, column)
                refs[2 * stream + half][...] = value.astype(BF)

    grads = call(
        body,
        (2,),
        [whole(columns.shape), whole(inputs.shape)],
        [on_rows(pair) if back else on_columns(pair)] * 4,
        [jax.ShapeDtypeStruct(shape, BF)] * 4,
        (order, columns, inputs),
    )
    return [(grads[0], grads[1]), (grads[2], grads[3])]


def steps_for(extents, lanes):
    tile = 128 if lanes else 16
    return 3 if all(extent % (3 * tile) == 0 for extent in extents) else 1


def assemble(groups):
    shapes = [(2 * group[0].shape[0], 2 * group[0].shape[1]) for group in groups]

    def body(order_ref, *refs):
        for item, (rows, _) in enumerate(shapes):
            out_ref = refs[4 * len(groups) + item]
            for side in range(2):

                @pl.when(pl.program_id(0) == side)
                def _():
                    out_ref[: rows // 2] = refs[4 * item + side][...]
                    out_ref[rows // 2 :] = refs[4 * item + 2 + side][...]

    flat = [array for group in groups for array in group]
    return call(
        body,
        (2,),
        [whole(array.shape) for array in flat],
        [on_columns((rows, columns // 2)) for rows, columns in shapes],
        [jax.ShapeDtypeStruct(shape, BF) for shape in shapes],
        (jnp.zeros((1,), jnp.int32), *flat),
    )


def add_and_cut(pairs, cuts):
    over_columns = [pair[0].shape[1] for pair, cut in zip(pairs, cuts) if cut == 0]
    over_rows = [pair[0].shape[0] for pair, cut in zip(pairs, cuts) if cut == 1]
    steps = min(steps_for(over_columns, True), steps_for(over_rows, False))
    in_specs, out_specs, out_shape = [], [], []
    for (first, _), cut in zip(pairs, cuts):
        rows, columns = first.shape
        if cut == 0:
            in_specs += [on_columns((rows, columns // steps))] * 2
            out_specs += [on_columns((rows // 2, columns // steps))] * 2
            out_shape += [jax.ShapeDtypeStruct((rows // 2, columns), BF)] * 2
        else:
            in_specs += [on_rows((rows // steps, columns))] * 2
            out_specs += [on_rows((rows // steps, columns // 2))] * 2
            out_shape += [jax.ShapeDtypeStruct((rows, columns // 2), BF)] * 2

    def body(order_ref, *refs):
        for item, cut in enumerate(cuts):
            total = refs[2 * item][...].astype(F32) + refs[2 * item + 1][...].astype(F32)
            total = total.astype(BF)
            outs = refs[2 * len(cuts) + 2 * item :]
            half = total.shape[cut] // 2
            outs[0][...] = total[:half] if cut == 0 else total[:, :half]
            outs[1][...] = total[half:] if cut == 0 else total[:, half:]

    flat = [array for pair in pairs for array in pair]
    halves = call(
        body, (steps,), in_specs, out_specs, out_shape, (jnp.zeros((1,), jnp.int32), *flat)
    )
    return [(halves[2 * item], halves[2 * item + 1]) for item in range(len(pairs))]


def add_and_stack(wides, talls):
    shapes = []
    for (wide, _), (tall, _) in zip(wides, talls):
        beside = wide.shape[1] // tall.shape[1]
        shapes.append((wide.shape[0] + tall.shape[0] // beside, wide.shape[1]))

    def body(order_ref, *refs):
        for item, (rows, columns) in enumerate(shapes):
            wide, wide_other, tall, tall_other = refs[4 * item : 4 * item + 4]
            out_ref = refs[4 * len(shapes) + item]
            top, width = wide.shape[0], tall.shape[1]
            out_ref[:top] = (wide[...].astype(F32) + wide_other[...].astype(F32)).astype(BF)
            total = (tall[...].astype(F32) + tall_other[...].astype(F32)).astype(BF)
            for part in range(columns // width):
                piece = total[part * (rows - top) : (part + 1) * (rows - top)]
                out_ref[top:, part * width : (part + 1) * width] = piece
            if columns % width:
                out_ref[top:, columns - columns % width :] = jnp.zeros(
                    (rows - top, columns % width), BF
                )

    flat = [array for pairs in zip(wides, talls) for pair in pairs for array in pair]
    return call(
        body,
        (1,),
        [whole(array.shape) for array in flat],
        [whole(shape) for shape in shapes],
        [jax.ShapeDtypeStruct(shape, BF) for shape in shapes],
        (jnp.zeros((1,), jnp.int32), *flat),
    )


def unpack(fronts, width, by_row_first):
    rows, columns = fronts[0].shape[0] // 4, fronts[0].shape[1]
    deep = rows - width

    def body(order_ref, *refs):
        shorter = rows - width
        for stream, by_row in enumerate(by_row_first):
            front_ref, qkv_ref, out_ref = refs[stream], refs[2 + 2 * stream], refs[3 + 2 * stream]
            for block in range(2):
                qkv_halves = []
                for half in range(2):
                    start = rows * (2 * block + half if by_row else 2 * half + block)
                    qkv_halves.append(front_ref[start : start + width])
                    lanes = slice(block * width, (block + 1) * width)
                    out_ref[half * shorter : (half + 1) * shorter, lanes] = front_ref[
                        start + width : start + rows, :width
                    ]
                qkv_ref[block * width : (block + 1) * width] = jnp.concatenate(qkv_halves, axis=1)

    shapes = [(2 * width, 2 * columns), (2 * deep, 2 * width)] * 2
    return call(
        body,
        (1,),
        [whole(front.shape) for front in fronts],
        [whole(shape) for shape in shapes],
        [jax.ShapeDtypeStruct(shape, BF) for shape in shapes],
        (jnp.zeros((1,), jnp.int32), *fronts),
    )


def rows_for(values, rows):
    gap = rows - values.shape[-2]
    return jnp.pad(values, [(0, 0)] * (values.ndim - 2) + [(0, gap), (0, 0)])


def modulation_grads(act, d_mod, mod_rows):
    sequences, count = act.shape
    width = d_mod.shape[-1]
    act = act.astype(F32)
    d_mod = jnp.moveaxis(d_mod, 0, 2).astype(F32).reshape(-1, sequences, width)

    def body(order_ref, act_ref, d_ref, *refs):
        for stream in range(2):
            d_row = d_ref[stream * mod_rows + pl.program_id(0)].astype(BF)
            refs[stream][0] = transposed_left(act_ref[...].astype(BF), d_row)

    spec = pl.BlockSpec((1, count, width), lambda step, order: (step, 0, 0))
    grads = call(
        body,
        (mod_rows,),
        [whole(act.shape), whole(d_mod.shape)],
        [spec] * 2,
        [jax.ShapeDtypeStruct((mod_rows, count, width), F32)] * 2,
        (jnp.zeros((1,), jnp.int32), act, d_mod),
    )
    return [jnp.transpose(grad, (1, 0, 2))[None] for grad in grads]


def condition_part(d_mod, weights):
    sequences, _, mod_rows, width = d_mod.shape
    inputs = weights[0].shape[0]
    d_mod = jnp.moveaxis(d_mod, 0, 2).astype(F32).reshape(-1, sequences, width)
    d_mod = rows_for(d_mod, 8)

    def body(order_ref, d_ref, image_ref, text_ref, out_ref):
        @pl.when(pl.program_id(0) == 0)
        def _():
            out_ref[...] = jnp.zeros_like(out_ref)

        for stream, weight_ref in enumerate((image_ref, text_ref)):
            d_row = d_ref[stream * mod_rows + pl.program_id(0)].astype(BF)
            out_ref[...] += transposed_right(d_row, weight_ref[0])

    spec = pl.BlockSpec((1, inputs, width), lambda step, order: (step, 0, 0))
    total = call(
        body,
        (mod_rows,),
        [whole(d_mod.shape), spec, spec],
        whole((8, inputs)),
        jax.ShapeDtypeStruct((8, inputs), F32),
        (jnp.zeros((1,), jnp.int32), d_mod, *[jnp.transpose(w, (1, 0, 2)) for w in weights]),
    )
    return total[:sequences]


def head_parts(packed_ref, head, size):
    start = head * 3 * size
    return [packed_ref[:, start + j * size : start + (j + 1) * size] for j in range(3)]


def attend(packed, order, size, count):
    tokens = packed.shape[0]
    heads = packed.shape[1] // (3 * size)
    scale = size ** (-0.5)

    def body(order_ref, packed_ref, out_ref, log_ref):
        keep = lax.broadcasted_iota(jnp.int32, (tokens, tokens), 0) < count
        for pair in range(heads // 2):
            attended = []
            for head in (2 * pair, 2 * pair + 1):
                query, key, value = head_parts(packed_ref, head, size)
                scores = transposed_right(key, query) * scale
                powers = jnp.where(keep, jnp.exp(scores), 0.0)
                log_total = jnp.log(jnp.sum(powers, axis=0, keepdims=True))
                log_ref[head : head + 1] = log_total
                probs = jnp.where(keep, jnp.exp(scores - log_total), 0.0).astype(BF)
                attended.append(transposed_left(value, probs))
            both = jnp.concatenate(attended, axis=0)
            out_ref[:, 2 * pair * size : 2 * (pair + 1) * size] = both.T.astype(BF)

    return call(
        body,
        (1,),
        [whole(packed.shape)],
        [whole((tokens, heads * size)), whole((heads, tokens))],
        [
            jax.ShapeDtypeStruct((tokens, heads * size), BF),
            jax.ShapeDtypeStruct((heads, tokens), F32),
        ],
        (order, packed),
    )


def attend_back(packed, attended, log_total, d_attended, order, size, count):
    tokens = packed.shape[0]
    heads = packed.shape[1] // (3 * size)
    scale = size ** (-0.5)

    def body(order_ref, packed_ref, attended_ref, log_ref, d_ref, out_ref):
        keep = lax.broadcasted_iota(jnp.int32, (tokens, tokens), 0) < count
        for pair in range(heads // 2):
            lanes = slice(2 * pair * size, 2 * (pair + 1) * size)
            d_pair = d_ref[:, lanes]
            both = d_pair.astype(F32) * attended_ref[:, lanes].astype(F32)
            both = both.T
            grads = []
            for side in range(2):
                head = 2 * pair + side
                delta = jnp.sum(both[side * size : (side + 1) * size], axis=0, keepdims=True)
                query, key, value = head_parts(packed_ref, head, size)
                d_out = d_pair[:, side * size : (side + 1) * size]
                scores = transposed_right(key, query) * scale
                weights = jnp.where(keep, jnp.exp(scores - log_ref[head : head + 1]), 0.0)
                d_value = product(weights.astype(BF), d_out)
                d_probs = transposed_right(value, d_out)
                d_scores = (weights * (d_probs - delta) * scale).astype(BF)
                d_key = product(d_scores, query)
                d_query = transposed_left(key, d_scores).T
                grads += [d_query, d_key, d_value]
            start = 2 * pair * 3 * size
            merged = jnp.concatenate(grads, axis=1).astype(BF)
            out_ref[:, start : start + 6 * size] = merged

    return call(
        body,
        (1,),
        [
            whole(packed.shape),
            whole(attended.shape),
            whole(log_total.shape),
            whole(d_attended.shape),
        ],
        whole(packed.shape),
        jax.ShapeDtypeStruct(packed.shape, BF),
        (order, packed, attended, log_total, d_attended),
    )


class Grid:
    def __init__(self):
        self.dps = lax.axis_size("dp")
        self.cols = lax.axis_size("col")
        self.dp = lax.axis_index("dp")
        self.row = lax.axis_index("row")
        self.col = lax.axis_index("col")

    def hop(self, dp, block, stream):
        mixed = (dp % self.cols) ^ block
        return ((mixed % 2) * 2 + mixed // 2) ^ (2 * stream)

    def along_plane(self, target):
        pairs = []
        for dp in range(self.dps):
            for col in range(self.cols):
                to_dp, to_col = target(dp, col)
                pairs.append((dp * self.cols + col, to_dp * self.cols + to_col % self.cols))
        return pairs

    def spread(self, values, stream):
        return lax.ppermute(
            values, PLANE, self.along_plane(lambda d, c: (d, c + self.hop(d, 0, stream)))
        )

    def bring_back(self, values, stream):
        return lax.ppermute(
            values, PLANE, self.along_plane(lambda d, c: (d, c - self.hop(d, 0, stream)))
        )

    def swap_dp(self, values, bit):
        return lax.ppermute(values, "dp", [(d, d ^ bit) for d in range(self.dps)])

    def swap_row(self, values):
        return lax.ppermute(values, "row", [(0, 1), (1, 0)])

    def col_others(self, values):
        return [
            lax.ppermute(values, "col", [(c, (c + shift) % self.cols) for c in range(self.cols)])
            for shift in range(1, self.cols)
        ]

    def copies(self, values):
        return jnp.broadcast_to(values[None], (self.cols, *values.shape))

    def exchange(self, values):
        return lax.all_to_all(values, "col", 0, 0, tiled=True)

    def everyone(self, values):
        return self.exchange(self.copies(values))

    def order(self):
        hops = [
            self.hop(self.dp, block, stream)
            for stream in (IMAGE, TEXT)
            for block in range(self.cols)
        ]
        return jnp.stack([(self.col - hop) % self.cols for hop in hops]).astype(jnp.int32)

    def piece(self, shard, axis, stream):
        width = shard.shape[axis] // self.cols
        index = (self.col + self.hop(self.dp, 0, stream)) % self.cols
        return lax.dynamic_slice_in_dim(shard, index * width, width, axis)

    def move(self, values, by_row):
        return self.swap_row(values) if by_row else self.swap_dp(values, 2)

    def fold_rest(self, pair):
        bit = self.dps // 2
        while bit >= self.cols:
            total = pair[0].astype(F32) + pair[1].astype(F32)
            half = total.shape[0] // 2
            upper = (self.dp // bit) % 2
            keep = lax.dynamic_slice_in_dim(total, upper * half, half, 0).astype(BF)
            send = lax.dynamic_slice_in_dim(total, (1 - upper) * half, half, 0).astype(BF)
            pair = (keep, self.swap_dp(send, bit))
            bit //= 2
        return pair

    def place(self, wides, talls):
        share = self.dps // self.cols
        if share > 1:
            talls = [self.fold_rest(pair) for pair in talls]
        cols_placed, rows_placed = [], []
        for stream, both in enumerate(add_and_stack(wides, talls)):
            pairs = self.along_plane(
                lambda d, c: (c * share + d // self.cols, c - self.hop(d, 0, stream))
            )
            moved = lax.ppermute(both, PLANE, pairs)
            top, width = wides[stream][0].shape[0], talls[stream][0].shape[1]
            cols_placed.append(moved[:top])
            parts = [
                moved[top:, part * width : (part + 1) * width]
                for part in range(moved.shape[1] // width)
            ]
            rows_placed.append(jnp.concatenate(parts))
        return cols_placed, rows_placed

    def place_end(self, parts):
        moved = jnp.stack(parts)
        moved = moved.reshape(len(parts), self.dps, -1, moved.shape[2])
        return lax.all_to_all(moved, "dp", 1, 1, tiled=True)

    def placed(self, moved):
        total = moved.astype(F32).reshape(moved.shape[0], self.cols, -1, *moved.shape[2:])
        total = jnp.sum(total, axis=2)
        return [
            jnp.concatenate([part[col] for col in range(self.cols)], axis=1)[None]
            for part in total
        ]


def after(values, *earlier):
    return lax.optimization_barrier((values, earlier))[0]


def added(parts):
    return sum(part.astype(F32) for part in parts)


def column_sum(parts):
    return jnp.sum(parts.astype(F32), axis=0)


def norm_forward(grid, values):
    width = values.shape[1]
    own_mean = jnp.mean(values, axis=1)
    centred = values - own_mean[:, None]
    packed = jnp.stack([own_mean, jnp.sum(centred * centred, axis=1)])
    everyone = grid.everyone(packed)
    mean = jnp.mean(everyone[:, 0], axis=0)
    squares = jnp.sum(everyone[:, 1] + width * (everyone[:, 0] - mean) ** 2, axis=0)
    inv_std = lax.rsqrt(squares / (width * grid.cols) + EPS)
    return ((values - mean[:, None]) * inv_std[:, None], inv_std[:, None], everyone)


def norm_backward(grid, grad_hat, normed, inv_std):
    full_width = grad_hat.shape[1] * grid.cols
    packed = jnp.stack([jnp.sum(grad_hat, axis=1), jnp.sum(grad_hat * normed, axis=1)])
    total = jnp.sum(grid.everyone(packed), axis=0) / full_width
    return inv_std * (grad_hat - total[0][:, None] - normed * total[1][:, None])


def shards(
    image_in,
    text_in,
    condition,
    image_mod_weight,
    image_mod_bias,
    image_qkv_weight,
    image_qv_bias,
    image_out_weight,
    image_out_bias,
    image_up_weight,
    image_up_bias,
    image_down_weight,
    image_down_bias,
    text_mod_weight,
    text_mod_bias,
    text_qkv_weight,
    text_qv_bias,
    text_out_weight,
    text_out_bias,
    text_up_weight,
    text_up_bias,
    text_down_weight,
    text_down_bias,
    image_cotangent,
    text_cotangent,
):
    grid = Grid()
    streams = (IMAGE, TEXT)
    seq_count = condition.shape[0]
    col_width = image_in.shape[1]
    order = grid.order()
    split = image_in.shape[0]
    count = split + text_in.shape[0]
    padding = -count % 16
    lengths = (split, text_in.shape[0] + padding)
    heads = image_qv_bias.shape[0]
    head_size = image_qv_bias.shape[2]
    mod_weights = (image_mod_weight, text_mod_weight)
    mod_rows = image_mod_weight.shape[0]

    def rows_of(values):
        return (values[:split], values[split:])

    def unpadded(values):
        return (values[:split], values[split:count])

    by_row_first = (True, False)

    def pieces(weights, axis):
        return [grid.piece(weight, axis, s) for s, weight in enumerate(weights)]

    def fetch(parts):
        return [grid.spread(part, s) for s, part in enumerate(parts)]

    def fetch_even(parts, axis):
        groups = []
        for s in streams:
            by_row = by_row_first[s]
            first, second = grid.move(parts[s], by_row), grid.move(parts[s], not by_row)
            corner = grid.move(first, not by_row)
            row_other, block_other = (first, second) if by_row else (second, first)
            edges = (row_other, block_other) if axis == 1 else (block_other, row_other)
            groups.append((parts[s], *edges, corner))
        return assemble(groups)

    def fetch_last(evens):
        return [(even, grid.swap_dp(even, 1)) for even in evens]

    def fold_core(grads):
        return [(even, grid.swap_dp(odd, 1)) for even, odd in grads]

    def cut_axes(axis, first):
        return [axis if by_row == first else 1 - axis for by_row in by_row_first]

    def fold(pairs, axes, first):
        flat = [pair for group in pairs for pair in group]
        halves = add_and_cut(flat, [cut for axis in axes for cut in cut_axes(axis, first)])
        return [halves[2 * group : 2 * group + 2] for group in range(len(pairs))]

    def move(groups, first):
        return [
            [(keep, grid.move(send, by_row_first[s] == first)) for s, (keep, send) in enumerate(group)]
            for group in groups
        ]

    def join(parts):
        return jnp.concatenate(parts, axis=0)

    qkv_pieces = pieces((image_qkv_weight, text_qkv_weight), 1)
    out_pieces = pieces((image_out_weight, text_out_weight), 0)
    front_pieces = [
        join([qkv_piece, jnp.pad(out_piece, ((0, 0), (0, qkv_piece.shape[1] - col_width)))])
        for qkv_piece, out_piece in zip(qkv_pieces, out_pieces)
    ]
    front_mine = fetch(front_pieces)
    front_other = [grid.move(front_mine[s], by_row_first[s]) for s in streams]
    image_in, text_in, condition = after((image_in, text_in, condition), front_pieces)

    def padded(parts):
        zeros = jnp.zeros((padding, col_width), F32)
        return join([part.astype(F32) for part in parts] + [zeros])

    act_cond = (condition * jax.nn.sigmoid(condition)).astype(BF)
    partial_mod = jnp.stack(
        [
            jnp.stack([product(act_cond, weight[:, j]) for j in range(6)], axis=1)
            for weight in mod_weights
        ],
        axis=1,
    )
    own_mod = lax.dynamic_index_in_dim(partial_mod, grid.row, 0, False)
    other_mod = lax.dynamic_index_in_dim(partial_mod, 1 - grid.row, 0, False)
    up_count = image_up_bias.shape[0] // grid.cols
    own_qv = jnp.stack([image_qv_bias, text_qv_bias])
    own_up = lax.dynamic_slice_in_dim(
        jnp.stack([image_up_bias, text_up_bias]), grid.col * up_count, up_count, 1
    )
    to_row = [values.reshape(-1, col_width) for values in (other_mod, own_qv, own_up)]
    cuts = (to_row[0].shape[0], to_row[0].shape[0] + to_row[1].shape[0])
    values = padded([image_in, text_in])
    xhat1, inv1, statistics = norm_forward(grid, values)
    to_row = after(jnp.concatenate(to_row), front_mine, statistics)
    from_row = jnp.split(grid.swap_row(to_row), cuts)
    modulation = own_mod + from_row[0].reshape(own_mod.shape)
    modulation = modulation + jnp.stack([image_mod_bias, text_mod_bias])

    def field(position):
        return join(
            [
                jnp.broadcast_to(modulation[s, position], (lengths[s], col_width))
                for s in streams
            ]
        )

    def token_sums(values):
        return jnp.stack([jnp.sum(part, axis=0) for part in rows_of(values)])

    qv_bias = jnp.concatenate([own_qv, from_row[1].reshape(own_qv.shape)], axis=1)
    bias_rows = jnp.stack(
        [qv_bias[:, :, 0], jnp.zeros(qv_bias[:, :, 0].shape, F32), qv_bias[:, :, 1]], axis=2
    ).reshape(2, -1)
    up_bias = jnp.concatenate([own_up, from_row[2].reshape(own_up.shape)], axis=1)
    out_bias = (image_out_bias, text_out_bias)
    down_bias = (image_down_bias, text_down_bias)

    def with_bias(values, bias):
        return join([part + bias[s][None, :] for s, part in enumerate(rows_of(values))])

    def keep_bf16(stream, rows, value, refs):
        refs[-1][rows] = value.astype(BF)

    def add_bias(stream, rows, value, refs):
        refs[1][rows] = (value + refs[0][stream : stream + 1]).astype(BF)

    def into_gelu(stream, rows, value, refs):
        gelu_value, gelu_slope = gelu_parts(value + refs[0][stream : stream + 1])
        refs[1][rows] = gelu_value.astype(BF)
        refs[2][rows] = gelu_slope

    def times_slope(stream, rows, value, refs):
        d_hidden = (value * refs[0][rows]).astype(BF)
        refs[1][rows] = d_hidden
        refs[2][stream : stream + 1] = jnp.sum(d_hidden.astype(F32), axis=0, keepdims=True)

    scale1 = 1.0 + field(1)
    normed1_own = (xhat1 * scale1 + field(0)).astype(BF)
    normed1_copies = after(grid.copies(normed1_own), front_mine)
    normed1 = grid.exchange(normed1_copies)
    front_pairs = [
        join([mine, other])
        for mine, other in zip(front_mine, after(front_other, normed1_copies))
    ]
    front_even = [
        join([front_pairs[s], grid.move(front_pairs[s], not by_row_first[s])]) for s in streams
    ]
    up_weights, down_weights = after(
        ((image_up_weight, text_up_weight), (image_down_weight, text_down_weight)), front_mine
    )
    up_pieces, down_pieces = pieces(up_weights, 1), pieces(down_weights, 0)
    up_mine = fetch(up_pieces)
    grad_out = padded([image_cotangent, text_cotangent])
    gate2 = field(5)
    d_branch2_own = (grad_out * gate2).astype(BF)
    d_branch2_copies = grid.copies(after(d_branch2_own, normed1_copies))
    normed1, front_even, up_mine, down_pieces, d_branch2_copies = lax.optimization_barrier(
        (normed1, front_even, up_mine, down_pieces, d_branch2_copies)
    )
    front_odd = [grid.swap_dp(even, 1) for even in front_even]
    evens = unpack(front_even, col_width, by_row_first)
    odds = unpack(front_odd, col_width, by_row_first)
    qkv_w = [(evens[2 * s], odds[2 * s]) for s in streams]
    out_w = [(evens[2 * s + 1], odds[2 * s + 1]) for s in streams]
    down_mine = fetch(down_pieces)
    d_branch2 = grid.exchange(d_branch2_copies)
    tokens = values.shape[0]
    (packed,) = mix(
        normed1, qkv_w, order, split, False, [bias_rows], [(tokens, BF)], add_bias
    )
    attn, log_total = attend(packed, order, head_size, count)
    attn_out = parts(attn, out_w, order, split, False)
    attn_out, up_mine, down_mine, d_branch2 = lax.optimization_barrier(
        (attn_out, up_mine, down_mine, d_branch2)
    )
    parts_out = grid.exchange(attn_out)
    up_even = fetch_even(up_mine, 1)
    parts_out, up_even, down_mine = lax.optimization_barrier((parts_out, up_even, down_mine))
    branch1 = with_bias(column_sum(parts_out), out_bias)

    gate1 = field(2)
    middle = values + gate1 * branch1
    xhat2, inv2, _ = norm_forward(grid, middle)
    scale2 = 1.0 + field(4)
    normed2_copies = grid.copies((xhat2 * scale2 + field(3)).astype(BF))
    normed2 = grid.exchange(normed2_copies)
    up_w = fetch_last(up_even)
    down_even = fetch_even(after(down_mine, normed2_copies), 0)
    normed2, up_w, down_even = lax.optimization_barrier((normed2, up_w, down_even))
    down_w = fetch_last(down_even)
    gelu, slope = mix(
        normed2, up_w, order, split, False, [up_bias], [(tokens, BF), (tokens, F32)], into_gelu
    )

    d_hidden, up_sums = mix(
        d_branch2, down_w, order, split, True, [slope], [(tokens, BF), (2, F32)], times_slope
    )
    hidden_back = parts(d_hidden, up_w, order, split, True)
    parts_normed2 = grid.exchange(hidden_back)
    gelu_late, d_hidden_late = after((gelu, d_hidden), hidden_back)
    down_fold = fold_core(weight_grads(d_branch2, gelu_late, order, split, False))
    up_fold = fold_core(weight_grads(normed2, d_hidden_late, order, split, True))
    gelu_down = parts(gelu_late, down_w, order, split, False)
    folds = fold([down_fold, up_fold], (0, 1), True)
    parts_normed2, folds, gelu_down = lax.optimization_barrier((parts_normed2, folds, gelu_down))
    folds = move(folds, True)
    d_normed2 = column_sum(parts_normed2)
    d_shift2 = token_sums(d_normed2)
    d_scale2 = token_sums(d_normed2 * xhat2)
    d_middle = grad_out + norm_backward(grid, d_normed2 * scale2, xhat2, inv2)

    d_gate1 = token_sums(d_middle * branch1)
    d_branch1_own = (d_middle * gate1).astype(BF)
    d_branch1 = grid.exchange(grid.copies(d_branch1_own))
    down_fold, up_fold = folds
    d_branch1, gelu_down, down_fold, up_fold = lax.optimization_barrier(
        (d_branch1, gelu_down, down_fold, up_fold)
    )
    parts_branch2 = grid.exchange(gelu_down)
    (d_attn,) = mix(d_branch1, out_w, order, split, True, [], [(tokens, BF)], keep_bf16)
    folds = move(fold([down_fold, up_fold], (0, 1), False), False)
    d_qkv = attend_back(packed, attn, log_total, d_attn, order, head_size, count)
    qkv_back = parts(d_qkv, qkv_w, order, split, True)
    qkv_back, parts_branch2, folds = lax.optimization_barrier((qkv_back, parts_branch2, folds))
    down_fold, up_fold = folds
    parts_normed1 = grid.exchange(qkv_back)
    d_qkv_late, attn_late = after((d_qkv, attn), qkv_back)
    qkv_fold = fold_core(weight_grads(normed1, d_qkv_late, order, split, True))
    out_fold = fold_core(weight_grads(d_branch1, attn_late, order, split, False))
    late_folds = fold([qkv_fold, out_fold], (1, 0), True)
    parts_normed1, late_folds = lax.optimization_barrier((parts_normed1, late_folds))
    down_fold, up_fold = after((down_fold, up_fold), parts_normed1)
    up_placed, down_placed = grid.place(up_fold, down_fold)
    late_folds = move(late_folds, True)
    d_normed1 = column_sum(parts_normed1)
    d_shift1 = token_sums(d_normed1)
    d_scale1 = token_sums(d_normed1 * xhat1)
    norm_back1 = norm_backward(grid, d_normed1 * scale1, xhat1, inv1)
    branch2 = with_bias(column_sum(parts_branch2), down_bias)
    outputs = unpadded((middle + gate2 * branch2).astype(BF))
    d_gate2 = token_sums(grad_out * branch2)
    head_sums = token_sums(d_qkv.astype(F32))
    head_sums = head_sums.reshape(2, 2, heads, 3, head_size)
    head_sums = jnp.stack([head_sums[:, :, :, 0], head_sums[:, :, :, 2]], axis=3)
    vectors = jnp.concatenate(
        [
            jnp.stack([d_shift1, d_scale1, d_gate1, d_shift2, d_scale2, d_gate2], axis=1),
            token_sums(d_branch1_own.astype(F32))[:, None],
            token_sums(d_branch2_own.astype(F32))[:, None],
            head_sums.reshape(2, -1, col_width),
            up_sums.reshape(2, -1, col_width),
        ],
        axis=1,
    ).astype(BF)
    norm_back1, late_folds = lax.optimization_barrier((norm_back1, late_folds))
    act_all = act_cond
    vectors = after(vectors, late_folds)
    everyone = jnp.stack([vectors, grid.swap_row(vectors)])
    bit = grid.dps // 2
    while bit:
        everyone = jnp.concatenate([everyone, grid.swap_dp(everyone, bit)])
        act_all = jnp.concatenate([act_all, grid.swap_dp(after(act_all, vectors), bit)])
        bit //= 2
    late_folds = move(fold(late_folds, (1, 0), False), False)
    up_moved = grid.place_end(up_placed)
    late_folds, up_moved, down_placed, everyone, act_all = lax.optimization_barrier(
        (late_folds, up_moved, down_placed, everyone, act_all)
    )
    qkv_fold, out_fold = late_folds
    qkv_placed, out_placed = grid.place(qkv_fold, out_fold)

    in_grads = unpadded(d_middle + norm_back1)
    vector_sums = jnp.sum(everyone.astype(F32), axis=0)
    feature_share = col_width // grid.dps
    shares = lax.dynamic_slice_in_dim(vector_sums, grid.dp * feature_share, feature_share, 2)

    def over_rows(rows, shape):
        halves = rows.reshape(grid.dps, 2, 2, 2, -1).astype(F32)
        total = jnp.sum(halves[:, 0, :, 0] + halves[:, 1, :, 1], axis=0)
        return total.reshape(2, *shape)

    head_rows = 2 * heads * 2 * head_size // col_width
    head_total = over_rows(everyone[:, :, 8 : 8 + head_rows], (heads, 2, head_size))
    up_total_own = over_rows(everyone[:, :, 8 + head_rows :], (up_count,))
    head_share = head_size // grid.dps
    head_total = lax.dynamic_slice_in_dim(head_total, grid.dp * head_share, head_share, 3)
    qv_b_grad = jnp.transpose(head_total, (0, 3, 1, 2))

    by_row = everyone[:, :, :6].reshape(grid.dps, 2, 2, 6, col_width)
    d_mod = jnp.where(grid.row == 0, by_row, by_row[:, ::-1]).reshape(-1, 2, 6, col_width)
    mod_share = mod_rows // grid.dps
    act_share = lax.dynamic_slice_in_dim(act_all, grid.dp * mod_share, mod_share, 1)
    qkv_placed, out_placed = lax.optimization_barrier((qkv_placed, out_placed))
    qkv_moved = grid.place_end(qkv_placed)
    mod_w_grad = modulation_grads(after(act_share, up_moved), d_mod, 6)
    own_d_mod = after(d_mod[:seq_count], qkv_placed)
    cond_part = condition_part(own_d_mod, mod_weights)
    last = jnp.stack([cond_part, up_total_own])
    lasts = [last] + grid.col_others(last)
    cond_sum = sum(item[0] for item in lasts)
    up_share = up_count * grid.cols // grid.dps
    up_from = (grid.col - grid.dp * grid.cols // grid.dps) % grid.cols
    up_chosen = sum(jnp.where(up_from == j, lasts[j][1], 0.0) for j in range(grid.cols))
    up_start = (grid.dp % (grid.dps // grid.cols)) * up_share
    up_b_grad = lax.dynamic_slice_in_dim(up_chosen, up_start, up_share, 1)
    qkv_total, up_total = grid.placed(qkv_moved), grid.placed(up_moved)
    down_total = [down_placed[s].astype(F32)[None] for s in streams]
    out_total = [out_placed[s].astype(F32)[None] for s in streams]
    sigmoid_cond = jax.nn.sigmoid(condition)
    condition_grad = cond_sum * sigmoid_cond * (1.0 + condition * (1.0 - sigmoid_cond))

    grads = []
    for s in streams:
        grads += [
            mod_w_grad[s],
            jnp.transpose(shares[s, :6])[None],
            qkv_total[s],
            qv_b_grad[s],
            out_total[s],
            shares[s, 6][None],
            up_total[s],
            up_b_grad[s][None],
            down_total[s],
            shares[s, 7][None],
        ]
    return (*outputs, *in_grads, condition_grad, *grads)


def solution(mesh):
    in_specs = (
        P(("dp", "row"), "col"),
        P(("dp", "row"), "col"),
        P("dp", "row"),
        P("row", None, "col"),
        P(None, "col"),
        P("col", "row"),
        P(("row", "col"), None, None),
        P("row", "col"),
        P("col"),
        P("col", "row"),
        P("row"),
        P("row", "col"),
        P("col"),
        P("row", None, "col"),
        P(None, "col"),
        P("col", "row"),
        P(("row", "col"), None, None),
        P("row", "col"),
        P("col"),
        P("col", "row"),
        P("row"),
        P("row", "col"),
        P("col"),
        P(("dp", "row"), "col"),
        P(("dp", "row"), "col"),
    )
    out_specs = (
        P(("dp", "row"), "col"),
        P(("dp", "row"), "col"),
        P(("dp", "row"), "col"),
        P(("dp", "row"), "col"),
        P("dp", "row"),
        P("row", "dp", None, "col"),
        P("col", "dp", None),
        P("col", "dp", "row"),
        P("dp", ("row", "col"), None),
        P("row", "dp", "col"),
        P("col", "dp"),
        P("col", "dp", "row"),
        P("row", "dp"),
        P("row", "dp", "col"),
        P("col", "dp"),
        P("row", "dp", None, "col"),
        P("col", "dp", None),
        P("col", "dp", "row"),
        P("dp", ("row", "col"), None),
        P("row", "dp", "col"),
        P("col", "dp"),
        P("col", "dp", "row"),
        P("row", "dp"),
        P("row", "dp", "col"),
        P("col", "dp"),
    )
    return jax.shard_map(shards, mesh=mesh, in_specs=in_specs, out_specs=out_specs, check_vma=False)
```

```python
import jax
import jax.numpy as jnp
from jax import lax
from jax.experimental import pallas as pl
from jax.experimental.pallas import tpu as pltpu
from jax.sharding import PartitionSpec as P

EPS = 1e-06
GELU_C = 0.7978845608028654
GELU_K = 0.044715
BF = jnp.bfloat16
F32 = jnp.float32
PLANE = ("dp", "col")
IMAGE, TEXT = 0, 1


def gelu_parts(hidden):
    tangent = jnp.tanh(GELU_C * (hidden + GELU_K * hidden * hidden * hidden))
    gelu_value = 0.5 * hidden * (1.0 + tangent)
    gelu_slope = 0.5 * (1.0 + tangent) + 0.5 * hidden * (1.0 - tangent * tangent) * GELU_C * (
        1.0 + 3.0 * GELU_K * hidden * hidden
    )
    return (gelu_value, gelu_slope)


def transposed_left(left_side, right_side):
    return lax.dot_general(
        left_side, right_side, (((0,), (0,)), ((), ())), preferred_element_type=F32
    )


def transposed_right(left_side, right_side):
    return lax.dot_general(
        left_side, right_side, (((1,), (1,)), ((), ())), preferred_element_type=F32
    )


def product(left_side, right_side):
    return jnp.dot(left_side, right_side, preferred_element_type=F32)


VMEM_BYTES = 56 * 1024 * 1024
FREE = pl.CostEstimate(flops=0, bytes_accessed=0, transcendentals=0)


def call(body, grid, in_specs, out_specs, out_shape, operands, scratch=()):
    return pl.pallas_call(
        body,
        grid_spec=pltpu.PrefetchScalarGridSpec(
            num_scalar_prefetch=1,
            grid=grid,
            in_specs=in_specs,
            out_specs=out_specs,
            scratch_shapes=scratch,
        ),
        out_shape=out_shape,
        cost_estimate=FREE,
        compiler_params=pltpu.CompilerParams(vmem_limit_bytes=VMEM_BYTES),
    )(*operands)


def whole(shape):
    return pl.BlockSpec(shape, lambda step, order: (0,) * len(shape))


def on_rows(shape):
    return pl.BlockSpec(shape, lambda step, order: (step, 0))


def on_columns(shape):
    return pl.BlockSpec(shape, lambda step, order: (0, step))


def mix(columns, weights, order, split, back, extra, outs, finish):
    tokens, width = columns.shape[1:]
    total = weights[0][0].shape[0 if back else 1]
    block = 512 if total % 512 == 0 else width
    pair = (block, 2 * width) if back else (2 * width, block)
    ranges = ((0, split), (split, tokens))

    def body(order_ref, columns_ref, *refs):
        multiply = transposed_right if back else product
        even_ref, odd_ref = refs[-2:]

        @pl.when(pl.program_id(0) == 0)
        def _():
            for stream, (low, high) in enumerate(ranges):
                for place, ref in enumerate((even_ref, odd_ref, even_ref, odd_ref)):
                    lanes = slice(place // 2 * width, (place // 2 + 1) * width)
                    ref[low:high, lanes] = columns_ref[order_ref[4 * stream + place], low:high]

        for stream, (low, high) in enumerate(ranges):
            value = multiply(even_ref[low:high], refs[2 * stream][...])
            value += multiply(odd_ref[low:high], refs[2 * stream + 1][...])
            finish(stream, slice(low, high), value, refs[4:-2])

    return call(
        body,
        (total // block,),
        [whole(columns.shape)]
        + [on_rows(pair) if back else on_columns(pair)] * 4
        + [on_columns((item.shape[0], block)) for item in extra],
        [on_columns((rows, block)) for rows, _ in outs],
        [jax.ShapeDtypeStruct((rows, total), kind) for rows, kind in outs],
        (order, columns, *weights[0], *weights[1], *extra),
        [pltpu.VMEM((tokens, 2 * width), BF)] * 2,
    )


def parts(inputs, weights, order, split, back):
    tokens, depth = inputs.shape
    width = weights[0][0].shape[0 if back else 1] // 2
    pair = (width, depth) if back else (depth, width)
    ranges = ((0, split), (split, tokens))

    def body(order_ref, inputs_ref, *refs):
        multiply = transposed_right if back else product
        for half in range(2):
            for stream, (low, high) in enumerate(ranges):
                place = order_ref[4 * stream + 2 * pl.program_id(0) + half]
                value = multiply(inputs_ref[low:high], refs[2 * stream + half][...])
                refs[4][place, low:high] = value.astype(BF)

    return call(
        body,
        (2,),
        [whole(inputs.shape)] + [on_rows(pair) if back else on_columns(pair)] * 4,
        whole((4, tokens, width)),
        jax.ShapeDtypeStruct((4, tokens, width), BF),
        (order, inputs, *weights[0], *weights[1]),
    )


def weight_grads(columns, inputs, order, split, back):
    tokens, width = columns.shape[1:]
    depth = inputs.shape[1]
    shape = (2 * width, depth) if back else (depth, 2 * width)
    pair = (width, depth) if back else (depth, width)
    ranges = ((0, split), (split, tokens))

    def body(order_ref, columns_ref, inputs_ref, *refs):
        for half in range(2):
            for stream, (low, high) in enumerate(ranges):
                place = order_ref[4 * stream + 2 * pl.program_id(0) + half]
                column = columns_ref[place, low:high]
                other = inputs_ref[low:high]
                if back:
                    value = transposed_left(column, other)
                else:
                    value = transposed_left(other, column)
                refs[2 * stream + half][...] = value.astype(BF)

    grads = call(
        body,
        (2,),
        [whole(columns.shape), whole(inputs.shape)],
        [on_rows(pair) if back else on_columns(pair)] * 4,
        [jax.ShapeDtypeStruct(shape, BF)] * 4,
        (order, columns, inputs),
    )
    return [(grads[0], grads[1]), (grads[2], grads[3])]


def steps_for(extents, lanes):
    tile = 128 if lanes else 16
    return 3 if all(extent % (3 * tile) == 0 for extent in extents) else 1


def assemble(groups):
    shapes = [(2 * group[0].shape[0], 2 * group[0].shape[1]) for group in groups]

    def body(order_ref, *refs):
        for item, (rows, _) in enumerate(shapes):
            out_ref = refs[4 * len(groups) + item]
            for side in range(2):

                @pl.when(pl.program_id(0) == side)
                def _():
                    out_ref[: rows // 2] = refs[4 * item + side][...]
                    out_ref[rows // 2 :] = refs[4 * item + 2 + side][...]

    flat = [array for group in groups for array in group]
    return call(
        body,
        (2,),
        [whole(array.shape) for array in flat],
        [on_columns((rows, columns // 2)) for rows, columns in shapes],
        [jax.ShapeDtypeStruct(shape, BF) for shape in shapes],
        (jnp.zeros((1,), jnp.int32), *flat),
    )


def add_and_cut(pairs, cuts):
    over_columns = [pair[0].shape[1] for pair, cut in zip(pairs, cuts) if cut == 0]
    over_rows = [pair[0].shape[0] for pair, cut in zip(pairs, cuts) if cut == 1]
    steps = min(steps_for(over_columns, True), steps_for(over_rows, False))
    in_specs, out_specs, out_shape = [], [], []
    for (first, _), cut in zip(pairs, cuts):
        rows, columns = first.shape
        if cut == 0:
            in_specs += [on_columns((rows, columns // steps))] * 2
            out_specs += [on_columns((rows // 2, columns // steps))] * 2
            out_shape += [jax.ShapeDtypeStruct((rows // 2, columns), BF)] * 2
        else:
            in_specs += [on_rows((rows // steps, columns))] * 2
            out_specs += [on_rows((rows // steps, columns // 2))] * 2
            out_shape += [jax.ShapeDtypeStruct((rows, columns // 2), BF)] * 2

    def body(order_ref, *refs):
        for item, cut in enumerate(cuts):
            total = refs[2 * item][...].astype(F32) + refs[2 * item + 1][...].astype(F32)
            total = total.astype(BF)
            outs = refs[2 * len(cuts) + 2 * item :]
            half = total.shape[cut] // 2
            outs[0][...] = total[:half] if cut == 0 else total[:, :half]
            outs[1][...] = total[half:] if cut == 0 else total[:, half:]

    flat = [array for pair in pairs for array in pair]
    halves = call(
        body, (steps,), in_specs, out_specs, out_shape, (jnp.zeros((1,), jnp.int32), *flat)
    )
    return [(halves[2 * item], halves[2 * item + 1]) for item in range(len(pairs))]


def add_and_stack(wides, talls):
    shapes = []
    for (wide, _), (tall, _) in zip(wides, talls):
        beside = wide.shape[1] // tall.shape[1]
        shapes.append((wide.shape[0] + tall.shape[0] // beside, wide.shape[1]))

    def body(order_ref, *refs):
        for item, (rows, columns) in enumerate(shapes):
            wide, wide_other, tall, tall_other = refs[4 * item : 4 * item + 4]
            out_ref = refs[4 * len(shapes) + item]
            top, width = wide.shape[0], tall.shape[1]
            out_ref[:top] = (wide[...].astype(F32) + wide_other[...].astype(F32)).astype(BF)
            total = (tall[...].astype(F32) + tall_other[...].astype(F32)).astype(BF)
            for part in range(columns // width):
                piece = total[part * (rows - top) : (part + 1) * (rows - top)]
                out_ref[top:, part * width : (part + 1) * width] = piece
            if columns % width:
                out_ref[top:, columns - columns % width :] = jnp.zeros(
                    (rows - top, columns % width), BF
                )

    flat = [array for pairs in zip(wides, talls) for pair in pairs for array in pair]
    return call(
        body,
        (1,),
        [whole(array.shape) for array in flat],
        [whole(shape) for shape in shapes],
        [jax.ShapeDtypeStruct(shape, BF) for shape in shapes],
        (jnp.zeros((1,), jnp.int32), *flat),
    )


def unpack(fronts, width, by_row_first):
    rows, columns = fronts[0].shape[0] // 4, fronts[0].shape[1]
    deep = rows - width

    def body(order_ref, *refs):
        shorter = rows - width
        for stream, by_row in enumerate(by_row_first):
            front_ref, qkv_ref, out_ref = refs[stream], refs[2 + 2 * stream], refs[3 + 2 * stream]
            for block in range(2):
                qkv_halves = []
                for half in range(2):
                    start = rows * (2 * block + half if by_row else 2 * half + block)
                    qkv_halves.append(front_ref[start : start + width])
                    lanes = slice(block * width, (block + 1) * width)
                    out_ref[half * shorter : (half + 1) * shorter, lanes] = front_ref[
                        start + width : start + rows, :width
                    ]
                qkv_ref[block * width : (block + 1) * width] = jnp.concatenate(qkv_halves, axis=1)

    shapes = [(2 * width, 2 * columns), (2 * deep, 2 * width)] * 2
    return call(
        body,
        (1,),
        [whole(front.shape) for front in fronts],
        [whole(shape) for shape in shapes],
        [jax.ShapeDtypeStruct(shape, BF) for shape in shapes],
        (jnp.zeros((1,), jnp.int32), *fronts),
    )


def rows_for(values, rows):
    gap = rows - values.shape[-2]
    return jnp.pad(values, [(0, 0)] * (values.ndim - 2) + [(0, gap), (0, 0)])


def modulation_grads(act, d_mod, mod_rows):
    sequences, count = act.shape
    width = d_mod.shape[-1]
    act = act.astype(F32)
    d_mod = jnp.moveaxis(d_mod, 0, 2).astype(F32).reshape(-1, sequences, width)

    def body(order_ref, act_ref, d_ref, *refs):
        for stream in range(2):
            d_row = d_ref[stream * mod_rows + pl.program_id(0)].astype(BF)
            refs[stream][0] = transposed_left(act_ref[...].astype(BF), d_row)

    spec = pl.BlockSpec((1, count, width), lambda step, order: (step, 0, 0))
    grads = call(
        body,
        (mod_rows,),
        [whole(act.shape), whole(d_mod.shape)],
        [spec] * 2,
        [jax.ShapeDtypeStruct((mod_rows, count, width), F32)] * 2,
        (jnp.zeros((1,), jnp.int32), act, d_mod),
    )
    return [jnp.transpose(grad, (1, 0, 2))[None] for grad in grads]


def condition_part(d_mod, weights):
    sequences, _, mod_rows, width = d_mod.shape
    inputs = weights[0].shape[0]
    d_mod = jnp.moveaxis(d_mod, 0, 2).astype(F32).reshape(-1, sequences, width)
    d_mod = rows_for(d_mod, 8)

    def body(order_ref, d_ref, image_ref, text_ref, out_ref):
        @pl.when(pl.program_id(0) == 0)
        def _():
            out_ref[...] = jnp.zeros_like(out_ref)

        for stream, weight_ref in enumerate((image_ref, text_ref)):
            d_row = d_ref[stream * mod_rows + pl.program_id(0)].astype(BF)
            out_ref[...] += transposed_right(d_row, weight_ref[0])

    spec = pl.BlockSpec((1, inputs, width), lambda step, order: (step, 0, 0))
    total = call(
        body,
        (mod_rows,),
        [whole(d_mod.shape), spec, spec],
        whole((8, inputs)),
        jax.ShapeDtypeStruct((8, inputs), F32),
        (jnp.zeros((1,), jnp.int32), d_mod, *[jnp.transpose(w, (1, 0, 2)) for w in weights]),
    )
    return total[:sequences]


def head_parts(packed_ref, head, size):
    start = head * 3 * size
    return [packed_ref[:, start + j * size : start + (j + 1) * size] for j in range(3)]


def attend(packed, order, size, count):
    tokens = packed.shape[0]
    heads = packed.shape[1] // (3 * size)
    scale = size ** (-0.5)

    def body(order_ref, packed_ref, out_ref, log_ref):
        keep = lax.broadcasted_iota(jnp.int32, (tokens, tokens), 0) < count
        for pair in range(heads // 2):
            attended = []
            for head in (2 * pair, 2 * pair + 1):
                query, key, value = head_parts(packed_ref, head, size)
                scores = transposed_right(key, query) * scale
                powers = jnp.where(keep, jnp.exp(scores), 0.0)
                log_total = jnp.log(jnp.sum(powers, axis=0, keepdims=True))
                log_ref[head : head + 1] = log_total
                probs = jnp.where(keep, jnp.exp(scores - log_total), 0.0).astype(BF)
                attended.append(transposed_left(value, probs))
            both = jnp.concatenate(attended, axis=0)
            out_ref[:, 2 * pair * size : 2 * (pair + 1) * size] = both.T.astype(BF)

    return call(
        body,
        (1,),
        [whole(packed.shape)],
        [whole((tokens, heads * size)), whole((heads, tokens))],
        [
            jax.ShapeDtypeStruct((tokens, heads * size), BF),
            jax.ShapeDtypeStruct((heads, tokens), F32),
        ],
        (order, packed),
    )


def attend_back(packed, attended, log_total, d_attended, order, size, count):
    tokens = packed.shape[0]
    heads = packed.shape[1] // (3 * size)
    scale = size ** (-0.5)

    def body(order_ref, packed_ref, attended_ref, log_ref, d_ref, out_ref):
        keep = lax.broadcasted_iota(jnp.int32, (tokens, tokens), 0) < count
        for pair in range(heads // 2):
            lanes = slice(2 * pair * size, 2 * (pair + 1) * size)
            d_pair = d_ref[:, lanes]
            both = d_pair.astype(F32) * attended_ref[:, lanes].astype(F32)
            both = both.T
            grads = []
            for side in range(2):
                head = 2 * pair + side
                delta = jnp.sum(both[side * size : (side + 1) * size], axis=0, keepdims=True)
                query, key, value = head_parts(packed_ref, head, size)
                d_out = d_pair[:, side * size : (side + 1) * size]
                scores = transposed_right(key, query) * scale
                weights = jnp.where(keep, jnp.exp(scores - log_ref[head : head + 1]), 0.0)
                d_value = product(weights.astype(BF), d_out)
                d_probs = transposed_right(value, d_out)
                d_scores = (weights * (d_probs - delta) * scale).astype(BF)
                d_key = product(d_scores, query)
                d_query = transposed_left(key, d_scores).T
                grads += [d_query, d_key, d_value]
            start = 2 * pair * 3 * size
            merged = jnp.concatenate(grads, axis=1).astype(BF)
            out_ref[:, start : start + 6 * size] = merged

    return call(
        body,
        (1,),
        [
            whole(packed.shape),
            whole(attended.shape),
            whole(log_total.shape),
            whole(d_attended.shape),
        ],
        whole(packed.shape),
        jax.ShapeDtypeStruct(packed.shape, BF),
        (order, packed, attended, log_total, d_attended),
    )


class Grid:
    def __init__(self):
        self.dps = lax.axis_size("dp")
        self.cols = lax.axis_size("col")
        self.dp = lax.axis_index("dp")
        self.row = lax.axis_index("row")
        self.col = lax.axis_index("col")

    def hop(self, dp, block, stream):
        mixed = (dp % self.cols) ^ block
        return ((mixed % 2) * 2 + mixed // 2) ^ (2 * stream)

    def along_plane(self, target):
        pairs = []
        for dp in range(self.dps):
            for col in range(self.cols):
                to_dp, to_col = target(dp, col)
                pairs.append((dp * self.cols + col, to_dp * self.cols + to_col % self.cols))
        return pairs

    def spread(self, values, stream):
        return lax.ppermute(
            values, PLANE, self.along_plane(lambda d, c: (d, c + self.hop(d, 0, stream)))
        )

    def bring_back(self, values, stream):
        return lax.ppermute(
            values, PLANE, self.along_plane(lambda d, c: (d, c - self.hop(d, 0, stream)))
        )

    def swap_dp(self, values, bit):
        return lax.ppermute(values, "dp", [(d, d ^ bit) for d in range(self.dps)])

    def swap_row(self, values):
        return lax.ppermute(values, "row", [(0, 1), (1, 0)])

    def col_others(self, values):
        return [
            lax.ppermute(values, "col", [(c, (c + shift) % self.cols) for c in range(self.cols)])
            for shift in range(1, self.cols)
        ]

    def copies(self, values):
        return jnp.broadcast_to(values[None], (self.cols, *values.shape))

    def exchange(self, values):
        return lax.all_to_all(values, "col", 0, 0, tiled=True)

    def everyone(self, values):
        return self.exchange(self.copies(values))

    def order(self):
        hops = [
            self.hop(self.dp, block, stream)
            for stream in (IMAGE, TEXT)
            for block in range(self.cols)
        ]
        return jnp.stack([(self.col - hop) % self.cols for hop in hops]).astype(jnp.int32)

    def piece(self, shard, axis, stream):
        width = shard.shape[axis] // self.cols
        index = (self.col + self.hop(self.dp, 0, stream)) % self.cols
        return lax.dynamic_slice_in_dim(shard, index * width, width, axis)

    def move(self, values, by_row):
        return self.swap_row(values) if by_row else self.swap_dp(values, 2)

    def fold_rest(self, pair):
        bit = self.dps // 2
        while bit >= self.cols:
            total = pair[0].astype(F32) + pair[1].astype(F32)
            half = total.shape[0] // 2
            upper = (self.dp // bit) % 2
            keep = lax.dynamic_slice_in_dim(total, upper * half, half, 0).astype(BF)
            send = lax.dynamic_slice_in_dim(total, (1 - upper) * half, half, 0).astype(BF)
            pair = (keep, self.swap_dp(send, bit))
            bit //= 2
        return pair

    def place(self, wides, talls):
        share = self.dps // self.cols
        if share > 1:
            talls = [self.fold_rest(pair) for pair in talls]
        cols_placed, rows_placed = [], []
        for stream, both in enumerate(add_and_stack(wides, talls)):
            pairs = self.along_plane(
                lambda d, c: (c * share + d // self.cols, c - self.hop(d, 0, stream))
            )
            moved = lax.ppermute(both, PLANE, pairs)
            top, width = wides[stream][0].shape[0], talls[stream][0].shape[1]
            cols_placed.append(moved[:top])
            parts = [
                moved[top:, part * width : (part + 1) * width]
                for part in range(moved.shape[1] // width)
            ]
            rows_placed.append(jnp.concatenate(parts))
        return cols_placed, rows_placed

    def place_end(self, parts):
        moved = jnp.stack(parts)
        moved = moved.reshape(len(parts), self.dps, -1, moved.shape[2])
        return lax.all_to_all(moved, "dp", 1, 1, tiled=True)

    def placed(self, moved):
        total = moved.astype(F32).reshape(moved.shape[0], self.cols, -1, *moved.shape[2:])
        total = jnp.sum(total, axis=2)
        return [
            jnp.concatenate([part[col] for col in range(self.cols)], axis=1)[None]
            for part in total
        ]


def after(values, *earlier):
    return lax.optimization_barrier((values, earlier))[0]


def added(parts):
    return sum(part.astype(F32) for part in parts)


def column_sum(parts):
    return jnp.sum(parts.astype(F32), axis=0)


def norm_forward(grid, values):
    width = values.shape[1]
    own_mean = jnp.mean(values, axis=1)
    centred = values - own_mean[:, None]
    packed = jnp.stack([own_mean, jnp.sum(centred * centred, axis=1)])
    everyone = grid.everyone(packed)
    mean = jnp.mean(everyone[:, 0], axis=0)
    squares = jnp.sum(everyone[:, 1] + width * (everyone[:, 0] - mean) ** 2, axis=0)
    inv_std = lax.rsqrt(squares / (width * grid.cols) + EPS)
    return ((values - mean[:, None]) * inv_std[:, None], inv_std[:, None], everyone)


def norm_backward(grid, grad_hat, normed, inv_std):
    full_width = grad_hat.shape[1] * grid.cols
    packed = jnp.stack([jnp.sum(grad_hat, axis=1), jnp.sum(grad_hat * normed, axis=1)])
    total = jnp.sum(grid.everyone(packed), axis=0) / full_width
    return inv_std * (grad_hat - total[0][:, None] - normed * total[1][:, None])


def shards(
    image_in,
    text_in,
    condition,
    image_mod_weight,
    image_mod_bias,
    image_qkv_weight,
    image_qv_bias,
    image_out_weight,
    image_out_bias,
    image_up_weight,
    image_up_bias,
    image_down_weight,
    image_down_bias,
    text_mod_weight,
    text_mod_bias,
    text_qkv_weight,
    text_qv_bias,
    text_out_weight,
    text_out_bias,
    text_up_weight,
    text_up_bias,
    text_down_weight,
    text_down_bias,
    image_cotangent,
    text_cotangent,
):
    grid = Grid()
    streams = (IMAGE, TEXT)
    seq_count = condition.shape[0]
    col_width = image_in.shape[1]
    order = grid.order()
    split = image_in.shape[0]
    count = split + text_in.shape[0]
    padding = -count % 16
    lengths = (split, text_in.shape[0] + padding)
    heads = image_qv_bias.shape[0]
    head_size = image_qv_bias.shape[2]
    mod_weights = (image_mod_weight, text_mod_weight)
    mod_rows = image_mod_weight.shape[0]

    def rows_of(values):
        return (values[:split], values[split:])

    def unpadded(values):
        return (values[:split], values[split:count])

    by_row_first = (True, False)

    def pieces(weights, axis):
        return [grid.piece(weight, axis, s) for s, weight in enumerate(weights)]

    def fetch(parts):
        return [grid.spread(part, s) for s, part in enumerate(parts)]

    def fetch_even(parts, axis):
        groups = []
        for s in streams:
            by_row = by_row_first[s]
            first, second = grid.move(parts[s], by_row), grid.move(parts[s], not by_row)
            corner = grid.move(first, not by_row)
            row_other, block_other = (first, second) if by_row else (second, first)
            edges = (row_other, block_other) if axis == 1 else (block_other, row_other)
            groups.append((parts[s], *edges, corner))
        return assemble(groups)

    def fetch_last(evens):
        return [(even, grid.swap_dp(even, 1)) for even in evens]

    def fold_core(grads):
        return [(even, grid.swap_dp(odd, 1)) for even, odd in grads]

    def cut_axes(axis, first):
        return [axis if by_row == first else 1 - axis for by_row in by_row_first]

    def fold(pairs, axes, first):
        flat = [pair for group in pairs for pair in group]
        halves = add_and_cut(flat, [cut for axis in axes for cut in cut_axes(axis, first)])
        return [halves[2 * group : 2 * group + 2] for group in range(len(pairs))]

    def move(groups, first):
        return [
            [(keep, grid.move(send, by_row_first[s] == first)) for s, (keep, send) in enumerate(group)]
            for group in groups
        ]

    def join(parts):
        return jnp.concatenate(parts, axis=0)

    qkv_pieces = pieces((image_qkv_weight, text_qkv_weight), 1)
    out_pieces = pieces((image_out_weight, text_out_weight), 0)
    front_pieces = [
        join([qkv_piece, jnp.pad(out_piece, ((0, 0), (0, qkv_piece.shape[1] - col_width)))])
        for qkv_piece, out_piece in zip(qkv_pieces, out_pieces)
    ]
    front_mine = fetch(front_pieces)
    front_other = [grid.move(front_mine[s], by_row_first[s]) for s in streams]
    image_in, text_in, condition = after((image_in, text_in, condition), front_pieces)

    def padded(parts):
        zeros = jnp.zeros((padding, col_width), F32)
        return join([part.astype(F32) for part in parts] + [zeros])

    act_cond = (condition * jax.nn.sigmoid(condition)).astype(BF)
    partial_mod = jnp.stack(
        [
            jnp.stack([product(act_cond, weight[:, j]) for j in range(6)], axis=1)
            for weight in mod_weights
        ],
        axis=1,
    )
    own_mod = lax.dynamic_index_in_dim(partial_mod, grid.row, 0, False)
    other_mod = lax.dynamic_index_in_dim(partial_mod, 1 - grid.row, 0, False)
    up_count = image_up_bias.shape[0] // grid.cols
    own_qv = jnp.stack([image_qv_bias, text_qv_bias])
    own_up = lax.dynamic_slice_in_dim(
        jnp.stack([image_up_bias, text_up_bias]), grid.col * up_count, up_count, 1
    )
    to_row = [values.reshape(-1, col_width) for values in (other_mod, own_qv, own_up)]
    cuts = (to_row[0].shape[0], to_row[0].shape[0] + to_row[1].shape[0])
    values = padded([image_in, text_in])
    xhat1, inv1, statistics = norm_forward(grid, values)
    to_row = after(jnp.concatenate(to_row), front_mine, statistics)
    from_row = jnp.split(grid.swap_row(to_row), cuts)
    modulation = own_mod + from_row[0].reshape(own_mod.shape)
    modulation = modulation + jnp.stack([image_mod_bias, text_mod_bias])

    def field(position):
        return join(
            [
                jnp.broadcast_to(modulation[s, position], (lengths[s], col_width))
                for s in streams
            ]
        )

    def token_sums(values):
        return jnp.stack([jnp.sum(part, axis=0) for part in rows_of(values)])

    qv_bias = jnp.concatenate([own_qv, from_row[1].reshape(own_qv.shape)], axis=1)
    bias_rows = jnp.stack(
        [qv_bias[:, :, 0], jnp.zeros(qv_bias[:, :, 0].shape, F32), qv_bias[:, :, 1]], axis=2
    ).reshape(2, -1)
    up_bias = jnp.concatenate([own_up, from_row[2].reshape(own_up.shape)], axis=1)
    out_bias = (image_out_bias, text_out_bias)
    down_bias = (image_down_bias, text_down_bias)

    def with_bias(values, bias):
        return join([part + bias[s][None, :] for s, part in enumerate(rows_of(values))])

    def keep_bf16(stream, rows, value, refs):
        refs[-1][rows] = value.astype(BF)

    def add_bias(stream, rows, value, refs):
        refs[1][rows] = (value + refs[0][stream : stream + 1]).astype(BF)

    def into_gelu(stream, rows, value, refs):
        gelu_value, gelu_slope = gelu_parts(value + refs[0][stream : stream + 1])
        refs[1][rows] = gelu_value.astype(BF)
        refs[2][rows] = gelu_slope

    def times_slope(stream, rows, value, refs):
        d_hidden = (value * refs[0][rows]).astype(BF)
        refs[1][rows] = d_hidden
        refs[2][stream : stream + 1] = jnp.sum(d_hidden.astype(F32), axis=0, keepdims=True)

    scale1 = 1.0 + field(1)
    normed1_own = (xhat1 * scale1 + field(0)).astype(BF)
    normed1_copies = after(grid.copies(normed1_own), front_mine)
    normed1 = grid.exchange(normed1_copies)
    front_pairs = [
        join([mine, other])
        for mine, other in zip(front_mine, after(front_other, normed1_copies))
    ]
    front_even = [
        join([front_pairs[s], grid.move(front_pairs[s], not by_row_first[s])]) for s in streams
    ]
    up_weights, down_weights = after(
        ((image_up_weight, text_up_weight), (image_down_weight, text_down_weight)), front_mine
    )
    up_pieces, down_pieces = pieces(up_weights, 1), pieces(down_weights, 0)
    up_mine = fetch(up_pieces)
    grad_out = padded([image_cotangent, text_cotangent])
    gate2 = field(5)
    d_branch2_own = (grad_out * gate2).astype(BF)
    d_branch2_copies = grid.copies(after(d_branch2_own, normed1_copies))
    normed1, front_even, up_mine, down_pieces, d_branch2_copies = lax.optimization_barrier(
        (normed1, front_even, up_mine, down_pieces, d_branch2_copies)
    )
    front_odd = [grid.swap_dp(even, 1) for even in front_even]
    evens = unpack(front_even, col_width, by_row_first)
    odds = unpack(front_odd, col_width, by_row_first)
    qkv_w = [(evens[2 * s], odds[2 * s]) for s in streams]
    out_w = [(evens[2 * s + 1], odds[2 * s + 1]) for s in streams]
    down_mine = fetch(down_pieces)
    d_branch2 = grid.exchange(d_branch2_copies)
    tokens = values.shape[0]
    (packed,) = mix(
        normed1, qkv_w, order, split, False, [bias_rows], [(tokens, BF)], add_bias
    )
    attn, log_total = attend(packed, order, head_size, count)
    attn_out = parts(attn, out_w, order, split, False)
    attn_out, up_mine, down_mine, d_branch2 = lax.optimization_barrier(
        (attn_out, up_mine, down_mine, d_branch2)
    )
    parts_out = grid.exchange(attn_out)
    up_even = fetch_even(up_mine, 1)
    parts_out, up_even, down_mine = lax.optimization_barrier((parts_out, up_even, down_mine))
    branch1 = with_bias(column_sum(parts_out), out_bias)

    gate1 = field(2)
    middle = values + gate1 * branch1
    xhat2, inv2, _ = norm_forward(grid, middle)
    scale2 = 1.0 + field(4)
    normed2_copies = grid.copies((xhat2 * scale2 + field(3)).astype(BF))
    normed2 = grid.exchange(normed2_copies)
    up_w = fetch_last(up_even)
    down_even = fetch_even(after(down_mine, normed2_copies), 0)
    normed2, up_w, down_even = lax.optimization_barrier((normed2, up_w, down_even))
    down_w = fetch_last(down_even)
    gelu, slope = mix(
        normed2, up_w, order, split, False, [up_bias], [(tokens, BF), (tokens, F32)], into_gelu
    )

    d_hidden, up_sums = mix(
        d_branch2, down_w, order, split, True, [slope], [(tokens, BF), (2, F32)], times_slope
    )
    hidden_back = parts(d_hidden, up_w, order, split, True)
    parts_normed2 = grid.exchange(hidden_back)
    gelu_late, d_hidden_late = after((gelu, d_hidden), hidden_back)
    down_fold = fold_core(weight_grads(d_branch2, gelu_late, order, split, False))
    up_fold = fold_core(weight_grads(normed2, d_hidden_late, order, split, True))
    gelu_down = parts(gelu_late, down_w, order, split, False)
    folds = fold([down_fold, up_fold], (0, 1), True)
    parts_normed2, folds, gelu_down = lax.optimization_barrier((parts_normed2, folds, gelu_down))
    folds = move(folds, True)
    d_normed2 = column_sum(parts_normed2)
    d_shift2 = token_sums(d_normed2)
    d_scale2 = token_sums(d_normed2 * xhat2)
    d_middle = grad_out + norm_backward(grid, d_normed2 * scale2, xhat2, inv2)

    d_gate1 = token_sums(d_middle * branch1)
    d_branch1_own = (d_middle * gate1).astype(BF)
    d_branch1 = grid.exchange(grid.copies(d_branch1_own))
    down_fold, up_fold = folds
    d_branch1, gelu_down, down_fold, up_fold = lax.optimization_barrier(
        (d_branch1, gelu_down, down_fold, up_fold)
    )
    parts_branch2 = grid.exchange(gelu_down)
    (d_attn,) = mix(d_branch1, out_w, order, split, True, [], [(tokens, BF)], keep_bf16)
    folds = move(fold([down_fold, up_fold], (0, 1), False), False)
    d_qkv = attend_back(packed, attn, log_total, d_attn, order, head_size, count)
    qkv_back = parts(d_qkv, qkv_w, order, split, True)
    qkv_back, parts_branch2, folds = lax.optimization_barrier((qkv_back, parts_branch2, folds))
    down_fold, up_fold = folds
    parts_normed1 = grid.exchange(qkv_back)
    d_qkv_late, attn_late = after((d_qkv, attn), qkv_back)
    qkv_fold = fold_core(weight_grads(normed1, d_qkv_late, order, split, True))
    out_fold = fold_core(weight_grads(d_branch1, attn_late, order, split, False))
    late_folds = fold([qkv_fold, out_fold], (1, 0), True)
    parts_normed1, late_folds = lax.optimization_barrier((parts_normed1, late_folds))
    down_fold, up_fold = after((down_fold, up_fold), parts_normed1)
    up_placed, down_placed = grid.place(up_fold, down_fold)
    late_folds = move(late_folds, True)
    d_normed1 = column_sum(parts_normed1)
    d_shift1 = token_sums(d_normed1)
    d_scale1 = token_sums(d_normed1 * xhat1)
    norm_back1 = norm_backward(grid, d_normed1 * scale1, xhat1, inv1)
    branch2 = with_bias(column_sum(parts_branch2), down_bias)
    outputs = unpadded((middle + gate2 * branch2).astype(BF))
    d_gate2 = token_sums(grad_out * branch2)
    head_sums = token_sums(d_qkv.astype(F32))
    head_sums = head_sums.reshape(2, 2, heads, 3, head_size)
    head_sums = jnp.stack([head_sums[:, :, :, 0], head_sums[:, :, :, 2]], axis=3)
    vectors = jnp.concatenate(
        [
            jnp.stack([d_shift1, d_scale1, d_gate1, d_shift2, d_scale2, d_gate2], axis=1),
            token_sums(d_branch1_own.astype(F32))[:, None],
            token_sums(d_branch2_own.astype(F32))[:, None],
            head_sums.reshape(2, -1, col_width),
            up_sums.reshape(2, -1, col_width),
        ],
        axis=1,
    ).astype(BF)
    norm_back1, late_folds = lax.optimization_barrier((norm_back1, late_folds))
    act_all = act_cond
    vectors = after(vectors, late_folds)
    everyone = jnp.stack([vectors, grid.swap_row(vectors)])
    bit = grid.dps // 2
    while bit:
        everyone = jnp.concatenate([everyone, grid.swap_dp(everyone, bit)])
        act_all = jnp.concatenate([act_all, grid.swap_dp(after(act_all, vectors), bit)])
        bit //= 2
    late_folds = move(fold(late_folds, (1, 0), False), False)
    up_moved = grid.place_end(up_placed)
    late_folds, up_moved, down_placed, everyone, act_all = lax.optimization_barrier(
        (late_folds, up_moved, down_placed, everyone, act_all)
    )
    qkv_fold, out_fold = late_folds
    qkv_placed, out_placed = grid.place(qkv_fold, out_fold)

    in_grads = unpadded(d_middle + norm_back1)
    vector_sums = jnp.sum(everyone.astype(F32), axis=0)
    feature_share = col_width // grid.dps
    shares = lax.dynamic_slice_in_dim(vector_sums, grid.dp * feature_share, feature_share, 2)

    def over_rows(rows, shape):
        halves = rows.reshape(grid.dps, 2, 2, 2, -1).astype(F32)
        total = jnp.sum(halves[:, 0, :, 0] + halves[:, 1, :, 1], axis=0)
        return total.reshape(2, *shape)

    head_rows = 2 * heads * 2 * head_size // col_width
    head_total = over_rows(everyone[:, :, 8 : 8 + head_rows], (heads, 2, head_size))
    up_total_own = over_rows(everyone[:, :, 8 + head_rows :], (up_count,))
    head_share = head_size // grid.dps
    head_total = lax.dynamic_slice_in_dim(head_total, grid.dp * head_share, head_share, 3)
    qv_b_grad = jnp.transpose(head_total, (0, 3, 1, 2))

    by_row = everyone[:, :, :6].reshape(grid.dps, 2, 2, 6, col_width)
    d_mod = jnp.where(grid.row == 0, by_row, by_row[:, ::-1]).reshape(-1, 2, 6, col_width)
    mod_share = mod_rows // grid.dps
    act_share = lax.dynamic_slice_in_dim(act_all, grid.dp * mod_share, mod_share, 1)
    qkv_placed, out_placed = lax.optimization_barrier((qkv_placed, out_placed))
    qkv_moved = grid.place_end(qkv_placed)
    mod_w_grad = modulation_grads(after(act_share, up_moved), d_mod, 6)
    own_d_mod = after(d_mod[:seq_count], qkv_placed)
    cond_part = condition_part(own_d_mod, mod_weights)
    last = jnp.stack([cond_part, up_total_own])
    lasts = [last] + grid.col_others(last)
    cond_sum = sum(item[0] for item in lasts)
    up_share = up_count * grid.cols // grid.dps
    up_from = (grid.col - grid.dp * grid.cols // grid.dps) % grid.cols
    up_chosen = sum(jnp.where(up_from == j, lasts[j][1], 0.0) for j in range(grid.cols))
    up_start = (grid.dp % (grid.dps // grid.cols)) * up_share
    up_b_grad = lax.dynamic_slice_in_dim(up_chosen, up_start, up_share, 1)
    qkv_total, up_total = grid.placed(qkv_moved), grid.placed(up_moved)
    down_total = [down_placed[s].astype(F32)[None] for s in streams]
    out_total = [out_placed[s].astype(F32)[None] for s in streams]
    sigmoid_cond = jax.nn.sigmoid(condition)
    condition_grad = cond_sum * sigmoid_cond * (1.0 + condition * (1.0 - sigmoid_cond))

    grads = []
    for s in streams:
        grads += [
            mod_w_grad[s],
            jnp.transpose(shares[s, :6])[None],
            qkv_total[s],
            qv_b_grad[s],
            out_total[s],
            shares[s, 6][None],
            up_total[s],
            up_b_grad[s][None],
            down_total[s],
            shares[s, 7][None],
        ]
    return (*outputs, *in_grads, condition_grad, *grads)


def solution(mesh):
    in_specs = (
        P(("dp", "row"), "col"),
        P(("dp", "row"), "col"),
        P("dp", "row"),
        P("row", None, "col"),
        P(None, "col"),
        P("col", "row"),
        P(("row", "col"), None, None),
        P("row", "col"),
        P("col"),
        P("col", "row"),
        P("row"),
        P("row", "col"),
        P("col"),
        P("row", None, "col"),
        P(None, "col"),
        P("col", "row"),
        P(("row", "col"), None, None),
        P("row", "col"),
        P("col"),
        P("col", "row"),
        P("row"),
        P("row", "col"),
        P("col"),
        P(("dp", "row"), "col"),
        P(("dp", "row"), "col"),
    )
    out_specs = (
        P(("dp", "row"), "col"),
        P(("dp", "row"), "col"),
        P(("dp", "row"), "col"),
        P(("dp", "row"), "col"),
        P("dp", "row"),
        P("row", "dp", None, "col"),
        P("col", "dp", None),
        P("col", "dp", "row"),
        P("dp", ("row", "col"), None),
        P("row", "dp", "col"),
        P("col", "dp"),
        P("col", "dp", "row"),
        P("row", "dp"),
        P("row", "dp", "col"),
        P("col", "dp"),
        P("row", "dp", None, "col"),
        P("col", "dp", None),
        P("col", "dp", "row"),
        P("dp", ("row", "col"), None),
        P("row", "dp", "col"),
        P("col", "dp"),
        P("col", "dp", "row"),
        P("row", "dp"),
        P("row", "dp", "col"),
        P("col", "dp"),
    )
    return jax.shard_map(shards, mesh=mesh, in_specs=in_specs, out_specs=out_specs, check_vma=False)
```
